256 devices in a mesh: blk: 256 (over x, y, z, core).
Axes of the slice: x: 4, y: 4, z: 8, core: 2. Of those that a mesh axis runs over, the one named last changes fastest.
Arguments:
- tracers: float32 [1024, 2, 2, 128, 128], P('blk'), may hold values from -6 to 6
- velocity: float32 [1024, 2, 2, 128, 128], P('blk'), may hold values from -5 to 5
- block_counts: int32 [256], replicated, may hold values from 1 to 4, as said below
- land_mask: int32 [26, 34], replicated, may hold values from 0 to 1, as said below
Outputs:
- tracers_out: float32 [1024, 2, 2, 128, 128], P('blk')
- velocity_out: float32 [1024, 2, 2, 128, 128], P('blk')
The draws below stay inside these ranges and needn't reach their ends.
Inputs may be any that keep to these rules, and one draw needn't show every extreme that they name: `block_counts`: they sum to 538; the first 68 entries are 1. `land_mask`: exactly 538 ocean blocks; the first 68 blocks in row-major order are ocean.
All inputs are finite; a program needn't handle non-finite values.
Results may differ from the reference program's by a relative error of at most 0.00002.
Values sent between devices are 32-bit elements; how exact they have to be, the bound alone decides.
No kernel may reach another device: no remote copies, remote signals or barrier semaphores. Data moves between devices by JAX's collectives and lax.ppermute only.
A program may use at most 128 MiB of HBM per device.

```python
import jax
import jax.numpy as jnp
from jax import lax

BLOCK_COLUMNS = 128
DEPTH_LEVELS = 2
SLOTS = 4
BCOLS = 34
SUBSTEPS = 2
ONES = 68
NOCEAN = 538
BROWS = 26
SLOT_COUNT = 1024
N_BLK = 256


def draw_block_counts(key, part):
    key = jax.random.fold_in(key, 11)
    rest = N_BLK - ONES
    values = (1 + jnp.arange(rest, dtype=jnp.int32) % SLOTS).astype(jnp.int32)
    shuffled = values[jax.random.permutation(key, rest)]
    return jnp.concatenate([jnp.ones((ONES,), jnp.int32), shuffled]).astype(jnp.int32)


def draw_land_mask(key, part):
    key = jax.random.fold_in(key, 12)
    rest = BROWS * BCOLS - ONES
    ranks = jax.random.permutation(key, rest)
    land_rest = (ranks < BROWS * BCOLS - NOCEAN).astype(jnp.int32)
    whole = jnp.concatenate([jnp.zeros((ONES,), jnp.int32), land_rest])
    return whole.reshape(BROWS, BCOLS).astype(jnp.int32)


def block_scale(own_key, shape, pieces, least, top_value):
    level, own = 1.0, jax.random.fold_in(own_key, 6)
    for dim, blocks in pieces:
        draws = jnp.exp(jax.random.uniform(jax.random.fold_in(own, dim), (blocks,), jnp.float32, least / len(pieces), top_value / len(pieces)))
        level = level * jnp.repeat(draws, shape[dim] // blocks).reshape([-1 if axis == dim else 1 for axis in range(len(shape))])
    return level


def noise(key, shape, spread, bound, pieces=(), kind=jnp.bfloat16):
    result = spread * jax.random.normal(key, shape, jnp.float32)
    if pieces:
        result = result * block_scale(key, shape, pieces, -0.22, 0.18)
    return jnp.clip(result, -bound, bound).astype(kind)


def setup_inputs(seed: int = 0) -> dict:
    arg_keys = jax.random.split(jax.random.key(seed), 5)
    tracers = noise(arg_keys[0], (SLOT_COUNT, 2, DEPTH_LEVELS, BLOCK_COLUMNS, BLOCK_COLUMNS), 1.0, 6.0, ((0, 256),), jnp.float32)
    velocity = noise(arg_keys[1], (SLOT_COUNT, 2, DEPTH_LEVELS, BLOCK_COLUMNS, BLOCK_COLUMNS), 0.7, 5.0, ((0, 256),), jnp.float32)
    block_counts = draw_block_counts(jax.random.fold_in(arg_keys[4], 71), 0)
    land_mask = draw_land_mask(jax.random.fold_in(arg_keys[4], 71), 0)
    return {"tracers": tracers, "velocity": velocity, "block_counts": block_counts, "land_mask": land_mask}


TIME_STEP = 0.1
DIFFUSIVITY = 0.5
VISCOSITY = 0.5
GRAVITY_SCALE = 0.5
CORIOLIS_MEAN = 1.0
CORIOLIS_SLOPE = 2.0


def sea_density(temper, salty):
    return -0.3 * temper + 0.6 * salty - 0.08 * temper * temper + 0.05 * temper * salty


def hydro_pressure(density_now):
    return GRAVITY_SCALE * (jnp.cumsum(density_now, axis=0) - 0.5 * density_now)


def neighbours(field, halo_south, halo_north, halo_west, halo_east):
    north_val = jnp.concatenate([field[:, 1:, :], halo_north[:, None, :]], axis=1)
    south_val = jnp.concatenate([halo_south[:, None, :], field[:, :-1, :]], axis=1)
    east_val = jnp.concatenate([field[:, :, 1:], halo_east[:, :, None]], axis=2)
    west_val = jnp.concatenate([halo_west[:, :, None], field[:, :, :-1]], axis=2)
    return north_val, south_val, east_val, west_val


def advance_substep(ocean_fields, halos, opens, first_row, rows_total):
    width = ocean_fields.shape[-1]
    spots = jnp.arange(width)
    open_n = jnp.where(spots == width - 1, opens[1], 1.0)[None, :, None]
    open_s = jnp.where(spots == 0, opens[0], 1.0)[None, :, None]
    open_e = jnp.where(spots == width - 1, opens[3], 1.0)[None, None, :]
    open_w = jnp.where(spots == 0, opens[2], 1.0)[None, None, :]

    def beside_all(index):
        return neighbours(ocean_fields[index], halos[0, index], halos[1, index], halos[2, index], halos[3, index])

    east_vel = ocean_fields[2]
    north_vel = ocean_fields[3]
    un_val, us_val, ue_val, uw_val = beside_all(2)
    vn_val, vs_val, ve_val, vw_val = beside_all(3)
    face_e = 0.5 * (east_vel + ue_val)
    face_w = 0.5 * (uw_val + east_vel)
    face_n = 0.5 * (north_vel + vn_val)
    face_s = 0.5 * (vs_val + north_vel)
    results = []
    for index in range(2):
        value = ocean_fields[index]
        cn_val, cs_val, east_center_value, cw_val = beside_all(index)
        flux_e = open_e * face_e * 0.5 * (value + east_center_value)
        flux_w = open_w * face_w * 0.5 * (cw_val + value)
        flux_n = open_n * face_n * 0.5 * (value + cn_val)
        flux_s = open_s * face_s * 0.5 * (cs_val + value)
        laplace = open_e * (east_center_value - value) + open_w * (cw_val - value) + open_n * (cn_val - value) + open_s * (cs_val - value)
        results.append(value + TIME_STEP * (-(flux_e - flux_w + flux_n - flux_s) + DIFFUSIVITY * laplace))
    press = hydro_pressure(sea_density(ocean_fields[0], ocean_fields[1]))
    halo_press = [hydro_pressure(sea_density(halos[side, 0], halos[side, 1])) for side in range(4)]
    pn_val, ps_val, pe_val, pw_val = neighbours(press, halo_press[0], halo_press[1], halo_press[2], halo_press[3])
    grad_x = 0.5 * (open_e * (pe_val - press) + open_w * (press - pw_val))
    grad_y = 0.5 * (open_n * (pn_val - press) + open_s * (press - ps_val))
    latitude = (first_row + spots.astype(jnp.float32) + 0.5) / rows_total
    coriolis = (CORIOLIS_MEAN + CORIOLIS_SLOPE * (latitude - 0.5))[None, :, None]
    lap_u = open_e * (ue_val - east_vel) + open_w * (uw_val - east_vel) + open_n * (un_val - east_vel) + open_s * (us_val - east_vel)
    lap_v = open_e * (ve_val - north_vel) + open_w * (vw_val - north_vel) + open_n * (vn_val - north_vel) + open_s * (vs_val - north_vel)
    results.append(east_vel + TIME_STEP * (coriolis * north_vel - grad_x + VISCOSITY * lap_u))
    results.append(north_vel + TIME_STEP * (-coriolis * east_vel - grad_y + VISCOSITY * lap_v))
    return jnp.stack(results)


def block_tables(block_counts, land_mask, device, slot_id):
    grid_rows, grid_cols = land_mask.shape
    flat_land = land_mask.reshape(-1).astype(jnp.int32)
    sea_flag = (1 - flat_land).astype(jnp.int32)
    ordering = jnp.argsort(flat_land, stable=True).astype(jnp.int32)
    position = (jnp.cumsum(sea_flag) - sea_flag).astype(jnp.int32)
    run_ends = jnp.cumsum(block_counts).astype(jnp.int32)
    run_starts = (run_ends - block_counts).astype(jnp.int32)
    list_pos = (run_starts[device] + slot_id).astype(jnp.int32)
    is_live = slot_id < block_counts[device]
    block_in_grid = ordering[jnp.clip(list_pos, 0, grid_rows * grid_cols - 1)]
    block_row = (block_in_grid // grid_cols).astype(jnp.int32)
    block_col = (block_in_grid % grid_cols).astype(jnp.int32)
    at_top = block_row == grid_rows - 1
    mirror_col = (grid_cols - 1 - block_col).astype(jnp.int32)
    nb_row = jnp.stack([block_row - 1, jnp.where(at_top, block_row, block_row + 1), block_row, block_row], axis=-1)
    nb_col = jnp.stack([block_col, jnp.where(at_top, mirror_col, block_col), (block_col + grid_cols - 1) % grid_cols, (block_col + 1) % grid_cols], axis=-1).astype(jnp.int32)
    exists = jnp.stack([block_row > 0, at_top | True, at_top | True, at_top | True], axis=-1)
    nb_grid = (jnp.clip(nb_row, 0, grid_rows - 1) * grid_cols + nb_col).astype(jnp.int32)
    is_wet = exists & (sea_flag[nb_grid] == 1)
    nb_pos = position[nb_grid]
    nb_owner = jnp.clip(jnp.searchsorted(run_ends, nb_pos, side="right").astype(jnp.int32), 0, block_counts.shape[0] - 1)
    nb_slot = (nb_pos - run_starts[nb_owner]).astype(jnp.int32)
    edge_id = jnp.stack([jnp.ones_like(block_row), jnp.where(at_top, 1, 0).astype(jnp.int32), jnp.full_like(block_row, 3), jnp.full_like(block_row, 2)], axis=-1)
    is_fold = jnp.stack([at_top & False, at_top, at_top & False, at_top & False], axis=-1)
    return is_live, block_row, nb_owner, nb_slot, edge_id, is_fold, is_wet


def edge_rims(ocean_fields):
    return jnp.stack([ocean_fields[:, :, :, 0, :], ocean_fields[:, :, :, -1, :], ocean_fields[:, :, :, :, 0], ocean_fields[:, :, :, :, -1]], axis=1)


def reference(tracers, velocity, block_counts, land_mask):
    total_slots = tracers.shape[0]
    slots = total_slots // block_counts.shape[0]
    width = tracers.shape[-1]
    slot_all = jnp.arange(total_slots, dtype=jnp.int32)
    device = (slot_all // slots).astype(jnp.int32)
    slot_id = (slot_all % slots).astype(jnp.int32)
    is_live, block_row, nb_owner, nb_slot, edge_id, is_fold, is_wet = block_tables(block_counts, land_mask, device, slot_id)
    nb_global = nb_owner * slots + jnp.clip(nb_slot, 0, slots - 1)
    take_at = (nb_global * 4 + edge_id).reshape(-1).astype(jnp.int32)
    opens = is_wet.astype(jnp.float32)
    first_row = (block_row * width).astype(jnp.float32)
    rows_total = float(land_mask.shape[0] * width)
    signs = jnp.array([1.0, 1.0, -1.0, -1.0], dtype=jnp.float32)[:, None, None]
    ocean_fields = jnp.concatenate([tracers, velocity], axis=1)
    for step in range(SUBSTEPS):
        rims = edge_rims(ocean_fields)
        flat = rims.reshape((total_slots * 4,) + rims.shape[2:])
        halos = flat[take_at].reshape((total_slots, 4) + rims.shape[2:])
        flipped = halos[..., ::-1] * signs
        halos = jnp.where(is_fold[:, :, None, None, None], flipped, halos)

        def one(items):
            return advance_substep(items[0], items[1], items[2], items[3], rows_total)

        ocean_fields = lax.map(one, (ocean_fields, halos, opens, first_row))
        ocean_fields = jnp.where(is_live[:, None, None, None, None], ocean_fields, jnp.zeros_like(ocean_fields))
    return ocean_fields[:, :2], ocean_fields[:, 2:]
```

```python
import jax
import jax.numpy as jnp
from jax import lax
from jax.experimental import pallas as pl
from jax.experimental.pallas import tpu as pltpu
from jax.sharding import PartitionSpec as P

DEVICES = 256
ROWS, COLS = 26, 34
WIDTH = 128
CAP = 8
MORE = 10
EDGE = 16
MSG_EDGES = 18
MSG = MSG_EDGES * EDGE + 8
CHUNK = CAP * EDGE + 16
SWAP = 16 * EDGE + 8
F32 = jnp.float32
I32 = jnp.int32


def params(mib):
    return pltpu.CompilerParams(vmem_limit_bytes=mib * 1024 * 1024)


VM = pl.BlockSpec(memory_space=pltpu.VMEM)
SM = pl.BlockSpec(memory_space=pltpu.SMEM)
HB = pl.BlockSpec(memory_space=pl.ANY)


def grid_ids(block_counts, land):
    sea = 1 - land.reshape(-1).astype(I32)
    cells = jnp.arange(ROWS * COLS, dtype=I32)
    pos = jnp.sum(jnp.where(cells[None, :] < cells[:, None], sea[None, :], 0), axis=1)
    devs = jnp.arange(DEVICES, dtype=I32)
    ends = jnp.sum(jnp.where(devs[None, :] <= devs[:, None], block_counts[None, :], 0), axis=1)
    past = ends[None, :] <= pos[:, None]
    owner = jnp.sum(past.astype(I32), axis=1)
    start = jnp.max(jnp.where(past, ends[None, :], 0), axis=1)
    ids = jnp.where(sea == 1, owner * 4 + pos - start, -1)
    return ids.reshape(ROWS, COLS)


def neighbour_ids(ids):
    none = jnp.full((1, COLS), -1, I32)
    south = jnp.concatenate([none, ids[:-1]], axis=0)
    north = jnp.concatenate([ids[1:], ids[-1:, ::-1]], axis=0)

    def west(x):
        return jnp.concatenate([x[:, -1:], x[:, :-1]], axis=1)

    def east(x):
        return jnp.concatenate([x[:, 1:], x[:, :1]], axis=1)

    sides = [south, north, west(ids), east(ids), west(south), east(south), west(north), east(north)]
    return jnp.stack([x.reshape(-1) for x in sides])


def exclusive_count(mask):
    n = mask.shape[-1]
    i = jnp.arange(n)
    return jnp.sum(mask[..., None, :] & (i[None, :] < i[:, None]), axis=-1).astype(I32)


def make_tables(block_counts, land, me):
    column, zed, core = me >> 4, (me >> 1) & 7, me & 1
    ids = grid_ids(block_counts, land)
    near = neighbour_ids(ids)
    flat = ids.reshape(-1)
    chip_d = flat >> 3
    chip_s = near[:4] >> 3
    away = (near[:4] >= 0) & (flat >= 0) & (chip_s != chip_d)
    kind = jnp.where(away, (chip_s & 7) + 8 * (chip_s > chip_d), -1)
    kinds = jnp.sum(kind[:, :, None] == jnp.arange(16), axis=0).astype(jnp.bfloat16)
    chips = (chip_d[None, :] == jnp.arange(DEVICES // 2)[:, None]).astype(jnp.bfloat16)
    loads = jnp.dot(chips, kinds, preferred_element_type=F32)
    overflow = jnp.max(loads) > CAP + 0.5

    want = column * 64 + jnp.arange(64, dtype=I32)
    hit = flat[None, :] == want[:, None]
    cell = jnp.arange(ROWS * COLS, dtype=I32)
    mine = jnp.sum(jnp.where(hit[:, None, :], near[None] + 1, 0), axis=-1) - 1
    place = jnp.sum(jnp.where(hit, cell[None, :] + 1, 0), axis=-1) - 1
    live = place >= 0
    row = place // COLS
    col = place % COLS
    top = live & (row == ROWS - 1)

    chip_s = mine >> 3
    t_s = mine & 7
    z_s = chip_s & 7
    delta = jnp.abs((chip_s >> 3) - column)
    chip_d = column * 8 + jnp.arange(64, dtype=I32)[:, None] // 8
    valid = mine >= 0
    down = core == 1
    flow = valid & jnp.where(down, chip_s > chip_d, chip_s < chip_d)
    fold = top[:, None] & jnp.array([False, True, False, False])
    up_edge = jnp.stack([t_s[:, 0], t_s[:, 1], jnp.full((64,), 8, I32), jnp.full((64,), 9, I32)], axis=1)
    down_edge = jnp.stack(
        [t_s[:, 0], t_s[:, 1] + jnp.where(top, 10, 0), jnp.full((64,), 9, I32), jnp.full((64,), 8, I32)], axis=1
    )
    edge = jnp.where(down, down_edge, up_edge)
    at = (delta[:, :4] * MSG + edge * EDGE).reshape(8, 32)
    send = (flow[:, :4] & (z_s[:, :4] == zed)).reshape(8, 32)
    rank = exclusive_count(send)
    ranks = jnp.arange(CAP + MORE)
    picks = jnp.sum(jnp.where(send[:, None, :] & (rank[:, None, :] == ranks[None, :, None]), at[:, None, :], 0), axis=-1)

    def my_chip(x):
        x = lax.dynamic_slice_in_dim(x, zed * 8, 8, axis=0)
        return jnp.where(down, jnp.concatenate([x[4:], x[:4]]), x)

    got = my_chip(flow[:, :4]).reshape(32)
    got_z = my_chip(z_s[:, :4]).reshape(32)
    chip_flow = lax.dynamic_slice_in_dim(flow[:, :4], zed * 8, 8, axis=0).reshape(32)
    chip_z = lax.dynamic_slice_in_dim(z_s[:, :4], zed * 8, 8, axis=0).reshape(32)
    i32 = jnp.arange(32)
    before = chip_flow[None, :] & (chip_z[None, :] == chip_z[:, None]) & (i32[None, :] < i32[:, None])
    got_rank = jnp.sum(before, axis=1).astype(I32)
    got_rank = jnp.where(down, jnp.concatenate([got_rank[16:], got_rank[:16]]), got_rank)
    first = got & (got_rank < CAP)
    take = jnp.where(first, got_z * CHUNK + got_rank * EDGE, 0)

    same = chip_s == chip_d
    c_flow = my_chip((flow | (valid & same & (core == 0)))[:, 4:])
    hi = jnp.array([0, 1, 0, 1], I32)
    lane = jnp.where(
        (jnp.array([False, False, True, True])[None, :] & ~top[:, None]),
        16 + 2 * t_s[:, 4:] + hi,
        2 * t_s[:, 4:] + jnp.where(top[:, None] & jnp.array([False, False, True, True]), 1 - hi, hi),
    )
    lane = my_chip(lane + 32 * (delta[:, 4:] & 3))
    c_row = my_chip(z_s[:, 4:] * CHUNK + CAP * EDGE + 8 * (delta[:, 4:] >> 2))
    dst = (jnp.arange(8)[:, None] & 3) * 4 + jnp.arange(4)[None, :]
    c_take = jnp.where(c_flow, c_row, 0).reshape(32)
    c_turn = jnp.where(c_flow, (dst - lane) & 127, 0).reshape(32)
    c_dst = jnp.where(c_flow, dst, 999).reshape(32).astype(I32)

    def own(x):
        return my_chip(x)[:4]

    o_id, o_row, o_top, o_live = own(mine), own(row), own(top), own(live)
    o_chip, o_t = o_id[:, :4] >> 3, o_id[:, :4] & 7
    chip = me >> 1
    from_edge = jnp.stack([jnp.full((4,), 1, I32), jnp.where(o_top, 1, 0), jnp.full((4,), 3, I32), jnp.full((4,), 2, I32)], axis=1)
    here = (o_t * 4 + from_edge) * EDGE
    there = jnp.arange(16, dtype=I32).reshape(4, 4) * EDGE
    own_base, other_base = 8 * 4 * EDGE, 8 * 4 * EDGE + SWAP
    lower = o_chip < chip
    flown = there + jnp.where(lower == (core == 0), own_base, other_base)
    source = jnp.where(o_chip == chip, here, flown)
    source = jnp.where(o_id[:, :4] >= 0, source, 8 * 4 * EDGE + 2 * SWAP)

    c_live = lax.dynamic_slice_in_dim(live, zed * 8, 8, axis=0)
    c_col = lax.dynamic_slice_in_dim(col, zed * 8, 8, axis=0)
    t8 = jnp.arange(8, dtype=I32)
    last = jnp.max(jnp.where(c_live, t8, 0))
    zero_col = jnp.max(jnp.where(c_live & (c_col == 0), t8, 0))
    end_col = jnp.min(jnp.where(c_live & (c_col == COLS - 1), t8, 7))
    up = jnp.concatenate([t8 * 4 + 1, (last * 4 + 3)[None], (zero_col * 4 + 2)[None], t8 * 4 + 1])
    dn = jnp.concatenate([t8 * 4, jnp.array([2], I32), (end_col * 4 + 3)[None], t8 * 4 + 1])
    message = jnp.where(down, dn, up) * EDGE

    wet = (o_id >= 0).astype(F32)
    lanes = jnp.arange(WIDTH)
    low = jnp.stack([jnp.stack([wet[:, 6], wet[:, 4]], 1).reshape(8), jnp.stack([wet[:, 5], wet[:, 4]], 1).reshape(8)])
    high = jnp.stack([jnp.stack([wet[:, 7], wet[:, 5]], 1).reshape(8), jnp.stack([wet[:, 7], wet[:, 6]], 1).reshape(8)])
    low = jnp.where(lanes == 0, low[..., None], 1.0)
    high = jnp.where(lanes == WIDTH - 1, high[..., None], 1.0)
    rowf = o_row.astype(F32) * WIDTH
    y_n = jnp.where(o_top, rowf + (WIDTH - 1), rowf + WIDTH)
    y_row = jnp.stack([y_n, rowf - 1.0], axis=1).reshape(8, 1) + jnp.zeros((1, WIDTH), F32)
    y_col = jnp.repeat(rowf, 2)[:, None] + lanes.astype(F32)[None, :]
    cor = jnp.stack([y_row, y_col])
    cor = (cor + 0.5) * (2.0 / (ROWS * WIDTH))
    strips = jnp.stack([low, high, cor], axis=1)
    east = jnp.where(lanes == WIDTH - 1, wet[:, 3:4], 1.0)
    west = jnp.where(lanes == 0, wet[:, 2:3], 1.0)
    ones = jnp.ones((WIDTH,), F32)
    alive = o_live.astype(F32)
    faces = jnp.stack(
        [east, west, wet[:, 1:2] * ones, wet[:, 0:1] * ones, rowf[:, None] * ones, alive[:, None] * ones] + [jnp.zeros((4, WIDTH), F32)] * 2,
        axis=1,
    )

    final = jnp.concatenate([source.reshape(16), (o_top & (o_id[:, 1] >= 0)).astype(I32), core[None].astype(I32)])
    return {
        "overflow": overflow,
        "message": jnp.concatenate([message, core[None]]).astype(I32),
        "picks": picks.astype(I32),
        "take": jnp.concatenate([take, c_take, c_turn, c_dst]).astype(I32),
        "got": got,
        "got_z": got_z,
        "got_rank": got_rank,
        "final": final.astype(I32),
        "top": o_top.astype(I32),
        "strips": strips,
        "faces": faces,
    }


def rims_kernel(tr, ve, out, turned):
    lane = lax.broadcasted_iota(I32, (WIDTH, WIDTH), 1) // 4
    gathered = jnp.zeros((WIDTH, WIDTH), F32)
    for slot in range(4):
        for fl in range(8):
            ref, k = (tr, fl) if fl < 4 else (ve, fl - 4)
            for depth in range(2):
                out[slot, 0, pl.ds(depth * 8 + fl, 1), :] = ref[slot, k, pl.ds(depth, 1), :]
                out[slot, 1, pl.ds(depth * 8 + fl, 1), :] = ref[slot, k, pl.ds(127 - depth, 1), :]
            tile = slot * 8 + fl
            rolled = pltpu.roll(ref[slot, k], (4 * tile + 2) % WIDTH, 1)
            gathered = jnp.where(lane == tile, rolled, gathered)
    turned[...] = gathered.T
    for slot in range(4):
        for j, (side, depth) in enumerate([(3, 1), (3, 0), (2, 0), (2, 1)]):
            out[slot, side, pl.ds(depth * 8, 8), :] = turned[pl.ds(slot * 32 + j, 8, stride=4), :]


def message_kernel(table, mine, other, chip, out):
    core = table[MSG_EDGES]
    flag = core == 0
    for t in range(4):
        for side in range(4):
            at = (t * 4 + side) * EDGE
            a, b = mine[pl.ds(at, EDGE), :], other[pl.ds(at, EDGE), :]
            chip[pl.ds(at, EDGE), :] = jnp.where(flag, a, b)
            chip[pl.ds(16 * EDGE + at, EDGE), :] = jnp.where(flag, b, a)
    for e in range(MSG_EDGES):
        at = pl.multiple_of(table[e], EDGE)
        out[pl.ds(e * EDGE, EDGE), :] = chip[pl.ds(at, EDGE), :]
    lane = lax.broadcasted_iota(I32, (8, WIDTH), 1) // 2
    corners = jnp.zeros((8, WIDTH), F32)
    for t in range(8):
        for side, base in ((1, 0), (0, 8)):
            x = chip[pl.ds((t * 4 + side) * EDGE, 8), :]
            corners = jnp.where(lane == base + t, pltpu.roll(x, 2 * (base + t) + 1, 1), corners)
    out[pl.ds(MSG_EDGES * EDGE, 8), :] = corners


def pack_kernel(table, m0, m1, m2, m3, c4, c5, out, held, far, sem):
    copies = [pltpu.make_async_copy(m, held.at[pl.ds(i * MSG, MSG)], sem.at[i]) for i, m in enumerate((m0, m1, m2, m3))]
    copies += [pltpu.make_async_copy(m, far.at[pl.ds(i * 8, 8)], sem.at[4 + i]) for i, m in enumerate((c4, c5))]
    for copy in copies:
        copy.start()
    for copy in copies:
        copy.wait()
    lane = lax.broadcasted_iota(I32, (8, WIDTH), 1) // 32
    near_c = jnp.zeros((8, WIDTH), F32)
    for i in range(4):
        x = held[pl.ds(i * MSG + MSG_EDGES * EDGE, 8), :]
        near_c = jnp.where(lane == i, pltpu.roll(x, 32 * i, 1) if i else x, near_c)
    far_c = jnp.where(lane == 0, far[pl.ds(0, 8), :], pltpu.roll(far[pl.ds(8, 8), :], 32, 1))
    for z in range(8):
        for r in range(CAP):
            at = pl.multiple_of(table[z * CAP + r], 8)
            out[pl.ds(z * CHUNK + r * EDGE, EDGE), :] = held[pl.ds(at, EDGE), :]
        out[pl.ds(z * CHUNK + CAP * EDGE, 8), :] = near_c
        out[pl.ds(z * CHUNK + CAP * EDGE + 8, 8), :] = far_c


def sort_kernel(table, got, own, other):
    lane = lax.broadcasted_iota(I32, (8, WIDTH), 1)
    for half, out in enumerate((own, other)):
        for e in range(16):
            at = pl.multiple_of(table[half * 16 + e], 8)
            out[pl.ds(e * EDGE, EDGE), :] = got[pl.ds(at, EDGE), :]
        corners = jnp.zeros((8, WIDTH), F32)
        for e in range(16):
            i = half * 16 + e
            at = pl.multiple_of(table[32 + i], 8)
            x = pltpu.roll(got[pl.ds(at, 8), :], table[64 + i], 1)
            corners = jnp.where(lane == table[96 + i], x, corners)
        out[pl.ds(16 * EDGE, 8), :] = corners


def pressure(t0, t1, s0, s1):
    r0 = t0 * (-0.3 - 0.08 * t0 + 0.05 * s0) + 0.6 * s0
    r1 = t1 * (-0.3 - 0.08 * t1 + 0.05 * s1) + 0.6 * s1
    return 0.25 * r0, 0.5 * r0 + 0.25 * r1


def stencil(c, e, w, n, s, oe, ow, on, os, f):
    def times(o, x):
        return x if o is None else o * x

    ue, uw = 0.025 * (c[2] + e[2]), 0.025 * (w[2] + c[2])
    vn, vs = 0.025 * (c[3] + n[3]), 0.025 * (s[3] + c[3])
    ae, be = times(oe, 0.05 - ue), times(oe, 0.05 + ue)
    aw, bw = times(ow, 0.05 + uw), times(ow, 0.05 - uw)
    an, bn = times(on, 0.05 - vn), times(on, 0.05 + vn)
    as_, bs = times(os, 0.05 + vs), times(os, 0.05 - vs)
    mid = 1.0 - ((be + bw) + (bn + bs))
    out = []
    for i in range(2):
        out.append(mid * c[i] + ((ae * e[i] + aw * w[i]) + (an * n[i] + as_ * s[i])))
    for i, (lo, hi, olo, ohi) in ((2, (w, e, ow, oe)), (3, (s, n, os, on))):
        lap = (times(oe, e[i] - c[i]) + times(ow, w[i] - c[i])) + (times(on, n[i] - c[i]) + times(os, s[i] - c[i]))
        grad = times(ohi, hi[4] - c[4]) + times(olo, c[4] - lo[4])
        turn = f * c[3] if i == 2 else -(f * c[2])
        out.append(c[i] + (0.1 * turn + 0.05 * (lap - grad)))
    return out


def steps_kernel(table, chip, own, other, strips, faces, tr, ve, tr_out, ve_out, held, hx, inn, crv, upd, cols, xa, xb, sem):
    sizes = (8 * 4 * EDGE, SWAP, SWAP)
    starts = (0, sizes[0], sizes[0] + SWAP)
    copies = [
        pltpu.make_async_copy(x, held.at[pl.ds(at, n)], sem.at[i]) for i, (x, at, n) in enumerate(zip((chip, own, other), starts, sizes))
    ]
    for copy in copies:
        copy.start()
    held[pl.ds(starts[2] + SWAP, EDGE), :] = jnp.zeros((EDGE, WIDTH), F32)
    for copy in copies:
        copy.wait()
    core = table[20]
    i0 = lax.broadcasted_iota(I32, (WIDTH, WIDTH), 0)
    i1 = lax.broadcasted_iota(I32, (WIDTH, WIDTH), 1)
    mirror = (i0 + i1 == WIDTH - 1).astype(F32)
    sub16 = lax.broadcasted_iota(I32, (EDGE, WIDTH), 0)
    sign = jnp.where((sub16 & 7) >= 4, -1.0, 1.0)
    lane8 = lax.broadcasted_iota(I32, (8, WIDTH), 1)
    sub8 = lax.broadcasted_iota(I32, (8, WIDTH), 0)
    even = (sub8 & 1) == 0
    corners = held[pl.ds(starts[1] + 16 * EDGE, 8), :] + held[pl.ds(starts[2] + 16 * EDGE, 8), :]
    sign8 = jnp.where(sub8 >= 4, -1.0, 1.0)

    for slot in range(4):
        fold = table[16 + slot] == 1
        top = table[21 + slot] == 1
        for side in range(4):
            at = pl.multiple_of(table[slot * 4 + side], 8)
            x = held[pl.ds(at, EDGE), :]
            if side == 1:
                flipped = jnp.dot(x, mirror, preferred_element_type=F32, precision=lax.Precision.HIGHEST) * sign
                x = jnp.where(fold, flipped, x)
            group, row = (0, 1) if side == 0 else (0, 0) if side == 1 else (1, 1) if side == 2 else (1, 0)
            row += slot * 2
            hx[group, :, row, :] = x
            inner = held[pl.ds(pl.multiple_of(core * (16 * EDGE) + (slot * 4 + side) * EDGE, 8), 8), :]
            inn[group, :, row, :] = inner
        for group, odd, lo, hi in ((0, 0, 2, 3), (0, 1, 0, 1), (1, 0, 1, 3), (1, 1, 0, 2)):
            vals = []
            for which, lane in ((lo, 0), (hi, WIDTH - 1)):
                v = pltpu.roll(corners, (lane - (slot * 4 + which)) % WIDTH, 1)
                if which >= 2:
                    v = jnp.where(top, v * sign8, v)
                vals.append(v)
            crv[group, :, slot * 2 + odd, :] = jnp.where(lane8 == 0, vals[0], vals[1])

    for group in range(2):
        low_o, high_o, cor = strips[group, 0], strips[group, 1], strips[group, 2]
        at_c, at_p, at_m, at_h, at_l = [], [], [], [], []
        for q in range(8):
            c, outer, inner, k = hx[group, q], hx[group, 8 + q], inn[group, q], crv[group, q]
            at_c.append(c)
            at_p.append(jnp.where(even, outer, inner))
            at_m.append(jnp.where(even, inner, outer))
            at_h.append(jnp.where(lane8 == WIDTH - 1, k, pltpu.roll(c, WIDTH - 1, 1)))
            at_l.append(jnp.where(lane8 == 0, k, pltpu.roll(c, 1, 1)))
        five = [x + list(pressure(x[0], x[1], x[2], x[3])) for x in (at_c, at_p, at_m, at_h, at_l)]
        for level in range(2):
            c, p, m, h, l = [[x[2 * i + level] for i in range(5)] for x in five]
            if group == 0:
                new = stencil(c, h, l, p, m, high_o, low_o, None, None, cor)
            else:
                new = stencil(c, p, m, h, l, None, None, high_o, low_o, cor)
            for i in range(4):
                upd[group, 2 * i + level] = new[i]

    for step in range(2):
        parts = [(hx if step == 0 else upd)[1, q] for q in range(8)]
        parts += list(pressure(parts[0], parts[1], parts[2], parts[3]))
        parts += [jnp.zeros((WIDTH - 80, WIDTH), F32)]
        cols[step] = jnp.concatenate(parts, axis=0).T

    lane = lax.broadcasted_iota(I32, (EDGE, WIDTH), 1)
    y16 = lax.broadcasted_iota(I32, (EDGE, WIDTH), 0).astype(F32)
    at_lo, at_hi = sub16 == 0, sub16 == EDGE - 1

    def one_slot(slot, carry):
        oe, ow = faces[slot, pl.ds(0, 1), :], faces[slot, pl.ds(1, 1), :]
        on, os = faces[slot, pl.ds(2, 1), :], faces[slot, pl.ds(3, 1), :]
        base = faces[slot, pl.ds(4, 1), :]
        alive = faces[slot, pl.ds(5, 1), :] > 0.5
        on16 = jnp.where(at_hi, on, 1.0)
        os16 = jnp.where(at_lo, os, 1.0)
        for step in range(2):
            src = xa if step == 0 else xb
            halo = hx if step == 0 else upd
            for q in range(8):
                src[q, pl.ds(7, 1), :] = halo[0, q, pl.ds(slot * 2 + 1, 1), :]
                src[q, pl.ds(136, 1), :] = halo[0, q, pl.ds(slot * 2, 1), :]
            if step == 0:
                for q in range(8):
                    ref, k = (tr, q) if q < 4 else (ve, q - 4)
                    src[q, pl.ds(8, WIDTH), :] = ref[slot, k]
            for r in range(0, 144, 16):
                p0, p1 = pressure(*[src[q, pl.ds(r, 16), :] for q in range(4)])
                src[8, pl.ds(r, 16), :] = p0
                src[9, pl.ds(r, 16), :] = p1
            for r in range(0, WIDTH, EDGE):
                f = (base + (y16 + (r + 0.5))) * (2.0 / (ROWS * WIDTH))
                for level in range(2):
                    c, e, w, n, s = [], [], [], [], []
                    for i in range(5):
                        q = 2 * i + level
                        x = src[q, pl.ds(8 + r, EDGE), :]
                        edge = pltpu.roll(cols[step, pl.ds(r, EDGE), :], WIDTH - 1 - q * 8 - 2 * slot, 1)
                        c.append(x)
                        e.append(jnp.where(lane == WIDTH - 1, edge, pltpu.roll(x, WIDTH - 1, 1)))
                        w.append(jnp.where(lane == 0, edge, pltpu.roll(x, 1, 1)))
                        n.append(src[q, pl.ds(9 + r, EDGE), :])
                        s.append(src[q, pl.ds(7 + r, EDGE), :])
                    new = stencil(
                        c, e, w, n, s, oe, ow, on16 if r == WIDTH - EDGE else None, os16 if r == 0 else None, f
                    )
                    for i in range(4):
                        if step == 0:
                            xb[2 * i + level, pl.ds(8 + r, EDGE), :] = new[i]
                        else:
                            out = tr_out if i < 2 else ve_out
                            out[slot, 2 * (i % 2) + level, pl.ds(r, EDGE), :] = jnp.where(alive, new[i], 0.0)
        return carry

    for src in (xa, xb):
        for q in range(8):
            src[q, pl.ds(0, 8), :] = jnp.zeros((8, WIDTH), F32)
            src[q, pl.ds(136, 8), :] = jnp.zeros((8, WIDTH), F32)
    lax.fori_loop(0, 4, one_slot, 0)


def shape(*dims):
    return jax.ShapeDtypeStruct(dims, F32)


def permute(x, pairs):
    return lax.ppermute(x, "blk", pairs)


def column_pairs(distance):
    pairs = []
    for i in range(DEVICES):
        j = i + 16 * distance * (1 if i % 2 == 0 else -1)
        if 0 <= j < DEVICES:
            pairs.append((i, j))
    return pairs


def exchange_z(x):
    groups = [[16 * a + 2 * z + c for z in range(8)] for a in range(16) for c in range(2)]
    return lax.all_to_all(x, "blk", 0, 0, axis_index_groups=groups, tiled=True)


def per_device(tracers, velocity, block_counts, land):
    me = lax.axis_index("blk").astype(I32)
    tab = make_tables(block_counts, land, me)
    tr = tracers.reshape(4, 4, WIDTH, WIDTH)
    ve = velocity.reshape(4, 4, WIDTH, WIDTH)
    swap = [(i, i ^ 1) for i in range(DEVICES)]

    rims = pl.pallas_call(
        rims_kernel,
        out_shape=shape(4, 4, EDGE, WIDTH),
        in_specs=[VM, VM],
        out_specs=VM,
        scratch_shapes=[pltpu.VMEM((WIDTH, WIDTH), F32)],
        compiler_params=params(16),
        name="rims",
    )(tr, ve)
    rims = rims.reshape(16 * EDGE, WIDTH)
    other = permute(rims, swap)
    chip, message = pl.pallas_call(
        message_kernel,
        out_shape=(shape(32 * EDGE, WIDTH), shape(MSG, WIDTH)),
        in_specs=[SM, VM, VM],
        out_specs=(VM, VM),
        compiler_params=params(16),
        name="message",
    )(tab["message"], rims, other)
    near = [permute(message, column_pairs(d)) for d in (1, 2, 3)]
    corners = message[MSG_EDGES * EDGE :]
    far = [permute(corners, column_pairs(d)) for d in (4, 5)]
    chunks = pl.pallas_call(
        pack_kernel,
        out_shape=shape(8 * CHUNK, WIDTH),
        in_specs=[SM] + [HB] * 6,
        out_specs=VM,
        scratch_shapes=[pltpu.VMEM((4 * MSG, WIDTH), F32), pltpu.VMEM((16, WIDTH), F32), pltpu.SemaphoreType.DMA((6,))],
        compiler_params=params(16),
        name="pack",
    )(tab["picks"][:, :CAP].reshape(-1), message, *near, *far)
    got = exchange_z(chunks.reshape(8, CHUNK, WIDTH)).reshape(8 * CHUNK, WIDTH)
    own, others = pl.pallas_call(
        sort_kernel,
        out_shape=(shape(SWAP, WIDTH), shape(SWAP, WIDTH)),
        in_specs=[SM, VM],
        out_specs=(VM, VM),
        compiler_params=params(16),
        name="sort",
    )(tab["take"], got)

    def second(args):
        own, others, message, near = args
        held = jnp.concatenate([message, *near])
        rows = tab["picks"][:, CAP:, None] + jnp.arange(EDGE, dtype=I32)
        more = exchange_z(held[rows].reshape(8, MORE * EDGE, WIDTH)).reshape(8 * MORE * EDGE, WIDTH)
        late = tab["got"] & (tab["got_rank"] >= CAP)
        start = jnp.where(late, tab["got_z"] * (MORE * EDGE) + (tab["got_rank"] - CAP) * EDGE, 0)
        new = more[start[:, None] + jnp.arange(EDGE, dtype=I32)]
        old = jnp.stack([own[: 16 * EDGE], others[: 16 * EDGE]]).reshape(32, EDGE, WIDTH)
        new = jnp.where(late[:, None, None], new, old).reshape(2, 16 * EDGE, WIDTH)
        return jnp.concatenate([new[0], own[16 * EDGE :]]), jnp.concatenate([new[1], others[16 * EDGE :]])

    own, others = lax.cond(tab["overflow"], second, lambda args: (args[0], args[1]), (own, others, message, near))
    theirs = permute(others, swap)

    tr_new, ve_new = pl.pallas_call(
        steps_kernel,
        out_shape=(shape(4, 4, WIDTH, WIDTH), shape(4, 4, WIDTH, WIDTH)),
        in_specs=[SM] + [HB] * 3 + [VM] * 4,
        out_specs=(VM, VM),
        scratch_shapes=[
            pltpu.VMEM((32 * EDGE + 2 * SWAP + EDGE, WIDTH), F32),
            pltpu.VMEM((2, EDGE, 8, WIDTH), F32),
            pltpu.VMEM((2, 8, 8, WIDTH), F32),
            pltpu.VMEM((2, 8, 8, WIDTH), F32),
            pltpu.VMEM((2, 8, 8, WIDTH), F32),
            pltpu.VMEM((2, WIDTH, WIDTH), F32),
            pltpu.VMEM((10, 144, WIDTH), F32),
            pltpu.VMEM((10, 144, WIDTH), F32),
            pltpu.SemaphoreType.DMA((3,)),
        ],
        compiler_params=params(32),
        name="steps",
    )(jnp.concatenate([tab["final"], tab["top"]]), chip, own, theirs, tab["strips"], tab["faces"], tr, ve)
    return tr_new.reshape(tracers.shape), ve_new.reshape(velocity.shape)


def solution(mesh):
    spec = P("blk", None, None, None, None)
    return jax.shard_map(
        per_device,
        mesh=mesh,
        in_specs=(spec, spec, P(), P()),
        out_specs=(spec, spec),
        check_vma=False,
    )
```

```python
import jax
import jax.numpy as jnp
from jax import lax
from jax.experimental import pallas as pl
from jax.experimental.pallas import tpu as pltpu
from jax.sharding import PartitionSpec as P

DEVICES = 256
ROWS, COLS = 26, 34
WIDTH = 128
CAP = 8
MORE = 10
EDGE = 16
MSG_EDGES = 18
MSG = MSG_EDGES * EDGE + 8
CHUNK = CAP * EDGE + 16
SWAP = 16 * EDGE + 8
F32 = jnp.float32
I32 = jnp.int32


def params(mib):
    return pltpu.CompilerParams(vmem_limit_bytes=mib * 1024 * 1024)


VM = pl.BlockSpec(memory_space=pltpu.VMEM)
SM = pl.BlockSpec(memory_space=pltpu.SMEM)
HB = pl.BlockSpec(memory_space=pl.ANY)


CODES = 28


def lane_iota(rows):
    return lax.broadcasted_iota(I32, (rows, WIDTH), 1)


def row_iota(rows):
    return lax.broadcasted_iota(I32, (rows, WIDTH), 0)


def exact_dot(a, b):
    return jnp.dot(a.astype(jnp.bfloat16), b.astype(jnp.bfloat16), preferred_element_type=F32)


def build_tables(me, counts, land, board, codes, mine, load):
    column, zed, core = me >> 4, (me >> 1) & 7, me & 1
    board[...] = jnp.ones((32, WIDTH), I32)
    board[pl.ds(0, ROWS), pl.ds(0, COLS)] = land[...]
    sea = board[...] == 0
    lane, row = lane_iota(32), row_iota(32)
    ones = sea.astype(F32)
    i, j = row_iota(WIDTH), lane_iota(WIDTH)
    along = exact_dot(ones, i <= j)
    totals = exact_dot(ones, i >= 0)
    li, lj = lax.broadcasted_iota(I32, (32, 32), 0), lax.broadcasted_iota(I32, (32, 32), 1)
    pos = (exact_dot(lj < li, totals) + along - ones).astype(I32)

    def device(n, carry):
        end, owner, start = carry
        for k in range(8):
            d = n * 8 + k
            end = end + counts[d]
            past = pos >= end
            owner = jnp.where(past, d + 1, owner)
            start = jnp.where(past, end, start)
        return end, owner, start

    zero = jnp.zeros((32, WIDTH), I32)
    _, owner, start = lax.fori_loop(0, DEVICES // 8, device, (jnp.int32(0), zero, zero))
    ids = jnp.where(sea, owner * 4 + pos - start, -1).astype(F32)

    def west(x):
        return jnp.where(lane == 0, pltpu.roll(x, WIDTH - COLS + 1, 1), pltpu.roll(x, 1, 1))

    def east(x):
        return jnp.where(lane == COLS - 1, pltpu.roll(x, COLS - 1, 1), pltpu.roll(x, WIDTH - 1, 1))

    mirror = (i + j == COLS - 1).astype(F32)
    folded = jnp.dot(ids, mirror, preferred_element_type=F32, precision=lax.Precision.HIGHEST)
    south = jnp.where(row == 0, -1.0, pltpu.roll(ids, 1, 0))
    north = jnp.where(row == ROWS - 1, folded, pltpu.roll(ids, 31, 0))
    near = [south, north, west(ids), east(ids), west(south), east(south), west(north), east(north)]
    pairs = [(near[2 * k] + 1.0) * 2048.0 + (near[2 * k + 1] + 1.0) for k in range(4)]
    place = (row * WIDTH + lane).astype(F32)

    chip = jnp.right_shift(ids.astype(I32), 3)
    kinds = []
    for k in range(4):
        source = jnp.right_shift(near[k].astype(I32), 3)
        away = sea & (source >= 0) & (source != chip)
        kinds.append(jnp.where(away, (source & 7) + jnp.where(source > chip, 8, 0), -1))
    kind_row = row_iota(16)
    counted = jnp.zeros((WIDTH, 16), F32)
    for r in range(ROWS):
        is_chip = (chip[r : r + 1, :] == i).astype(jnp.bfloat16)
        of_kind = sum((kinds[k][r : r + 1, :] == kind_row).astype(F32) for k in range(4)).astype(jnp.bfloat16)
        counted += lax.dot_general(is_chip, of_kind, (((1,), (1,)), ((), ())), preferred_element_type=F32)
    load[...] = jnp.broadcast_to(jnp.max(counted), (8, WIDTH)).astype(I32)

    slot = row_iota(64)
    want = (column * 64 + slot).astype(F32)
    found = [jnp.zeros((64, WIDTH), F32) for _ in range(4)] + [jnp.full((64, WIDTH), -1.0, F32)]
    for r in range(ROWS):
        hit = ids[r : r + 1, :] == want
        for k, x in enumerate(pairs + [place]):
            found[k] = jnp.where(hit, x[r : r + 1, :], found[k])
    found = [jnp.max(x, axis=1, keepdims=True).astype(I32) for x in found]
    place = found[4]
    live = place >= 0
    block_row, block_col = jnp.right_shift(place, 7), place & 127
    top = live & (block_row == ROWS - 1)
    ids8 = []
    for k in range(4):
        ids8 += [jnp.right_shift(found[k], 11) - 1, (found[k] & 2047) - 1]
    slot1 = lax.broadcasted_iota(I32, (64, 1), 0)
    here = column * 8 + jnp.right_shift(slot1, 3)
    down = core == 1
    items = {}
    for k in range(8):
        valid = ids8[k] >= 0
        source, t = jnp.right_shift(ids8[k], 3), ids8[k] & 7
        z, delta = source & 7, jnp.abs(jnp.right_shift(source, 3) - column)
        lower, same = source < here, source == here
        items[16 + k] = valid.astype(I32)
        if k < 4:
            flow = valid & ~same & (lower != down)
            if k < 2:
                edge = t if k == 0 else t + jnp.where(top & down, 10, 0)
            else:
                edge = jnp.where(down, 11 - k, 6 + k)
            at = delta * (MSG // 8) + edge * (EDGE // 8) + 1
            items[k] = jnp.where(flow & (z == zed), at, 0)
            items[4 + k] = jnp.where(flow, z, -1)
            of = (1, 0, 3, 2)[k]
            if k == 1:
                of = jnp.where(top, 1, 0)
            close = (t * 4 + of) * (EDGE // 8)
            base = jnp.where(lower != down, 4 * EDGE, 4 * EDGE + SWAP // 8)
            far = ((slot1 & 3) * 4 + k) * (EDGE // 8) + base
            items[8 + k] = jnp.where(valid, jnp.where(same, close, far), 4 * EDGE + 2 * SWAP // 8)
        else:
            flow = valid & ((lower | same) != down)
            hi = (0, 1, 0, 1)[k - 4]
            lane_at = 2 * t + hi
            if k >= 6:
                lane_at = jnp.where(top, 2 * t + 1 - hi, 16 + 2 * t + hi)
            at = z * (CHUNK // 8) + CAP * EDGE // 8 + jnp.right_shift(delta, 2)
            items[8 + k] = jnp.where(flow, at * WIDTH + 32 * (delta & 3) + lane_at, -1)
    items[24], items[25], items[26], items[27] = live.astype(I32), top.astype(I32), block_row, block_col
    lane64 = lane_iota(64)
    table = jnp.zeros((64, WIDTH), I32)
    for k in range(CODES):
        table = jnp.where(lane64 == k, items[k], table)
    codes[...] = table
    mine[...] = codes[pl.ds(pl.multiple_of(zed * 8, 8), 8), :]


def start_kernel(counts, land, tr_hbm, ve_hbm, out, codes, mine, load, board, tr, ve, turned, sem):
    copies = [pltpu.make_async_copy(tr_hbm, tr, sem.at[0]), pltpu.make_async_copy(ve_hbm, ve, sem.at[1])]
    for copy in copies:
        copy.start()
    build_tables(lax.axis_index("blk").astype(I32), counts, land, board, codes, mine, load)
    for copy in copies:
        copy.wait()
    lane = lane_iota(WIDTH) // 4
    gathered = jnp.zeros((WIDTH, WIDTH), F32)
    for slot in range(4):
        for fl in range(8):
            ref, k = (tr, fl) if fl < 4 else (ve, fl - 4)
            for depth in range(2):
                out[pl.ds((slot * 4 + 0) * EDGE + depth * 8 + fl, 1), :] = ref[slot, k, pl.ds(depth, 1), :]
                out[pl.ds((slot * 4 + 1) * EDGE + depth * 8 + fl, 1), :] = ref[slot, k, pl.ds(127 - depth, 1), :]
            tile = slot * 8 + fl
            rolled = pltpu.roll(ref[slot, k], (4 * tile + 2) % WIDTH, 1)
            gathered = jnp.where(lane == tile, rolled, gathered)
    turned[...] = gathered.T
    for slot in range(4):
        for j, (side, depth) in enumerate([(3, 1), (3, 0), (2, 0), (2, 1)]):
            out[pl.ds((slot * 4 + side) * EDGE + depth * 8, 8), :] = turned[pl.ds(slot * 32 + j, 8, stride=4), :]


def message_kernel(table, mine, other, chip, out):
    core = lax.axis_index("blk").astype(I32) & 1
    flag = core == 0
    for t in range(4):
        for side in range(4):
            at = (t * 4 + side) * EDGE
            a, b = mine[pl.ds(at, EDGE), :], other[pl.ds(at, EDGE), :]
            chip[pl.ds(at, EDGE), :] = jnp.where(flag, a, b)
            chip[pl.ds(16 * EDGE + at, EDGE), :] = jnp.where(flag, b, a)
    last, first_col, last_col = jnp.int32(0), jnp.int32(0), jnp.int32(0)
    for t in range(8):
        live, col = table[t, 24] == 1, table[t, 27]
        last = jnp.where(live, t, last)
        first_col = jnp.where(live & (col == 0), t, first_col)
        live, col = table[7 - t, 24] == 1, table[7 - t, 27]
        last_col = jnp.where(live & (col == COLS - 1), 7 - t, last_col)
    for t in range(8):
        at = pl.multiple_of(jnp.where(flag, t * 4 + 1, t * 4) * EDGE, EDGE)
        out[pl.ds(t * EDGE, EDGE), :] = chip[pl.ds(at, EDGE), :]
        out[pl.ds((10 + t) * EDGE, EDGE), :] = chip[pl.ds((t * 4 + 1) * EDGE, EDGE), :]
    for e, edge in ((8, jnp.where(flag, last * 4 + 3, 2)), (9, jnp.where(flag, first_col * 4 + 2, last_col * 4 + 3))):
        at = pl.multiple_of(edge * EDGE, EDGE)
        out[pl.ds(e * EDGE, EDGE), :] = chip[pl.ds(at, EDGE), :]
    lane = lax.broadcasted_iota(I32, (8, WIDTH), 1) // 2
    corners = jnp.zeros((8, WIDTH), F32)
    for t in range(8):
        for side, base in ((1, 0), (0, 8)):
            x = chip[pl.ds((t * 4 + side) * EDGE, 8), :]
            corners = jnp.where(lane == base + t, pltpu.roll(x, 2 * (base + t) + 1, 1), corners)
    out[pl.ds(MSG_EDGES * EDGE, 8), :] = corners


def pack_kernel(codes, m0, m1, m2, m3, c4, c5, out, held, far, table, sem):
    copies = [pltpu.make_async_copy(m, held.at[pl.ds(i * MSG, MSG)], sem.at[i]) for i, m in enumerate((m0, m1, m2, m3))]
    copies += [pltpu.make_async_copy(m, far.at[pl.ds(i * 8, 8)], sem.at[4 + i]) for i, m in enumerate((c4, c5))]
    for copy in copies:
        copy.start()
    for z in range(8):
        for r in range(CAP):
            table[z * 32 + r] = 0
        count = jnp.int32(0)
        for t in range(8):
            for side in range(4):
                code = codes[z * 8 + t, side]
                table[z * 32 + count] = code
                count += (code > 0).astype(I32)
    for copy in copies:
        copy.wait()
    lane = lax.broadcasted_iota(I32, (8, WIDTH), 1) // 32
    near_c = jnp.zeros((8, WIDTH), F32)
    for i in range(4):
        x = held[pl.ds(i * MSG + MSG_EDGES * EDGE, 8), :]
        near_c = jnp.where(lane == i, pltpu.roll(x, 32 * i, 1) if i else x, near_c)
    far_c = jnp.where(lane == 0, far[pl.ds(0, 8), :], pltpu.roll(far[pl.ds(8, 8), :], 32, 1))
    for z in range(8):
        for r in range(CAP):
            at = pl.multiple_of(jnp.maximum(table[z * 32 + r] - 1, 0) * 8, 8)
            out[pl.ds(z * CHUNK + r * EDGE, EDGE), :] = held[pl.ds(at, EDGE), :]
        out[pl.ds(z * CHUNK + CAP * EDGE, 8), :] = near_c
        out[pl.ds(z * CHUNK + CAP * EDGE + 8, 8), :] = far_c


def sort_kernel(table, got, own, other, taken, rows):
    core = lax.axis_index("blk").astype(I32) & 1
    for z in range(8):
        taken[z] = 0
    for t in range(8):
        for side in range(4):
            code = table[t, 4 + side]
            z = jnp.maximum(code, 0)
            rank = taken[z]
            taken[z] = rank + (code >= 0).astype(I32)
            rows[t * 4 + side] = z * CHUNK + jnp.minimum(rank, CAP - 1) * EDGE
    lane = lane_iota(8)
    for half, out in enumerate((own, other)):
        first = (core ^ half) * 4
        corners = jnp.zeros((8, WIDTH), F32)
        for e in range(16):
            at = pl.multiple_of(rows[first * 4 + e], 8)
            out[pl.ds(e * EDGE, EDGE), :] = got[pl.ds(at, EDGE), :]
            code = table[first + e // 4, 12 + e % 4]
            turn = (e - code) & (WIDTH - 1)
            at = pl.multiple_of(jnp.right_shift(jnp.maximum(code, 0), 7) * 8, 8)
            corners = jnp.where(lane == jnp.where(code >= 0, e, -1), pltpu.roll(got[pl.ds(at, 8), :], turn, 1), corners)
        out[pl.ds(16 * EDGE, 8), :] = corners


def pressure(t0, t1, s0, s1):
    r0 = t0 * (-0.3 - 0.08 * t0 + 0.05 * s0) + 0.6 * s0
    r1 = t1 * (-0.3 - 0.08 * t1 + 0.05 * s1) + 0.6 * s1
    return 0.25 * r0, 0.5 * r0 + 0.25 * r1


def stencil(c, e, w, n, s, oe, ow, on, os, f):
    def times(o, x):
        return x if o is None else o * x

    ue, uw = 0.025 * (c[2] + e[2]), 0.025 * (w[2] + c[2])
    vn, vs = 0.025 * (c[3] + n[3]), 0.025 * (s[3] + c[3])
    ae, be = times(oe, 0.05 - ue), times(oe, 0.05 + ue)
    aw, bw = times(ow, 0.05 + uw), times(ow, 0.05 - uw)
    an, bn = times(on, 0.05 - vn), times(on, 0.05 + vn)
    as_, bs = times(os, 0.05 + vs), times(os, 0.05 - vs)
    mid = 1.0 - ((be + bw) + (bn + bs))
    out = []
    for i in range(2):
        out.append(mid * c[i] + ((ae * e[i] + aw * w[i]) + (an * n[i] + as_ * s[i])))
    for i, (lo, hi, olo, ohi) in ((2, (w, e, ow, oe)), (3, (s, n, os, on))):
        lap = (times(oe, e[i] - c[i]) + times(ow, w[i] - c[i])) + (times(on, n[i] - c[i]) + times(os, s[i] - c[i]))
        grad = times(ohi, hi[4] - c[4]) + times(olo, c[4] - lo[4])
        turn = f * c[3] if i == 2 else -(f * c[2])
        out.append(c[i] + (0.1 * turn + 0.05 * (lap - grad)))
    return out


def steps_kernel(table, chip, own, other, tr, ve, tr_out, ve_out, held, hx, inn, crv, upd, cols, xa, xb, sem):
    sizes = (8 * 4 * EDGE, SWAP, SWAP)
    starts = (0, sizes[0], sizes[0] + SWAP)
    copies = [
        pltpu.make_async_copy(x, held.at[pl.ds(at, n)], sem.at[i]) for i, (x, at, n) in enumerate(zip((chip, own, other), starts, sizes))
    ]
    for copy in copies:
        copy.start()
    held[pl.ds(starts[2] + SWAP, EDGE), :] = jnp.zeros((EDGE, WIDTH), F32)
    for copy in copies:
        copy.wait()
    core = lax.axis_index("blk").astype(I32) & 1

    def item(slot, k):
        return table[core * 4 + slot, k]

    def factor(slot, k):
        return item(slot, k).astype(F32)

    i0 = lax.broadcasted_iota(I32, (WIDTH, WIDTH), 0)
    i1 = lax.broadcasted_iota(I32, (WIDTH, WIDTH), 1)
    mirror = (i0 + i1 == WIDTH - 1).astype(F32)
    sub16 = lax.broadcasted_iota(I32, (EDGE, WIDTH), 0)
    sign = jnp.where((sub16 & 7) >= 4, -1.0, 1.0)
    lane8 = lax.broadcasted_iota(I32, (8, WIDTH), 1)
    sub8 = lax.broadcasted_iota(I32, (8, WIDTH), 0)
    even = (sub8 & 1) == 0
    corners = held[pl.ds(starts[1] + 16 * EDGE, 8), :] + held[pl.ds(starts[2] + 16 * EDGE, 8), :]
    sign8 = jnp.where(sub8 >= 4, -1.0, 1.0)

    for slot in range(4):
        top = item(slot, 25) == 1
        for side in range(4):
            at = pl.multiple_of(item(slot, 8 + side) * 8, 8)
            x = held[pl.ds(at, EDGE), :]
            if side == 1:
                flipped = jnp.dot(x, mirror, preferred_element_type=F32, precision=lax.Precision.HIGHEST) * sign
                x = jnp.where(top, flipped, x)
            group, row = (0, 1) if side == 0 else (0, 0) if side == 1 else (1, 1) if side == 2 else (1, 0)
            row += slot * 2
            hx[group, :, row, :] = x
            inner = held[pl.ds(pl.multiple_of(core * (16 * EDGE) + (slot * 4 + side) * EDGE, 8), 8), :]
            inn[group, :, row, :] = inner
        for group, odd, lo, hi in ((0, 0, 2, 3), (0, 1, 0, 1), (1, 0, 1, 3), (1, 1, 0, 2)):
            vals = []
            for which, lane in ((lo, 0), (hi, WIDTH - 1)):
                v = pltpu.roll(corners, (lane - (slot * 4 + which)) % WIDTH, 1)
                if which >= 2:
                    v = jnp.where(top, v * sign8, v)
                vals.append(v)
            crv[group, :, slot * 2 + odd, :] = jnp.where(lane8 == 0, vals[0], vals[1])

    for group in range(2):
        low_o, high_o, cor = jnp.ones((8, WIDTH), F32), jnp.ones((8, WIDTH), F32), jnp.zeros((8, WIDTH), F32)
        for slot in range(4):
            first = factor(slot, 26) * float(WIDTH)
            for odd in range(2):
                lo, hi = ((22, 23), (20, 21))[odd] if group == 0 else ((21, 23), (20, 22))[odd]
                here = sub8 == slot * 2 + odd
                low_o = jnp.where(here & (lane8 == 0), factor(slot, lo), low_o)
                high_o = jnp.where(here & (lane8 == WIDTH - 1), factor(slot, hi), high_o)
                if group == 1:
                    y = first
                elif odd:
                    y = first - 1.0
                else:
                    y = first + jnp.where(item(slot, 25) == 1, WIDTH - 1.0, float(WIDTH))
                cor = jnp.where(here, y, cor)
        if group == 1:
            cor = cor + lane8.astype(F32)
        cor = (cor + 0.5) * (2.0 / (ROWS * WIDTH))
        at_c, at_p, at_m, at_h, at_l = [], [], [], [], []
        for q in range(8):
            c, outer, inner, k = hx[group, q], hx[group, 8 + q], inn[group, q], crv[group, q]
            at_c.append(c)
            at_p.append(jnp.where(even, outer, inner))
            at_m.append(jnp.where(even, inner, outer))
            at_h.append(jnp.where(lane8 == WIDTH - 1, k, pltpu.roll(c, WIDTH - 1, 1)))
            at_l.append(jnp.where(lane8 == 0, k, pltpu.roll(c, 1, 1)))
        five = [x + list(pressure(x[0], x[1], x[2], x[3])) for x in (at_c, at_p, at_m, at_h, at_l)]
        for level in range(2):
            c, p, m, h, l = [[x[2 * i + level] for i in range(5)] for x in five]
            if group == 0:
                new = stencil(c, h, l, p, m, high_o, low_o, None, None, cor)
            else:
                new = stencil(c, p, m, h, l, None, None, high_o, low_o, cor)
            for i in range(4):
                upd[group, 2 * i + level] = new[i]

    for step in range(2):
        parts = [(hx if step == 0 else upd)[1, q] for q in range(8)]
        parts += list(pressure(parts[0], parts[1], parts[2], parts[3]))
        parts += [jnp.zeros((WIDTH - 80, WIDTH), F32)]
        cols[step] = jnp.concatenate(parts, axis=0).T

    lane = lax.broadcasted_iota(I32, (EDGE, WIDTH), 1)
    y16 = lax.broadcasted_iota(I32, (EDGE, WIDTH), 0).astype(F32)
    at_lo, at_hi = sub16 == 0, sub16 == EDGE - 1

    def one_slot(slot, carry):
        oe = jnp.where(lane == WIDTH - 1, factor(slot, 19), 1.0)
        ow = jnp.where(lane == 0, factor(slot, 18), 1.0)
        on16 = jnp.where(at_hi, factor(slot, 17), 1.0)
        os16 = jnp.where(at_lo, factor(slot, 16), 1.0)
        base = factor(slot, 26) * float(WIDTH)
        alive = item(slot, 24) == 1
        for step in range(2):
            src = xa if step == 0 else xb
            halo = hx if step == 0 else upd
            for q in range(8):
                src[q, pl.ds(7, 1), :] = halo[0, q, pl.ds(slot * 2 + 1, 1), :]
                src[q, pl.ds(136, 1), :] = halo[0, q, pl.ds(slot * 2, 1), :]
            if step == 0:
                for q in range(8):
                    ref, k = (tr, q) if q < 4 else (ve, q - 4)
                    src[q, pl.ds(8, WIDTH), :] = ref[slot, k]
            for r in range(0, 144, 16):
                p0, p1 = pressure(*[src[q, pl.ds(r, 16), :] for q in range(4)])
                src[8, pl.ds(r, 16), :] = p0
                src[9, pl.ds(r, 16), :] = p1
            for r in range(0, WIDTH, EDGE):
                f = (base + (y16 + (r + 0.5))) * (2.0 / (ROWS * WIDTH))
                for level in range(2):
                    c, e, w, n, s = [], [], [], [], []
                    for i in range(5):
                        q = 2 * i + level
                        x = src[q, pl.ds(8 + r, EDGE), :]
                        edge = pltpu.roll(cols[step, pl.ds(r, EDGE), :], WIDTH - 1 - q * 8 - 2 * slot, 1)
                        c.append(x)
                        e.append(jnp.where(lane == WIDTH - 1, edge, pltpu.roll(x, WIDTH - 1, 1)))
                        w.append(jnp.where(lane == 0, edge, pltpu.roll(x, 1, 1)))
                        n.append(src[q, pl.ds(9 + r, EDGE), :])
                        s.append(src[q, pl.ds(7 + r, EDGE), :])
                    new = stencil(
                        c, e, w, n, s, oe, ow, on16 if r == WIDTH - EDGE else None, os16 if r == 0 else None, f
                    )
                    for i in range(4):
                        if step == 0:
                            xb[2 * i + level, pl.ds(8 + r, EDGE), :] = new[i]
                        else:
                            out = tr_out if i < 2 else ve_out
                            out[slot, 2 * (i % 2) + level, pl.ds(r, EDGE), :] = jnp.where(alive, new[i], 0.0)
        return carry

    for src in (xa, xb):
        for q in range(8):
            src[q, pl.ds(0, 8), :] = jnp.zeros((8, WIDTH), F32)
            src[q, pl.ds(136, 8), :] = jnp.zeros((8, WIDTH), F32)
    lax.fori_loop(0, 4, one_slot, 0)


def shape(*dims):
    return jax.ShapeDtypeStruct(dims, F32)


def table_shape(rows):
    return jax.ShapeDtypeStruct((rows, WIDTH), I32)


def exclusive_count(mask):
    i = jnp.arange(mask.shape[-1])
    return jnp.sum(mask[..., None, :] & (i[None, :] < i[:, None]), axis=-1).astype(I32)


def permute(x, pairs):
    return lax.ppermute(x, "blk", pairs)


def column_pairs(distance):
    return [(i, (i + 16 * distance * (1 if i % 2 == 0 else -1)) % DEVICES) for i in range(DEVICES)]


def exchange_z(x):
    groups = [[16 * a + 2 * z + c for z in range(8)] for a in range(16) for c in range(2)]
    return lax.all_to_all(x, "blk", 0, 0, axis_index_groups=groups, tiled=True)


def per_device(tracers, velocity, block_counts, land):
    tr = tracers.reshape(4, 4, WIDTH, WIDTH)
    ve = velocity.reshape(4, 4, WIDTH, WIDTH)
    swap = [(i, i ^ 1) for i in range(DEVICES)]

    rims, codes, mine, load = pl.pallas_call(
        start_kernel,
        out_shape=(shape(16 * EDGE, WIDTH), table_shape(64), table_shape(8), table_shape(8)),
        in_specs=[SM, VM, HB, HB],
        out_specs=(VM, VM, VM, VM),
        scratch_shapes=[
            pltpu.VMEM((32, WIDTH), I32),
            pltpu.VMEM((4, 4, WIDTH, WIDTH), F32),
            pltpu.VMEM((4, 4, WIDTH, WIDTH), F32),
            pltpu.VMEM((WIDTH, WIDTH), F32),
            pltpu.SemaphoreType.DMA((2,)),
        ],
        compiler_params=params(32),
        name="start",
    )(block_counts, land, tr, ve)
    other = permute(rims, swap)
    chip, message = pl.pallas_call(
        message_kernel,
        out_shape=(shape(32 * EDGE, WIDTH), shape(MSG, WIDTH)),
        in_specs=[SM, VM, VM],
        out_specs=(VM, VM),
        compiler_params=params(16),
        name="message",
    )(mine, rims, other)
    near = [permute(message, column_pairs(d)) for d in (1, 2, 3)]
    corners = message[MSG_EDGES * EDGE :]
    far = [permute(corners, column_pairs(d)) for d in (4, 5)]
    chunks = pl.pallas_call(
        pack_kernel,
        out_shape=shape(8 * CHUNK, WIDTH),
        in_specs=[SM] + [HB] * 6,
        out_specs=VM,
        scratch_shapes=[
            pltpu.VMEM((4 * MSG, WIDTH), F32),
            pltpu.VMEM((16, WIDTH), F32),
            pltpu.SMEM((8 * 32,), I32),
            pltpu.SemaphoreType.DMA((6,)),
        ],
        compiler_params=params(16),
        name="pack",
    )(codes, message, *near, *far)
    got = exchange_z(chunks.reshape(8, CHUNK, WIDTH)).reshape(8 * CHUNK, WIDTH)
    own, others = pl.pallas_call(
        sort_kernel,
        out_shape=(shape(SWAP, WIDTH), shape(SWAP, WIDTH)),
        in_specs=[SM, VM],
        out_specs=(VM, VM),
        scratch_shapes=[pltpu.SMEM((8,), I32), pltpu.SMEM((32,), I32)],
        compiler_params=params(16),
        name="sort",
    )(mine, got)

    def second(args):
        own, others, codes, mine, message, near = args
        down = (lax.axis_index("blk").astype(I32) & 1) == 1
        held = jnp.concatenate([message, *near])
        send = codes[:, :4].reshape(8, 32)
        rank = exclusive_count(send > 0)
        late = jnp.arange(CAP, CAP + MORE)
        picks = jnp.sum(jnp.where((send > 0)[:, None] & (rank[:, None] == late[None, :, None]), send[:, None] - 1, 0), axis=-1)
        rows = picks[:, :, None] * 8 + jnp.arange(EDGE, dtype=I32)
        more = exchange_z(held[rows].reshape(8, MORE * EDGE, WIDTH)).reshape(8 * MORE * EDGE, WIDTH)
        zed = mine[:, 4:8].reshape(32)
        i32 = jnp.arange(32)
        rank = jnp.sum((zed[None] >= 0) & (zed[None] == zed[:, None]) & (i32[None] < i32[:, None]), axis=1).astype(I32)
        late = (zed >= 0) & (rank >= CAP)
        start = jnp.where(late, zed * (MORE * EDGE) + (rank - CAP) * EDGE, 0)
        start, late = [jnp.where(down, jnp.concatenate([x[16:], x[:16]]), x) for x in (start, late)]
        new = more[start[:, None] + jnp.arange(EDGE, dtype=I32)]
        old = jnp.stack([own[: 16 * EDGE], others[: 16 * EDGE]]).reshape(32, EDGE, WIDTH)
        new = jnp.where(late[:, None, None], new, old).reshape(2, 16 * EDGE, WIDTH)
        return jnp.concatenate([new[0], own[16 * EDGE :]]), jnp.concatenate([new[1], others[16 * EDGE :]])

    own, others = lax.cond(
        load[0, 0] > CAP, second, lambda args: (args[0], args[1]), (own, others, codes, mine, message, near)
    )
    theirs = permute(others, swap)

    tr_new, ve_new = pl.pallas_call(
        steps_kernel,
        out_shape=(shape(4, 4, WIDTH, WIDTH), shape(4, 4, WIDTH, WIDTH)),
        in_specs=[SM] + [HB] * 3 + [VM] * 2,
        out_specs=(VM, VM),
        scratch_shapes=[
            pltpu.VMEM((32 * EDGE + 2 * SWAP + EDGE, WIDTH), F32),
            pltpu.VMEM((2, EDGE, 8, WIDTH), F32),
            pltpu.VMEM((2, 8, 8, WIDTH), F32),
            pltpu.VMEM((2, 8, 8, WIDTH), F32),
            pltpu.VMEM((2, 8, 8, WIDTH), F32),
            pltpu.VMEM((2, WIDTH, WIDTH), F32),
            pltpu.VMEM((10, 144, WIDTH), F32),
            pltpu.VMEM((10, 144, WIDTH), F32),
            pltpu.SemaphoreType.DMA((3,)),
        ],
        compiler_params=params(32),
        name="steps",
    )(mine, chip, own, theirs, tr, ve)
    return tr_new.reshape(tracers.shape), ve_new.reshape(velocity.shape)


def solution(mesh):
    spec = P("blk", None, None, None, None)
    return jax.shard_map(
        per_device,
        mesh=mesh,
        in_specs=(spec, spec, P(), P()),
        out_specs=(spec, spec),
        check_vma=False,
    )
```

```python
import jax
import jax.numpy as jnp
from jax import lax
from jax.experimental import pallas as pl
from jax.experimental.pallas import tpu as pltpu
from jax.sharding import PartitionSpec as P

DEVICES = 256
ROWS, COLS = 26, 34
WIDTH = 128
CAP = 7
MORE = 11
EDGE = 16
MSG_EDGES = 18
MSG = MSG_EDGES * EDGE + 8
CHUNK = CAP * EDGE + 16
SWAP = 16 * EDGE + 8
F32 = jnp.float32
I32 = jnp.int32


def params(mib):
    return pltpu.CompilerParams(vmem_limit_bytes=mib * 1024 * 1024)


VM = pl.BlockSpec(memory_space=pltpu.VMEM)
SM = pl.BlockSpec(memory_space=pltpu.SMEM)
HB = pl.BlockSpec(memory_space=pl.ANY)


CODES = 28


def lane_iota(rows):
    return lax.broadcasted_iota(I32, (rows, WIDTH), 1)


def row_iota(rows):
    return lax.broadcasted_iota(I32, (rows, WIDTH), 0)


def exact_dot(a, b):
    return jnp.dot(a.astype(jnp.bfloat16), b.astype(jnp.bfloat16), preferred_element_type=F32)


def build_tables(me, counts, land, board, codes, mine, picks, load):
    column, zed, core = me >> 4, (me >> 1) & 7, me & 1
    board[...] = jnp.ones((32, WIDTH), I32)
    board[pl.ds(0, ROWS), pl.ds(0, COLS)] = land[...]
    sea = board[...] == 0
    lane, row = lane_iota(32), row_iota(32)
    ones = sea.astype(F32)
    i, j = row_iota(WIDTH), lane_iota(WIDTH)
    along = exact_dot(ones, i <= j)
    totals = exact_dot(ones, i >= 0)
    li, lj = lax.broadcasted_iota(I32, (32, 32), 0), lax.broadcasted_iota(I32, (32, 32), 1)
    pos = (exact_dot(lj < li, totals) + along - ones).astype(I32)

    def device(n, carry):
        end, owner, start = carry
        for k in range(8):
            d = n * 8 + k
            end = end + counts[d]
            past = pos >= end
            owner = jnp.where(past, d + 1, owner)
            start = jnp.where(past, end, start)
        return end, owner, start

    zero = jnp.zeros((32, WIDTH), I32)
    _, owner, start = lax.fori_loop(0, DEVICES // 8, device, (jnp.int32(0), zero, zero))
    ids = jnp.where(sea, owner * 4 + pos - start, -1).astype(F32)

    def west(x):
        return jnp.where(lane == 0, pltpu.roll(x, WIDTH - COLS + 1, 1), pltpu.roll(x, 1, 1))

    def east(x):
        return jnp.where(lane == COLS - 1, pltpu.roll(x, COLS - 1, 1), pltpu.roll(x, WIDTH - 1, 1))

    mirror = (i + j == COLS - 1).astype(F32)
    folded = jnp.dot(ids, mirror, preferred_element_type=F32, precision=lax.Precision.HIGHEST)
    south = jnp.where(row == 0, -1.0, pltpu.roll(ids, 1, 0))
    north = jnp.where(row == ROWS - 1, folded, pltpu.roll(ids, 31, 0))
    near = [south, north, west(ids), east(ids), west(south), east(south), west(north), east(north)]
    pairs = [(near[2 * k] + 1.0) * 2048.0 + (near[2 * k + 1] + 1.0) for k in range(4)]
    place = (row * WIDTH + lane).astype(F32)

    chip = jnp.right_shift(ids.astype(I32), 3)
    kinds = []
    for k in range(4):
        source = jnp.right_shift(near[k].astype(I32), 3)
        away = sea & (source >= 0) & (source != chip)
        kinds.append(jnp.where(away, (source & 7) + jnp.where(source > chip, 8, 0), -1))
    kind_row = row_iota(16)
    counted = jnp.zeros((WIDTH, 16), F32)
    for r in range(ROWS):
        is_chip = (chip[r : r + 1, :] == i).astype(jnp.bfloat16)
        of_kind = sum((kinds[k][r : r + 1, :] == kind_row).astype(F32) for k in range(4)).astype(jnp.bfloat16)
        counted += lax.dot_general(is_chip, of_kind, (((1,), (1,)), ((), ())), preferred_element_type=F32)
    load[...] = jnp.broadcast_to(jnp.max(counted), (8, WIDTH)).astype(I32)

    slot = row_iota(64)
    want = (column * 64 + slot).astype(F32)
    found = [jnp.zeros((64, WIDTH), F32) for _ in range(4)] + [jnp.full((64, WIDTH), -1.0, F32)]
    for r in range(ROWS):
        hit = ids[r : r + 1, :] == want
        for k, x in enumerate(pairs + [place]):
            found[k] = jnp.where(hit, x[r : r + 1, :], found[k])
    found = [jnp.max(x, axis=1, keepdims=True).astype(I32) for x in found]
    place = found[4]
    live = place >= 0
    block_row, block_col = jnp.right_shift(place, 7), place & 127
    top = live & (block_row == ROWS - 1)
    ids8 = []
    for k in range(4):
        ids8 += [jnp.right_shift(found[k], 11) - 1, (found[k] & 2047) - 1]
    slot1 = lax.broadcasted_iota(I32, (64, 1), 0)
    here = column * 8 + jnp.right_shift(slot1, 3)
    down = core == 1
    items = {}
    for k in range(8):
        valid = ids8[k] >= 0
        source, t = jnp.right_shift(ids8[k], 3), ids8[k] & 7
        z, delta = source & 7, jnp.abs(jnp.right_shift(source, 3) - column)
        lower, same = source < here, source == here
        items[16 + k] = valid.astype(I32)
        if k < 4:
            flow = valid & ~same & (lower != down)
            if k < 2:
                edge = t if k == 0 else t + jnp.where(top & down, 10, 0)
            else:
                edge = jnp.where(down, 11 - k, 6 + k)
            at = delta * (MSG // 8) + edge * (EDGE // 8) + 1
            items[k] = jnp.where(flow & (z == zed), at, 0)
            items[4 + k] = jnp.where(flow, z, -1)
            of = (1, 0, 3, 2)[k]
            if k == 1:
                of = jnp.where(top, 1, 0)
            close = (t * 4 + of) * (EDGE // 8)
            base = jnp.where(lower != down, 4 * EDGE, 4 * EDGE + SWAP // 8)
            far = ((slot1 & 3) * 4 + k) * (EDGE // 8) + base
            items[8 + k] = jnp.where(valid, jnp.where(same, close, far), 4 * EDGE + 2 * SWAP // 8)
        else:
            flow = valid & ((lower | same) != down)
            hi = (0, 1, 0, 1)[k - 4]
            lane_at = 2 * t + hi
            if k >= 6:
                lane_at = jnp.where(top, 2 * t + 1 - hi, 16 + 2 * t + hi)
            at = z * (CHUNK // 8) + CAP * EDGE // 8 + jnp.right_shift(delta, 2)
            items[8 + k] = jnp.where(flow, at * WIDTH + 32 * (delta & 3) + lane_at, -1)
    items[24], items[25], items[26], items[27] = live.astype(I32), top.astype(I32), block_row, block_col
    sends = [items[k] > 0 for k in range(4)]
    lane64, slot64 = lane_iota(64), row_iota(64)
    masks = jnp.zeros((64, WIDTH), F32)
    for k in range(4):
        masks = jnp.where((lane64 == k) & sends[k], 1.0, masks)
    si, sj = lax.broadcasted_iota(I32, (64, 64), 0), lax.broadcasted_iota(I32, (64, 64), 1)
    before = exact_dot((sj < si) & (jnp.right_shift(si, 3) == jnp.right_shift(sj, 3)), masks)
    rank = jnp.sum(before, axis=1, keepdims=True).astype(I32)
    placed = jnp.zeros((64, WIDTH), F32)
    for k in range(4):
        placed = jnp.where(sends[k] & (lane64 == rank), items[k].astype(F32), placed)
        rank = rank + sends[k].astype(I32)
    zi, zj = lax.broadcasted_iota(I32, (8, 64), 0), lax.broadcasted_iota(I32, (8, 64), 1)
    picks[...] = exact_dot(jnp.right_shift(zj, 3) == zi, placed).astype(I32)
    table = jnp.zeros((64, WIDTH), I32)
    for k in range(CODES):
        table = jnp.where(lane64 == k, items[k], table)
    codes[...] = table
    mine[...] = codes[pl.ds(pl.multiple_of(zed * 8, 8), 8), :]


def start_kernel(counts, land, tr_hbm, ve_hbm, out, codes, mine, picks, load, board, tr, ve, turned, sem):
    copies = [pltpu.make_async_copy(tr_hbm, tr, sem.at[0]), pltpu.make_async_copy(ve_hbm, ve, sem.at[1])]
    for copy in copies:
        copy.start()
    build_tables(lax.axis_index("blk").astype(I32), counts, land, board, codes, mine, picks, load)
    for copy in copies:
        copy.wait()
    lane = lane_iota(WIDTH) // 4
    gathered = jnp.zeros((WIDTH, WIDTH), F32)
    for slot in range(4):
        for fl in range(8):
            ref, k = (tr, fl) if fl < 4 else (ve, fl - 4)
            for depth in range(2):
                out[pl.ds((slot * 4 + 0) * EDGE + depth * 8 + fl, 1), :] = ref[slot, k, pl.ds(depth, 1), :]
                out[pl.ds((slot * 4 + 1) * EDGE + depth * 8 + fl, 1), :] = ref[slot, k, pl.ds(127 - depth, 1), :]
            tile = slot * 8 + fl
            rolled = pltpu.roll(ref[slot, k], (4 * tile + 2) % WIDTH, 1)
            gathered = jnp.where(lane == tile, rolled, gathered)
    turned[...] = gathered.T
    for slot in range(4):
        for j, (side, depth) in enumerate([(3, 1), (3, 0), (2, 0), (2, 1)]):
            out[pl.ds((slot * 4 + side) * EDGE + depth * 8, 8), :] = turned[pl.ds(slot * 32 + j, 8, stride=4), :]


def message_kernel(table_hbm, mine, other, chip, out, table, sem):
    fetch = pltpu.make_async_copy(table_hbm, table, sem.at[0])
    fetch.start()
    core = lax.axis_index("blk").astype(I32) & 1
    flag = core == 0
    for t in range(4):
        for side in range(4):
            at = (t * 4 + side) * EDGE
            a, b = mine[pl.ds(at, EDGE), :], other[pl.ds(at, EDGE), :]
            chip[pl.ds(at, EDGE), :] = jnp.where(flag, a, b)
            chip[pl.ds(16 * EDGE + at, EDGE), :] = jnp.where(flag, b, a)
    for t in range(8):
        at = pl.multiple_of(jnp.where(flag, t * 4 + 1, t * 4) * EDGE, EDGE)
        out[pl.ds(t * EDGE, EDGE), :] = chip[pl.ds(at, EDGE), :]
        out[pl.ds((10 + t) * EDGE, EDGE), :] = chip[pl.ds((t * 4 + 1) * EDGE, EDGE), :]
    lane = lax.broadcasted_iota(I32, (8, WIDTH), 1) // 2
    corners = jnp.zeros((8, WIDTH), F32)
    for t in range(8):
        for side, base in ((1, 0), (0, 8)):
            x = chip[pl.ds((t * 4 + side) * EDGE, 8), :]
            corners = jnp.where(lane == base + t, pltpu.roll(x, 2 * (base + t) + 1, 1), corners)
    out[pl.ds(MSG_EDGES * EDGE, 8), :] = corners
    fetch.wait()
    last, first_col, last_col = jnp.int32(0), jnp.int32(0), jnp.int32(0)
    for t in range(8):
        live, col = table[t, 24] == 1, table[t, 27]
        last = jnp.where(live, t, last)
        first_col = jnp.where(live & (col == 0), t, first_col)
        live, col = table[7 - t, 24] == 1, table[7 - t, 27]
        last_col = jnp.where(live & (col == COLS - 1), 7 - t, last_col)
    for e, edge in ((8, jnp.where(flag, last * 4 + 3, 2)), (9, jnp.where(flag, first_col * 4 + 2, last_col * 4 + 3))):
        at = pl.multiple_of(edge * EDGE, EDGE)
        out[pl.ds(e * EDGE, EDGE), :] = chip[pl.ds(at, EDGE), :]


def pack_kernel(picks_hbm, m0, m1, m2, m3, c4, c5, out, picks, held, packed, sem, sent):
    messages = (m0, m1, m2, m3)
    fetch = pltpu.make_async_copy(picks_hbm, picks, sem.at[14])
    fetch.start()
    copies = [
        pltpu.make_async_copy(m.at[pl.ds(MSG_EDGES * EDGE, 8)] if i < 4 else m, held.at[pl.ds(i * 8, 8)], sem.at[i])
        for i, m in enumerate((*messages, c4, c5))
    ]
    for copy in copies:
        copy.start()

    def edges(wait):
        for z in range(8):
            for r in range(CAP):
                code = picks[z, r]
                for k, m in enumerate(messages):

                    @pl.when((code > k * (MSG // 8)) & (code <= (k + 1) * (MSG // 8)))
                    def _():
                        row = pl.multiple_of((code - 1 - k * (MSG // 8)) * 8, EDGE)
                        to = out.at[pl.ds(z * CHUNK + r * EDGE, EDGE)]
                        copy = pltpu.make_async_copy(m.at[pl.ds(row, EDGE)], to, sent.at[0])
                        copy.wait() if wait else copy.start()

    fetch.wait()
    edges(False)
    for copy in copies:
        copy.wait()
    lane = lane_iota(8) // 32
    near_c = held[pl.ds(0, 8), :]
    for i in range(1, 4):
        near_c = jnp.where(lane == i, pltpu.roll(held[pl.ds(i * 8, 8), :], 32 * i, 1), near_c)
    packed[pl.ds(0, 8), :] = near_c
    packed[pl.ds(8, 8), :] = jnp.where(lane == 0, held[pl.ds(32, 8), :], pltpu.roll(held[pl.ds(40, 8), :], 32, 1))
    copies = [
        pltpu.make_async_copy(packed, out.at[pl.ds(z * CHUNK + CAP * EDGE, 16)], sem.at[6 + z]) for z in range(8)
    ]
    for copy in copies:
        copy.start()
    edges(True)
    for copy in copies:
        copy.wait()


def sort_kernel(table_hbm, got, own, other, table, taken, rows, sem):
    fetch = pltpu.make_async_copy(table_hbm, table, sem.at[0])
    fetch.start()
    core = lax.axis_index("blk").astype(I32) & 1
    for z in range(8):
        taken[z] = 0
    fetch.wait()
    for t in range(8):
        for side in range(4):
            code = table[t, 4 + side]
            z = jnp.maximum(code, 0)
            rank = taken[z]
            taken[z] = rank + (code >= 0).astype(I32)
            rows[t * 4 + side] = z * CHUNK + jnp.minimum(rank, CAP - 1) * EDGE
    lane = lane_iota(8)
    for half, out in enumerate((own, other)):
        first = (core ^ half) * 4
        corners = jnp.zeros((8, WIDTH), F32)
        for e in range(16):
            at = pl.multiple_of(rows[first * 4 + e], EDGE)
            out[pl.ds(e * EDGE, EDGE), :] = got[pl.ds(at, EDGE), :]
            code = table[first + e // 4, 12 + e % 4]
            turn = (e - code) & (WIDTH - 1)
            at = pl.multiple_of(jnp.right_shift(jnp.maximum(code, 0), 7) * 8, 8)
            corners = jnp.where(lane == jnp.where(code >= 0, e, -1), pltpu.roll(got[pl.ds(at, 8), :], turn, 1), corners)
        out[pl.ds(16 * EDGE, 8), :] = corners


def pressure(t0, t1, s0, s1):
    r0 = t0 * (-0.3 - 0.08 * t0 + 0.05 * s0) + 0.6 * s0
    r1 = t1 * (-0.3 - 0.08 * t1 + 0.05 * s1) + 0.6 * s1
    return 0.25 * r0, 0.5 * r0 + 0.25 * r1


def stencil(c, e, w, n, s, oe, ow, on, os, f):
    def times(o, x):
        return x if o is None else o * x

    ue, uw = 0.025 * (c[2] + e[2]), 0.025 * (w[2] + c[2])
    vn, vs = 0.025 * (c[3] + n[3]), 0.025 * (s[3] + c[3])
    ae, be = times(oe, 0.05 - ue), times(oe, 0.05 + ue)
    aw, bw = times(ow, 0.05 + uw), times(ow, 0.05 - uw)
    an, bn = times(on, 0.05 - vn), times(on, 0.05 + vn)
    as_, bs = times(os, 0.05 + vs), times(os, 0.05 - vs)
    mid = 1.0 - ((be + bw) + (bn + bs))
    out = []
    for i in range(2):
        out.append(mid * c[i] + ((ae * e[i] + aw * w[i]) + (an * n[i] + as_ * s[i])))
    for i, (lo, hi, olo, ohi) in ((2, (w, e, ow, oe)), (3, (s, n, os, on))):
        lap = (times(oe, e[i] - c[i]) + times(ow, w[i] - c[i])) + (times(on, n[i] - c[i]) + times(os, s[i] - c[i]))
        grad = times(ohi, hi[4] - c[4]) + times(olo, c[4] - lo[4])
        turn = f * c[3] if i == 2 else -(f * c[2])
        out.append(c[i] + (0.1 * turn + 0.05 * (lap - grad)))
    return out


def inner_kernel(table, tr, ve, tr_out, ve_out, rims, xa, xb, gathered):
    core = lax.axis_index("blk").astype(I32) & 1
    y16 = lax.broadcasted_iota(I32, (EDGE, WIDTH), 0).astype(F32)
    lane = lane_iota(WIDTH)
    for src in (xa, xb):
        for q in range(10):
            src[q, pl.ds(0, 8), :] = jnp.zeros((8, WIDTH), F32)
            src[q, pl.ds(136, 8), :] = jnp.zeros((8, WIDTH), F32)

    def one_slot(slot, carry):
        base = table[core * 4 + slot, 26].astype(F32) * float(WIDTH)
        alive = table[core * 4 + slot, 24] == 1
        for q in range(8):
            ref, k = (tr, q) if q < 4 else (ve, q - 4)
            xa[q, pl.ds(8, WIDTH), :] = ref[slot, k]
        for step, src in enumerate((xa, xb)):
            for r in range(8, 8 + WIDTH, EDGE):
                p0, p1 = pressure(*[src[q, pl.ds(r, EDGE), :] for q in range(4)])
                src[8, pl.ds(r, EDGE), :] = p0
                src[9, pl.ds(r, EDGE), :] = p1
            for r in range(0, WIDTH, EDGE):
                f = (base + (y16 + (r + 0.5))) * (2.0 / (ROWS * WIDTH))
                for level in range(2):
                    c, e, w, n, s = [], [], [], [], []
                    for i in range(5):
                        q = 2 * i + level
                        x = src[q, pl.ds(8 + r, EDGE), :]
                        c.append(x)
                        e.append(pltpu.roll(x, WIDTH - 1, 1))
                        w.append(pltpu.roll(x, 1, 1))
                        n.append(src[q, pl.ds(9 + r, EDGE), :])
                        s.append(src[q, pl.ds(7 + r, EDGE), :])
                    new = stencil(c, e, w, n, s, None, None, None, None, f)
                    for i in range(4):
                        if step == 0:
                            xb[2 * i + level, pl.ds(8 + r, EDGE), :] = new[i]
                        else:
                            out = tr_out if i < 2 else ve_out
                            out[slot, 2 * (i % 2) + level, pl.ds(r, EDGE), :] = jnp.where(alive, new[i], 0.0)
        for q in range(8):
            at = pl.multiple_of(slot * 4 * EDGE, EDGE)
            for ring in range(2):
                rims[pl.ds(at + ring * 8 + q, 1), :] = xb[q, pl.ds(8 + 1 + ring, 1), :]
                rims[pl.ds(at + EDGE + ring * 8 + q, 1), :] = xb[q, pl.ds(8 + 126 - ring, 1), :]
            tile = slot * 8 + q
            x = xb[q, pl.ds(8, WIDTH), :]
            a, b = pltpu.roll(x, (tile * 4 + 3) & (WIDTH - 1), 1), pltpu.roll(x, (tile * 4 + 1) & (WIDTH - 1), 1)
            mine = jnp.right_shift(lane, 2) == tile
            gathered[...] = jnp.where(mine, jnp.where((lane & 3) < 2, a, b), gathered[...])
        return carry

    gathered[...] = jnp.zeros((WIDTH, WIDTH), F32)
    lax.fori_loop(0, 4, one_slot, 0)
    gathered[...] = gathered[...].T
    for slot in range(4):
        for j, (side, ring) in enumerate([(3, 1), (3, 0), (2, 0), (2, 1)]):
            rims[pl.ds((slot * 4 + side) * EDGE + ring * 8, 8), :] = gathered[pl.ds(slot * 32 + j, 8, stride=4), :]


def lateral(x, ring):
    even = (row_iota(8) & 1) == 0
    up, down = pltpu.roll(x, 7, 0), pltpu.roll(x, 1, 0)
    back = pltpu.roll(x, WIDTH - ring, 1) if ring else x
    ahead = pltpu.roll(x, ring, 1) if ring else x
    low = jnp.where(even, pltpu.roll(up, ring + 1, 1), back)
    high = jnp.where(even, ahead, pltpu.roll(down, WIDTH - 1 - ring, 1))
    return low, high


def final_kernel(
    table, chip, own, other, edges, rims, tr, ve, tr_out, ve_out, held, hx, inn, mid, crv, upd, first, r0, r1, turned, res_t, res_v, sem, sent
):
    sizes = (8 * 4 * EDGE, SWAP, SWAP)
    starts = (0, sizes[0], sizes[0] + SWAP)
    copies = [
        pltpu.make_async_copy(x, held.at[pl.ds(at, n)], sem.at[i]) for i, (x, at, n) in enumerate(zip((chip, own, other), starts, sizes))
    ]
    for copy in copies:
        copy.start()
    held[pl.ds(starts[2] + SWAP, EDGE), :] = jnp.zeros((EDGE, WIDTH), F32)
    core = lax.axis_index("blk").astype(I32) & 1

    def item(slot, k):
        return table[core * 4 + slot, k]

    def factor(slot, k):
        return item(slot, k).astype(F32)

    i0, i1 = row_iota(WIDTH), lane_iota(WIDTH)
    mirror = (i0 + i1 == WIDTH - 1).astype(F32)
    sign = jnp.where((row_iota(EDGE) & 7) >= 4, -1.0, 1.0)
    lane8, sub8 = lane_iota(8), row_iota(8)
    even = (sub8 & 1) == 0
    sign8 = jnp.where(sub8 >= 4, -1.0, 1.0)
    where_to = ((0, 1), (0, 0), (1, 1), (1, 0))

    for slot in range(4):
        for side in range(4):
            group, odd = where_to[side]
            at = (slot * 4 + side) * EDGE
            inn[group, :, slot * 2 + odd, :] = edges[pl.ds(at, EDGE), :]
            mid[group, :, slot * 2 + odd, :] = rims[pl.ds(at, EDGE), :]
    for copy in copies:
        copy.wait()
    corners = held[pl.ds(starts[1] + 16 * EDGE, 8), :] + held[pl.ds(starts[2] + 16 * EDGE, 8), :]
    for slot in range(4):
        top = item(slot, 25) == 1
        for side in range(4):
            group, odd = where_to[side]
            x = held[pl.ds(pl.multiple_of(item(slot, 8 + side) * 8, 8), EDGE), :]
            if side == 1:
                flipped = jnp.dot(x, mirror, preferred_element_type=F32, precision=lax.Precision.HIGHEST) * sign
                x = jnp.where(top, flipped, x)
            hx[group, :, slot * 2 + odd, :] = x
        for group, odd, lo, hi in ((0, 0, 2, 3), (0, 1, 0, 1), (1, 0, 1, 3), (1, 1, 0, 2)):
            vals = []
            for which, lane in ((lo, 0), (hi, WIDTH - 1)):
                v = pltpu.roll(corners, (lane - (slot * 4 + which)) % WIDTH, 1)
                if which >= 2:
                    v = jnp.where(top, v * sign8, v)
                vals.append(v)
            crv[group, :, slot * 2 + odd, :] = jnp.where(lane8 == 0, vals[0], vals[1])

    def strip(group, c, outer, inner, low, high, o_out, o_low, o_high, cor, out):
        at_c, at_p, at_m, at_h, at_l = [], [], [], [], []
        for q in range(8):
            x = c(q)
            at_c.append(x)
            at_p.append(jnp.where(even, outer(q), inner(q)))
            at_m.append(jnp.where(even, inner(q), outer(q)))
            lo, hi = low(q), high(q)
            at_h.append(jnp.where(lane8 == WIDTH - 1, hi, pltpu.roll(x, WIDTH - 1, 1)))
            at_l.append(jnp.where(lane8 == 0, lo, pltpu.roll(x, 1, 1)))
        five = [x + list(pressure(x[0], x[1], x[2], x[3])) for x in (at_c, at_p, at_m, at_h, at_l)]
        o_pos = None if o_out is None else jnp.where(even, o_out, 1.0)
        o_neg = None if o_out is None else jnp.where(even, 1.0, o_out)
        for level in range(2):
            c, p, m, h, l = [[x[2 * i + level] for i in range(5)] for x in five]
            if group == 0:
                new = stencil(c, h, l, p, m, o_high, o_low, o_pos, o_neg, cor)
            else:
                new = stencil(c, p, m, h, l, o_pos, o_neg, o_high, o_low, cor)
            for i in range(4):
                out[group, 2 * i + level] = new[i]

    def by_row(values):
        x = jnp.zeros((8, WIDTH), F32)
        for slot in range(4):
            for odd in range(2):
                x = jnp.where(sub8 == slot * 2 + odd, values(slot, odd), x)
        return x

    def ends(x, where):
        return jnp.where(lane8 == where, x, 1.0)

    scale = 2.0 / (ROWS * WIDTH)
    base = by_row(lambda slot, odd: factor(slot, 26) * float(WIDTH))
    halo_row = by_row(
        lambda slot, odd: -1.0 if odd else jnp.where(item(slot, 25) == 1, WIDTH - 1.0, float(WIDTH)),
    )
    across = (base + lane8.astype(F32) + 0.5) * scale
    o_out, o_low, o_high, cor0, cor1 = [], [], [], [], []
    for group in range(2):
        o_out.append(by_row(lambda slot, odd: factor(slot, ((17, 16), (19, 18))[group][odd])))
        lo, hi = ((18, 19), (16, 17))[group]
        o_low.append(ends(by_row(lambda slot, odd: factor(slot, lo)), 0))
        o_high.append(ends(by_row(lambda slot, odd: factor(slot, hi)), WIDTH - 1))
        if group == 0:
            cor0.append((base + jnp.where(even, WIDTH - 1.0, 0.0) + 0.5) * scale)
            cor1.append((base + jnp.where(even, WIDTH - 2.0, 1.0) + 0.5) * scale)
        else:
            cor0.append(across)
            cor1.append(across)

    for group in range(2):
        lo, hi = ((22, 23), (20, 21)) if group == 0 else ((21, 23), (20, 22))
        corner_low = ends(by_row(lambda slot, odd: factor(slot, (lo, hi)[odd][0])), 0)
        corner_high = ends(by_row(lambda slot, odd: factor(slot, (lo, hi)[odd][1])), WIDTH - 1)
        cor = (base + halo_row + 0.5) * scale if group == 0 else across
        strip(
            group,
            lambda q: hx[group, q],
            lambda q: hx[group, 8 + q],
            lambda q: inn[group, q],
            lambda q: crv[group, q],
            lambda q: crv[group, q],
            None,
            corner_low,
            corner_high,
            cor,
            upd,
        )
    for group in range(2):
        beyond = [lateral(hx[1 - group, q], 0) for q in range(8)]
        strip(
            group,
            lambda q: inn[group, q],
            lambda q: hx[group, q],
            lambda q: inn[group, 8 + q],
            lambda q: beyond[q][0],
            lambda q: beyond[q][1],
            o_out[group],
            o_low[group],
            o_high[group],
            cor0[group],
            first,
        )
    for group in range(2):
        for q in range(8):
            for ring in (1, 2):
                low, high = lateral(first[1 - group, q], ring)
                x = mid[group, (ring - 1) * 8 + q]
                mid[group, (ring - 1) * 8 + q] = jnp.where(lane8 == 0, low, jnp.where(lane8 == WIDTH - 1, high, x))
    for group in range(2):
        beyond0 = [lateral(upd[1 - group, q], 0) for q in range(8)]
        strip(
            group,
            lambda q: first[group, q],
            lambda q: upd[group, q],
            lambda q: mid[group, q],
            lambda q: beyond0[q][0],
            lambda q: beyond0[q][1],
            o_out[group],
            o_low[group],
            o_high[group],
            cor0[group],
            r0,
        )
        beyond1 = [lateral(upd[1 - group, q], 1) for q in range(8)]
        strip(
            group,
            lambda q: mid[group, q],
            lambda q: first[group, q],
            lambda q: mid[group, 8 + q],
            lambda q: beyond1[q][0],
            lambda q: beyond1[q][1],
            None,
            o_low[group],
            o_high[group],
            cor1[group],
            r1,
        )

    live8 = by_row(lambda slot, odd: factor(slot, 24)) > 0.5
    for group in range(2):
        for q in range(8):
            r0[group, q] = jnp.where(live8, r0[group, q], 0.0)
            r1[group, q] = jnp.where(live8, r1[group, q], 0.0)
    for q in range(8):
        for slot in range(4):
            for j, (ring, odd) in enumerate(((r1, 0), (r0, 0), (r0, 1), (r1, 1))):
                turned[pl.ds((slot * 8 + q) * 4 + j, 1), :] = ring[1, q, pl.ds(slot * 2 + odd, 1), :]
    turned[...] = turned[...].T
    lane16 = lane_iota(EDGE)
    rim = (lane16 < 2) | (lane16 >= WIDTH - 2)
    out_copies = []
    for slot in range(4):
        for q in range(8):
            src, res, k = (tr, res_t, q) if q < 4 else (ve, res_v, q - 4)
            tile = slot * 8 + q
            for r in range(0, WIDTH, EDGE):
                x = pltpu.roll(turned[pl.ds(r, EDGE), :], (-(tile * 4 + 2)) % WIDTH, 1)
                res[slot, k, pl.ds(r, EDGE), :] = jnp.where(rim, x, src[slot, k, pl.ds(r, EDGE), :])
            for ring, rr in ((0, r0), (1, r1)):
                res[slot, k, pl.ds(ring, 1), :] = rr[0, q, pl.ds(slot * 2 + 1, 1), :]
                res[slot, k, pl.ds(WIDTH - 1 - ring, 1), :] = rr[0, q, pl.ds(slot * 2, 1), :]
        for i, (res, out) in enumerate(((res_t, tr_out), (res_v, ve_out))):
            copy = pltpu.make_async_copy(res.at[slot], out.at[slot], sent.at[slot * 2 + i])
            copy.start()
            out_copies.append(copy)
    for copy in out_copies:
        copy.wait()


def shape(*dims):
    return jax.ShapeDtypeStruct(dims, F32)


def table_shape(rows):
    return jax.ShapeDtypeStruct((rows, WIDTH), I32)


def exclusive_count(mask):
    i = jnp.arange(mask.shape[-1])
    return jnp.sum(mask[..., None, :] & (i[None, :] < i[:, None]), axis=-1).astype(I32)


def permute(x, pairs):
    return lax.ppermute(x, "blk", pairs)


def column_pairs(distance):
    return [(i, (i + 16 * distance * (1 if i % 2 == 0 else -1)) % DEVICES) for i in range(DEVICES)]


def exchange_z(x):
    groups = [[16 * a + 2 * z + c for z in range(8)] for a in range(16) for c in range(2)]
    return lax.all_to_all(x, "blk", 0, 0, axis_index_groups=groups, tiled=True)


def per_device(tracers, velocity, block_counts, land):
    tr = tracers.reshape(4, 4, WIDTH, WIDTH)
    ve = velocity.reshape(4, 4, WIDTH, WIDTH)
    swap = [(i, i ^ 1) for i in range(DEVICES)]

    rims, codes, mine, picks, load = pl.pallas_call(
        start_kernel,
        out_shape=(shape(16 * EDGE, WIDTH), table_shape(64), table_shape(8), table_shape(8), table_shape(8)),
        in_specs=[SM, VM, HB, HB],
        out_specs=(VM, VM, VM, VM, VM),
        scratch_shapes=[
            pltpu.VMEM((32, WIDTH), I32),
            pltpu.VMEM((4, 4, WIDTH, WIDTH), F32),
            pltpu.VMEM((4, 4, WIDTH, WIDTH), F32),
            pltpu.VMEM((WIDTH, WIDTH), F32),
            pltpu.SemaphoreType.DMA((2,)),
        ],
        compiler_params=params(60),
        name="start",
    )(block_counts, land, tr, ve)
    other = permute(rims, swap)
    chip, message = pl.pallas_call(
        message_kernel,
        out_shape=(shape(32 * EDGE, WIDTH), shape(MSG, WIDTH)),
        in_specs=[HB, VM, VM],
        out_specs=(VM, VM),
        scratch_shapes=[pltpu.SMEM((8, WIDTH), I32), pltpu.SemaphoreType.DMA((1,))],
        compiler_params=params(16),
        name="message",
    )(mine, rims, other)
    near = [permute(message, column_pairs(d)) for d in (1, 2, 3)]
    corners = message[MSG_EDGES * EDGE :]
    far = [permute(corners, column_pairs(d)) for d in (4, 5)]
    chunks = pl.pallas_call(
        pack_kernel,
        out_shape=shape(8 * CHUNK, WIDTH),
        in_specs=[HB] * 7,
        out_specs=HB,
        scratch_shapes=[
            pltpu.SMEM((8, WIDTH), I32),
            pltpu.VMEM((48, WIDTH), F32),
            pltpu.VMEM((16, WIDTH), F32),
            pltpu.SemaphoreType.DMA((15,)),
            pltpu.SemaphoreType.DMA((1,)),
        ],
        compiler_params=params(16),
        name="pack",
    )(picks, message, *near, *far)
    tr, ve, chunks = lax.optimization_barrier((tr, ve, chunks))
    tr_inner, ve_inner, inner_rims = pl.pallas_call(
        inner_kernel,
        out_shape=(shape(4, 4, WIDTH, WIDTH), shape(4, 4, WIDTH, WIDTH), shape(16 * EDGE, WIDTH)),
        in_specs=[SM, VM, VM],
        out_specs=(VM, VM, VM),
        scratch_shapes=[
            pltpu.VMEM((10, 144, WIDTH), F32),
            pltpu.VMEM((10, 144, WIDTH), F32),
            pltpu.VMEM((WIDTH, WIDTH), F32),
        ],
        compiler_params=params(32),
        cost_estimate=pl.CostEstimate(flops=60_000_000, bytes_accessed=8_000_000, transcendentals=0),
        name="inner",
    )(mine, tr, ve)
    got = exchange_z(chunks.reshape(8, CHUNK, WIDTH)).reshape(8 * CHUNK, WIDTH)
    got, tr_inner, ve_inner, inner_rims = lax.optimization_barrier((got, tr_inner, ve_inner, inner_rims))
    own, others = pl.pallas_call(
        sort_kernel,
        out_shape=(shape(SWAP, WIDTH), shape(SWAP, WIDTH)),
        in_specs=[HB, VM],
        out_specs=(VM, VM),
        scratch_shapes=[
            pltpu.SMEM((8, WIDTH), I32),
            pltpu.SMEM((8,), I32),
            pltpu.SMEM((32,), I32),
            pltpu.SemaphoreType.DMA((1,)),
        ],
        compiler_params=params(16),
        name="sort",
    )(mine, got)

    def second(args):
        own, others, codes, mine, message, near = args
        down = (lax.axis_index("blk").astype(I32) & 1) == 1
        held = jnp.concatenate([message, *near])
        send = codes[:, :4].reshape(8, 32)
        rank = exclusive_count(send > 0)
        late = jnp.arange(CAP, CAP + MORE)
        picks = jnp.sum(jnp.where((send > 0)[:, None] & (rank[:, None] == late[None, :, None]), send[:, None] - 1, 0), axis=-1)
        rows = picks[:, :, None] * 8 + jnp.arange(EDGE, dtype=I32)
        more = exchange_z(held[rows].reshape(8, MORE * EDGE, WIDTH)).reshape(8 * MORE * EDGE, WIDTH)
        zed = mine[:, 4:8].reshape(32)
        i32 = jnp.arange(32)
        rank = jnp.sum((zed[None] >= 0) & (zed[None] == zed[:, None]) & (i32[None] < i32[:, None]), axis=1).astype(I32)
        late = (zed >= 0) & (rank >= CAP)
        start = jnp.where(late, zed * (MORE * EDGE) + (rank - CAP) * EDGE, 0)
        start, late = [jnp.where(down, jnp.concatenate([x[16:], x[:16]]), x) for x in (start, late)]
        new = more[start[:, None] + jnp.arange(EDGE, dtype=I32)]
        old = jnp.stack([own[: 16 * EDGE], others[: 16 * EDGE]]).reshape(32, EDGE, WIDTH)
        new = jnp.where(late[:, None, None], new, old).reshape(2, 16 * EDGE, WIDTH)
        return jnp.concatenate([new[0], own[16 * EDGE :]]), jnp.concatenate([new[1], others[16 * EDGE :]])

    own, others = lax.cond(
        load[0, 0] > CAP, second, lambda args: (args[0], args[1]), (own, others, codes, mine, message, near)
    )
    theirs = permute(others, swap)

    tr_new, ve_new = pl.pallas_call(
        final_kernel,
        out_shape=(shape(4, 4, WIDTH, WIDTH), shape(4, 4, WIDTH, WIDTH)),
        in_specs=[SM] + [HB] * 3 + [VM] * 4,
        out_specs=(HB, HB),
        scratch_shapes=[
            pltpu.VMEM((32 * EDGE + 2 * SWAP + EDGE, WIDTH), F32),
            pltpu.VMEM((2, EDGE, 8, WIDTH), F32),
            pltpu.VMEM((2, EDGE, 8, WIDTH), F32),
            pltpu.VMEM((2, EDGE, 8, WIDTH), F32),
            pltpu.VMEM((2, 8, 8, WIDTH), F32),
            pltpu.VMEM((2, 8, 8, WIDTH), F32),
            pltpu.VMEM((2, 8, 8, WIDTH), F32),
            pltpu.VMEM((2, 8, 8, WIDTH), F32),
            pltpu.VMEM((2, 8, 8, WIDTH), F32),
            pltpu.VMEM((WIDTH, WIDTH), F32),
            pltpu.VMEM((4, 4, WIDTH, WIDTH), F32),
            pltpu.VMEM((4, 4, WIDTH, WIDTH), F32),
            pltpu.SemaphoreType.DMA((3,)),
            pltpu.SemaphoreType.DMA((8,)),
        ],
        compiler_params=params(32),
        name="final",
    )(mine, chip, own, theirs, rims, inner_rims, tr_inner, ve_inner)
    return tr_new.reshape(tracers.shape), ve_new.reshape(velocity.shape)


def solution(mesh):
    spec = P("blk", None, None, None, None)
    return jax.shard_map(
        per_device,
        mesh=mesh,
        in_specs=(spec, spec, P(), P()),
        out_specs=(spec, spec),
        check_vma=False,
    )
```

```python
import jax
import jax.numpy as jnp
from jax import lax
from jax.experimental import pallas as pl
from jax.experimental.pallas import tpu as pltpu
from jax.sharding import PartitionSpec as P

DEVICES = 256
ROWS, COLS = 26, 34
WIDTH = 128
CAP = 7
MORE = 11
EDGE = 16
MSG_EDGES = 18
MSG = MSG_EDGES * EDGE + 8
CHUNK = CAP * EDGE + 16
SWAP = 16 * EDGE + 8
F32 = jnp.float32
I32 = jnp.int32


def params(mib):
    return pltpu.CompilerParams(vmem_limit_bytes=mib * 1024 * 1024)


VM = pl.BlockSpec(memory_space=pltpu.VMEM)
SM = pl.BlockSpec(memory_space=pltpu.SMEM)
HB = pl.BlockSpec(memory_space=pl.ANY)


CODES = 28


def lane_iota(rows):
    return lax.broadcasted_iota(I32, (rows, WIDTH), 1)


def row_iota(rows):
    return lax.broadcasted_iota(I32, (rows, WIDTH), 0)


def exact_dot(a, b):
    return jnp.dot(a.astype(jnp.bfloat16), b.astype(jnp.bfloat16), preferred_element_type=F32)


def ids_kernel(counts_hbm, land_hbm, grid, marks, counts, land, board, sem):
    copies = [pltpu.make_async_copy(counts_hbm, counts, sem.at[0]), pltpu.make_async_copy(land_hbm, land, sem.at[1])]
    for copy in copies:
        copy.start()
    for copy in copies:
        copy.wait()
    me = lax.axis_index("blk").astype(I32)
    board[...] = jnp.ones((32, WIDTH), I32)
    board[pl.ds(0, ROWS), pl.ds(0, COLS)] = land[...]
    sea = board[...] == 0
    lane, row = lane_iota(32), row_iota(32)
    ones = sea.astype(F32)
    i, j = row_iota(WIDTH), lane_iota(WIDTH)
    along = exact_dot(ones, i <= j)
    totals = exact_dot(ones, i >= 0)
    li, lj = lax.broadcasted_iota(I32, (32, 32), 0), lax.broadcasted_iota(I32, (32, 32), 1)
    pos = (exact_dot(lj < li, totals) + along - ones).astype(I32)

    def device(n, carry):
        end, owner, start = carry
        for k in range(8):
            d = n * 8 + k
            end = end + counts[d]
            past = pos >= end
            owner = jnp.where(past, d + 1, owner)
            start = jnp.where(past, end, start)
        return end, owner, start

    zero = jnp.zeros((32, WIDTH), I32)
    _, owner, start = lax.fori_loop(0, DEVICES // 8, device, (jnp.int32(0), zero, zero))
    ids = jnp.where(sea, owner * 4 + pos - start, -1)
    grid[...] = ids
    slot = (ids & 7).astype(F32)
    here = jnp.right_shift(ids, 3) == jnp.right_shift(me, 1)
    last = jnp.max(jnp.where(here, slot, 0.0))
    first_col = jnp.max(jnp.where(here & (lane == 0), slot, 0.0))
    last_col = -jnp.max(jnp.where(here & (lane == COLS - 1), -slot, -7.0))
    lane8 = lane_iota(8)
    marks[...] = jnp.where(lane8 == 0, last, jnp.where(lane8 == 1, first_col, last_col)).astype(I32)


def tables_kernel(grid, codes, mine, picks, load):
    me = lax.axis_index("blk").astype(I32)
    column, zed, core = me >> 4, (me >> 1) & 7, me & 1
    ids = grid[...].astype(F32)
    sea = ids >= 0.0
    lane, row = lane_iota(32), row_iota(32)
    i, j = row_iota(WIDTH), lane_iota(WIDTH)
    zero = jnp.zeros((32, WIDTH), I32)

    def west(x):
        return jnp.where(lane == 0, pltpu.roll(x, WIDTH - COLS + 1, 1), pltpu.roll(x, 1, 1))

    def east(x):
        return jnp.where(lane == COLS - 1, pltpu.roll(x, COLS - 1, 1), pltpu.roll(x, WIDTH - 1, 1))

    mirror = (i + j == COLS - 1).astype(F32)
    folded = jnp.dot(ids, mirror, preferred_element_type=F32, precision=lax.Precision.HIGHEST)
    south = jnp.where(row == 0, -1.0, pltpu.roll(ids, 1, 0))
    north = jnp.where(row == ROWS - 1, folded, pltpu.roll(ids, 31, 0))
    near = [south, north, west(ids), east(ids), west(south), east(south), west(north), east(north)]
    pairs = [(near[2 * k] + 1.0) * 2048.0 + (near[2 * k + 1] + 1.0) for k in range(4)]
    place = (row * WIDTH + lane).astype(F32)

    chip = jnp.right_shift(ids.astype(I32), 3)
    kinds = []
    for k in range(4):
        source = jnp.right_shift(near[k].astype(I32), 3)
        away = sea & (source >= 0) & (source != chip)
        kinds.append(jnp.where(away, (source & 7) + jnp.where(source > chip, 8, 0), -1))
    kind_row = row_iota(16)
    counted = jnp.zeros((WIDTH, 16), F32)
    for r in range(ROWS):
        is_chip = (chip[r : r + 1, :] == i).astype(jnp.bfloat16)
        of_kind = sum((kinds[k][r : r + 1, :] == kind_row).astype(F32) for k in range(4)).astype(jnp.bfloat16)
        counted += lax.dot_general(is_chip, of_kind, (((1,), (1,)), ((), ())), preferred_element_type=F32)
    load[...] = jnp.broadcast_to(jnp.max(counted), (8, WIDTH)).astype(I32)
    home = jnp.right_shift(chip, 3)
    beyond = zero
    for x in near:
        source = jnp.right_shift(x.astype(I32), 3)
        column_s, z_s = jnp.right_shift(source, 3), source & 7
        gap = home - column_s
        reached = (gap >= -2) & (gap <= 2)
        reached |= (gap == 3) & (column_s <= 1) & (z_s >= 6)
        reached |= (gap == -3) & (column_s <= 4) & (z_s <= 1)
        reached |= ((gap == 4) & (source == 0)) | ((gap == -4) & (source == 33))
        beyond = jnp.where(sea & (source >= 0) & ~reached, 1, beyond)
    missed = jnp.broadcast_to(jnp.max(beyond.astype(F32)), (8, WIDTH)).astype(I32)
    load[...] = jnp.where(lane_iota(8) == 1, missed, load[...])

    slot = row_iota(64)
    want = (column * 64 + slot).astype(F32)
    found = [jnp.zeros((64, WIDTH), F32) for _ in range(4)] + [jnp.full((64, WIDTH), -1.0, F32)]
    for r in range(ROWS):
        hit = ids[r : r + 1, :] == want
        for k, x in enumerate(pairs + [place]):
            found[k] = jnp.where(hit, x[r : r + 1, :], found[k])
    found = [jnp.max(x, axis=1, keepdims=True).astype(I32) for x in found]
    place = found[4]
    live = place >= 0
    block_row, block_col = jnp.right_shift(place, 7), place & 127
    top = live & (block_row == ROWS - 1)
    ids8 = []
    for k in range(4):
        ids8 += [jnp.right_shift(found[k], 11) - 1, (found[k] & 2047) - 1]
    slot1 = lax.broadcasted_iota(I32, (64, 1), 0)
    here = column * 8 + jnp.right_shift(slot1, 3)
    down = core == 1
    items = {}
    for k in range(8):
        valid = ids8[k] >= 0
        source, t = jnp.right_shift(ids8[k], 3), ids8[k] & 7
        z, delta = source & 7, jnp.abs(jnp.right_shift(source, 3) - column)
        lower, same = source < here, source == here
        items[16 + k] = valid.astype(I32)
        if k < 4:
            flow = valid & ~same & (lower != down)
            if k < 2:
                edge = t if k == 0 else t + jnp.where(top & down, 10, 0)
            else:
                edge = jnp.where(down, 11 - k, 6 + k)
            at = delta * (MSG // 8) + edge * (EDGE // 8) + 1
            items[k] = jnp.where(flow & (z == zed), at, 0)
            items[4 + k] = jnp.where(flow, z, -1)
            of = (1, 0, 3, 2)[k]
            if k == 1:
                of = jnp.where(top, 1, 0)
            close = (t * 4 + of) * (EDGE // 8)
            base = jnp.where(lower != down, 4 * EDGE, 4 * EDGE + SWAP // 8)
            far = ((slot1 & 3) * 4 + k) * (EDGE // 8) + base
            items[8 + k] = jnp.where(valid, jnp.where(same, close, far), 4 * EDGE + 2 * SWAP // 8)
        else:
            flow = valid & ((lower | same) != down)
            hi = (0, 1, 0, 1)[k - 4]
            lane_at = 2 * t + hi
            if k >= 6:
                lane_at = jnp.where(top, 2 * t + 1 - hi, 16 + 2 * t + hi)
            at = z * (CHUNK // 8) + CAP * EDGE // 8 + jnp.right_shift(delta, 2)
            items[8 + k] = jnp.where(flow, at * WIDTH + 32 * (delta & 3) + lane_at, -1)
    items[24], items[25], items[26], items[27] = live.astype(I32), top.astype(I32), block_row, block_col
    sends = [items[k] > 0 for k in range(4)]
    lane64, slot64 = lane_iota(64), row_iota(64)
    masks = jnp.zeros((64, WIDTH), F32)
    for k in range(4):
        masks = jnp.where((lane64 == k) & sends[k], 1.0, masks)
    si, sj = lax.broadcasted_iota(I32, (64, 64), 0), lax.broadcasted_iota(I32, (64, 64), 1)
    before = exact_dot((sj < si) & (jnp.right_shift(si, 3) == jnp.right_shift(sj, 3)), masks)
    rank = jnp.sum(before, axis=1, keepdims=True).astype(I32)
    placed = jnp.zeros((64, WIDTH), F32)
    for k in range(4):
        placed = jnp.where(sends[k] & (lane64 == rank), items[k].astype(F32), placed)
        rank = rank + sends[k].astype(I32)
    zi, zj = lax.broadcasted_iota(I32, (8, 64), 0), lax.broadcasted_iota(I32, (8, 64), 1)
    picks[...] = exact_dot(jnp.right_shift(zj, 3) == zi, placed).astype(I32)
    table = jnp.zeros((64, WIDTH), I32)
    for k in range(CODES):
        table = jnp.where(lane64 == k, items[k], table)
    codes[...] = table
    mine[...] = codes[pl.ds(pl.multiple_of(zed * 8, 8), 8), :]


def rims_kernel(tr, ve, out, turned):
    lane = lane_iota(WIDTH) // 4
    gathered = jnp.zeros((WIDTH, WIDTH), F32)
    for slot in range(4):
        for fl in range(8):
            ref, k = (tr, fl) if fl < 4 else (ve, fl - 4)
            for depth in range(2):
                out[pl.ds((slot * 4 + 0) * EDGE + depth * 8 + fl, 1), :] = ref[slot, k, pl.ds(depth, 1), :]
                out[pl.ds((slot * 4 + 1) * EDGE + depth * 8 + fl, 1), :] = ref[slot, k, pl.ds(127 - depth, 1), :]
            tile = slot * 8 + fl
            rolled = pltpu.roll(ref[slot, k], (4 * tile + 2) % WIDTH, 1)
            gathered = jnp.where(lane == tile, rolled, gathered)
    turned[...] = gathered.T
    for slot in range(4):
        for j, (side, depth) in enumerate([(3, 1), (3, 0), (2, 0), (2, 1)]):
            out[pl.ds((slot * 4 + side) * EDGE + depth * 8, 8), :] = turned[pl.ds(slot * 32 + j, 8, stride=4), :]


def message_kernel(table_hbm, mine, other, chip, out, table, sem):
    fetch = pltpu.make_async_copy(table_hbm, table, sem.at[0])
    fetch.start()
    core = lax.axis_index("blk").astype(I32) & 1
    flag = core == 0
    for t in range(4):
        for side in range(4):
            at = (t * 4 + side) * EDGE
            a, b = mine[pl.ds(at, EDGE), :], other[pl.ds(at, EDGE), :]
            chip[pl.ds(at, EDGE), :] = jnp.where(flag, a, b)
            chip[pl.ds(16 * EDGE + at, EDGE), :] = jnp.where(flag, b, a)
    for t in range(8):
        at = pl.multiple_of(jnp.where(flag, t * 4 + 1, t * 4) * EDGE, EDGE)
        out[pl.ds(t * EDGE, EDGE), :] = chip[pl.ds(at, EDGE), :]
        out[pl.ds((10 + t) * EDGE, EDGE), :] = chip[pl.ds((t * 4 + 1) * EDGE, EDGE), :]
    lane = lax.broadcasted_iota(I32, (8, WIDTH), 1) // 2
    corners = jnp.zeros((8, WIDTH), F32)
    for t in range(8):
        for side, base in ((1, 0), (0, 8)):
            x = chip[pl.ds((t * 4 + side) * EDGE, 8), :]
            corners = jnp.where(lane == base + t, pltpu.roll(x, 2 * (base + t) + 1, 1), corners)
    out[pl.ds(MSG_EDGES * EDGE, 8), :] = corners
    fetch.wait()
    last, first_col, last_col = table[0, 0], table[0, 1], table[0, 2]
    for e, edge in ((8, jnp.where(flag, last * 4 + 3, 2)), (9, jnp.where(flag, first_col * 4 + 2, last_col * 4 + 3))):
        at = pl.multiple_of(edge * EDGE, EDGE)
        out[pl.ds(e * EDGE, EDGE), :] = chip[pl.ds(at, EDGE), :]


def pack_kernel(picks_hbm, m0, m1, m2, m3, c4, c5, out, picks, started, held, packed, sem, sent):
    messages = (m0, m1, m2, m3)
    fetch = pltpu.make_async_copy(picks_hbm, picks, sem.at[14])
    fetch.start()
    copies = [
        pltpu.make_async_copy(m.at[pl.ds(MSG_EDGES * EDGE, 8)] if i < 4 else m, held.at[pl.ds(i * 8, 8)], sem.at[i])
        for i, m in enumerate((*messages, c4, c5))
    ]
    for copy in copies:
        copy.start()
    started[0] = 0
    fetch.wait()

    def edge(k, r):
        code = picks[k, r]

        @pl.when(code > 0)
        def _():
            started[0] = started[0] + 1
            for i, m in enumerate(messages):

                @pl.when((code > i * (MSG // 8)) & (code <= (i + 1) * (MSG // 8)))
                def _():
                    row = pl.multiple_of((code - 1 - i * (MSG // 8)) * 8, EDGE)
                    pltpu.make_async_copy(m.at[pl.ds(row, EDGE)], out.at[pl.ds(k * CHUNK + r * EDGE, EDGE)], sent.at[0]).start()

            if r + 1 < CAP:
                edge(k, r + 1)

    for k in range(8):
        edge(k, 0)
    for copy in copies:
        copy.wait()
    lane = lane_iota(8) // 32
    near_c = held[pl.ds(0, 8), :]
    for i in range(1, 4):
        near_c = jnp.where(lane == i, pltpu.roll(held[pl.ds(i * 8, 8), :], 32 * i, 1), near_c)
    packed[pl.ds(0, 8), :] = near_c
    packed[pl.ds(8, 8), :] = jnp.where(lane == 0, held[pl.ds(32, 8), :], pltpu.roll(held[pl.ds(40, 8), :], 32, 1))
    copies = [pltpu.make_async_copy(packed, out.at[pl.ds(k * CHUNK + CAP * EDGE, 16)], sem.at[6 + k]) for k in range(8)]
    for copy in copies:
        copy.start()

    def wait(i, carry):
        pltpu.make_async_copy(m0.at[pl.ds(0, EDGE)], out.at[pl.ds(0, EDGE)], sent.at[0]).wait()
        return carry

    lax.fori_loop(0, started[0], wait, 0)
    for copy in copies:
        copy.wait()


def sort_kernel(table_hbm, got_in, own, other, table, taken, rows, got, sem):
    fetch = pltpu.make_async_copy(table_hbm, table, sem.at[0])
    fetch.start()
    copies = [
        pltpu.make_async_copy(got_in.at[pl.ds(z * CHUNK, CHUNK)], got.at[pl.ds(z * CHUNK, CHUNK)], sem.at[1 + z]) for z in range(8)
    ]
    for copy in copies:
        copy.start()
    core = lax.axis_index("blk").astype(I32) & 1
    for z in range(8):
        taken[z] = 0
    fetch.wait()
    for t in range(8):
        for side in range(4):
            code = table[t, 4 + side]
            z = jnp.maximum(code, 0)
            rank = taken[z]
            taken[z] = rank + (code >= 0).astype(I32)
            rows[t * 4 + side] = z * CHUNK + jnp.minimum(rank, CAP - 1) * EDGE
    for copy in copies:
        copy.wait()
    lane = lane_iota(8)
    for half, out in enumerate((own, other)):
        first = (core ^ half) * 4
        corners = jnp.zeros((8, WIDTH), F32)
        for e in range(16):
            at = pl.multiple_of(rows[first * 4 + e], EDGE)
            out[pl.ds(e * EDGE, EDGE), :] = got[pl.ds(at, EDGE), :]
            code = table[first + e // 4, 12 + e % 4]
            turn = (e - code) & (WIDTH - 1)
            at = pl.multiple_of(jnp.right_shift(jnp.maximum(code, 0), 7) * 8, 8)
            corners = jnp.where(lane == jnp.where(code >= 0, e, -1), pltpu.roll(got[pl.ds(at, 8), :], turn, 1), corners)
        out[pl.ds(16 * EDGE, 8), :] = corners


def pressure(t0, t1, s0, s1):
    r0 = t0 * (-0.3 - 0.08 * t0 + 0.05 * s0) + 0.6 * s0
    r1 = t1 * (-0.3 - 0.08 * t1 + 0.05 * s1) + 0.6 * s1
    return 0.25 * r0, 0.5 * r0 + 0.25 * r1


def stencil(c, e, w, n, s, oe, ow, on, os, f):
    def times(o, x):
        return x if o is None else o * x

    ue, uw = 0.025 * (c[2] + e[2]), 0.025 * (w[2] + c[2])
    vn, vs = 0.025 * (c[3] + n[3]), 0.025 * (s[3] + c[3])
    ae, be = times(oe, 0.05 - ue), times(oe, 0.05 + ue)
    aw, bw = times(ow, 0.05 + uw), times(ow, 0.05 - uw)
    an, bn = times(on, 0.05 - vn), times(on, 0.05 + vn)
    as_, bs = times(os, 0.05 + vs), times(os, 0.05 - vs)
    mid = 1.0 - ((be + bw) + (bn + bs))
    out = []
    for i in range(2):
        out.append(mid * c[i] + ((ae * e[i] + aw * w[i]) + (an * n[i] + as_ * s[i])))
    for i, (lo, hi, olo, ohi) in ((2, (w, e, ow, oe)), (3, (s, n, os, on))):
        lap = (times(oe, e[i] - c[i]) + times(ow, w[i] - c[i])) + (times(on, n[i] - c[i]) + times(os, s[i] - c[i]))
        grad = times(ohi, hi[4] - c[4]) + times(olo, c[4] - lo[4])
        turn = f * c[3] if i == 2 else -(f * c[2])
        out.append(c[i] + (0.1 * turn + 0.05 * (lap - grad)))
    return out


def inner_kernel(table, tr, ve, tr_out, ve_out, rims, xa, xb, gathered):
    core = lax.axis_index("blk").astype(I32) & 1
    y16 = lax.broadcasted_iota(I32, (EDGE, WIDTH), 0).astype(F32)
    lane = lane_iota(WIDTH)
    for src in (xa, xb):
        for q in range(10):
            src[q, pl.ds(0, 8), :] = jnp.zeros((8, WIDTH), F32)
            src[q, pl.ds(136, 8), :] = jnp.zeros((8, WIDTH), F32)

    def one_slot(slot, carry):
        base = table[core * 4 + slot, 26].astype(F32) * float(WIDTH)
        alive = table[core * 4 + slot, 24] == 1
        for q in range(8):
            ref, k = (tr, q) if q < 4 else (ve, q - 4)
            xa[q, pl.ds(8, WIDTH), :] = ref[slot, k]
        for step, src in enumerate((xa, xb)):
            for r in range(8, 8 + WIDTH, EDGE):
                p0, p1 = pressure(*[src[q, pl.ds(r, EDGE), :] for q in range(4)])
                src[8, pl.ds(r, EDGE), :] = p0
                src[9, pl.ds(r, EDGE), :] = p1
            for r in range(0, WIDTH, EDGE):
                f = (base + (y16 + (r + 0.5))) * (2.0 / (ROWS * WIDTH))
                for level in range(2):
                    c, e, w, n, s = [], [], [], [], []
                    for i in range(5):
                        q = 2 * i + level
                        x = src[q, pl.ds(8 + r, EDGE), :]
                        c.append(x)
                        e.append(pltpu.roll(x, WIDTH - 1, 1))
                        w.append(pltpu.roll(x, 1, 1))
                        n.append(src[q, pl.ds(9 + r, EDGE), :])
                        s.append(src[q, pl.ds(7 + r, EDGE), :])
                    new = stencil(c, e, w, n, s, None, None, None, None, f)
                    for i in range(4):
                        if step == 0:
                            xb[2 * i + level, pl.ds(8 + r, EDGE), :] = new[i]
                        else:
                            out = tr_out if i < 2 else ve_out
                            out[slot, 2 * (i % 2) + level, pl.ds(r, EDGE), :] = jnp.where(alive, new[i], 0.0)
        for q in range(8):
            at = pl.multiple_of(slot * 4 * EDGE, EDGE)
            for ring in range(2):
                rims[pl.ds(at + ring * 8 + q, 1), :] = xb[q, pl.ds(8 + 1 + ring, 1), :]
                rims[pl.ds(at + EDGE + ring * 8 + q, 1), :] = xb[q, pl.ds(8 + 126 - ring, 1), :]
            tile = slot * 8 + q
            x = xb[q, pl.ds(8, WIDTH), :]
            a, b = pltpu.roll(x, (tile * 4 + 3) & (WIDTH - 1), 1), pltpu.roll(x, (tile * 4 + 1) & (WIDTH - 1), 1)
            mine = jnp.right_shift(lane, 2) == tile
            gathered[...] = jnp.where(mine, jnp.where((lane & 3) < 2, a, b), gathered[...])
        return carry

    gathered[...] = jnp.zeros((WIDTH, WIDTH), F32)
    lax.fori_loop(0, 4, one_slot, 0)
    gathered[...] = gathered[...].T
    for slot in range(4):
        for j, (side, ring) in enumerate([(3, 1), (3, 0), (2, 0), (2, 1)]):
            rims[pl.ds((slot * 4 + side) * EDGE + ring * 8, 8), :] = gathered[pl.ds(slot * 32 + j, 8, stride=4), :]


def lateral(x, ring):
    even = (row_iota(8) & 1) == 0
    up, down = pltpu.roll(x, 7, 0), pltpu.roll(x, 1, 0)
    back = pltpu.roll(x, WIDTH - ring, 1) if ring else x
    ahead = pltpu.roll(x, ring, 1) if ring else x
    low = jnp.where(even, pltpu.roll(up, ring + 1, 1), back)
    high = jnp.where(even, ahead, pltpu.roll(down, WIDTH - 1 - ring, 1))
    return low, high


def final_kernel(
    table, chip, own, other, edges, rims, tr, ve, tr_out, ve_out, held, hx, inn, mid, crv, upd, first, r0, r1, turned, res_t, res_v, sem, sent
):
    sizes = (8 * 4 * EDGE, SWAP, SWAP)
    starts = (0, sizes[0], sizes[0] + SWAP)
    copies = [
        pltpu.make_async_copy(x, held.at[pl.ds(at, n)], sem.at[i]) for i, (x, at, n) in enumerate(zip((chip, own, other), starts, sizes))
    ]
    for copy in copies:
        copy.start()
    held[pl.ds(starts[2] + SWAP, EDGE), :] = jnp.zeros((EDGE, WIDTH), F32)
    core = lax.axis_index("blk").astype(I32) & 1

    def item(slot, k):
        return table[core * 4 + slot, k]

    def factor(slot, k):
        return item(slot, k).astype(F32)

    i0, i1 = row_iota(WIDTH), lane_iota(WIDTH)
    mirror = (i0 + i1 == WIDTH - 1).astype(F32)
    sign = jnp.where((row_iota(EDGE) & 7) >= 4, -1.0, 1.0)
    lane8, sub8 = lane_iota(8), row_iota(8)
    even = (sub8 & 1) == 0
    sign8 = jnp.where(sub8 >= 4, -1.0, 1.0)
    where_to = ((0, 1), (0, 0), (1, 1), (1, 0))

    for slot in range(4):
        for side in range(4):
            group, odd = where_to[side]
            at = (slot * 4 + side) * EDGE
            inn[group, :, slot * 2 + odd, :] = edges[pl.ds(at, EDGE), :]
            mid[group, :, slot * 2 + odd, :] = rims[pl.ds(at, EDGE), :]
    for copy in copies:
        copy.wait()
    corners = held[pl.ds(starts[1] + 16 * EDGE, 8), :] + held[pl.ds(starts[2] + 16 * EDGE, 8), :]
    for slot in range(4):
        top = item(slot, 25) == 1
        for side in range(4):
            group, odd = where_to[side]
            x = held[pl.ds(pl.multiple_of(item(slot, 8 + side) * 8, 8), EDGE), :]
            if side == 1:
                flipped = jnp.dot(x, mirror, preferred_element_type=F32, precision=lax.Precision.HIGHEST) * sign
                x = jnp.where(top, flipped, x)
            hx[group, :, slot * 2 + odd, :] = x
        for group, odd, lo, hi in ((0, 0, 2, 3), (0, 1, 0, 1), (1, 0, 1, 3), (1, 1, 0, 2)):
            vals = []
            for which, lane in ((lo, 0), (hi, WIDTH - 1)):
                v = pltpu.roll(corners, (lane - (slot * 4 + which)) % WIDTH, 1)
                if which >= 2:
                    v = jnp.where(top, v * sign8, v)
                vals.append(v)
            crv[group, :, slot * 2 + odd, :] = jnp.where(lane8 == 0, vals[0], vals[1])

    def strip(group, c, outer, inner, low, high, o_out, o_low, o_high, cor, out):
        at_c, at_p, at_m, at_h, at_l = [], [], [], [], []
        for q in range(8):
            x = c(q)
            at_c.append(x)
            at_p.append(jnp.where(even, outer(q), inner(q)))
            at_m.append(jnp.where(even, inner(q), outer(q)))
            lo, hi = low(q), high(q)
            at_h.append(jnp.where(lane8 == WIDTH - 1, hi, pltpu.roll(x, WIDTH - 1, 1)))
            at_l.append(jnp.where(lane8 == 0, lo, pltpu.roll(x, 1, 1)))
        five = [x + list(pressure(x[0], x[1], x[2], x[3])) for x in (at_c, at_p, at_m, at_h, at_l)]
        o_pos = None if o_out is None else jnp.where(even, o_out, 1.0)
        o_neg = None if o_out is None else jnp.where(even, 1.0, o_out)
        for level in range(2):
            c, p, m, h, l = [[x[2 * i + level] for i in range(5)] for x in five]
            if group == 0:
                new = stencil(c, h, l, p, m, o_high, o_low, o_pos, o_neg, cor)
            else:
                new = stencil(c, p, m, h, l, o_pos, o_neg, o_high, o_low, cor)
            for i in range(4):
                out[group, 2 * i + level] = new[i]

    def by_row(values):
        x = jnp.zeros((8, WIDTH), F32)
        for slot in range(4):
            for odd in range(2):
                x = jnp.where(sub8 == slot * 2 + odd, values(slot, odd), x)
        return x

    def ends(x, where):
        return jnp.where(lane8 == where, x, 1.0)

    scale = 2.0 / (ROWS * WIDTH)
    base = by_row(lambda slot, odd: factor(slot, 26) * float(WIDTH))
    halo_row = by_row(
        lambda slot, odd: -1.0 if odd else jnp.where(item(slot, 25) == 1, WIDTH - 1.0, float(WIDTH)),
    )
    across = (base + lane8.astype(F32) + 0.5) * scale
    o_out, o_low, o_high, cor0, cor1 = [], [], [], [], []
    for group in range(2):
        o_out.append(by_row(lambda slot, odd: factor(slot, ((17, 16), (19, 18))[group][odd])))
        lo, hi = ((18, 19), (16, 17))[group]
        o_low.append(ends(by_row(lambda slot, odd: factor(slot, lo)), 0))
        o_high.append(ends(by_row(lambda slot, odd: factor(slot, hi)), WIDTH - 1))
        if group == 0:
            cor0.append((base + jnp.where(even, WIDTH - 1.0, 0.0) + 0.5) * scale)
            cor1.append((base + jnp.where(even, WIDTH - 2.0, 1.0) + 0.5) * scale)
        else:
            cor0.append(across)
            cor1.append(across)

    for group in range(2):
        lo, hi = ((22, 23), (20, 21)) if group == 0 else ((21, 23), (20, 22))
        corner_low = ends(by_row(lambda slot, odd: factor(slot, (lo, hi)[odd][0])), 0)
        corner_high = ends(by_row(lambda slot, odd: factor(slot, (lo, hi)[odd][1])), WIDTH - 1)
        cor = (base + halo_row + 0.5) * scale if group == 0 else across
        strip(
            group,
            lambda q: hx[group, q],
            lambda q: hx[group, 8 + q],
            lambda q: inn[group, q],
            lambda q: crv[group, q],
            lambda q: crv[group, q],
            None,
            corner_low,
            corner_high,
            cor,
            upd,
        )
    for group in range(2):
        beyond = [lateral(hx[1 - group, q], 0) for q in range(8)]
        strip(
            group,
            lambda q: inn[group, q],
            lambda q: hx[group, q],
            lambda q: inn[group, 8 + q],
            lambda q: beyond[q][0],
            lambda q: beyond[q][1],
            o_out[group],
            o_low[group],
            o_high[group],
            cor0[group],
            first,
        )
    for group in range(2):
        for q in range(8):
            for ring in (1, 2):
                low, high = lateral(first[1 - group, q], ring)
                x = mid[group, (ring - 1) * 8 + q]
                mid[group, (ring - 1) * 8 + q] = jnp.where(lane8 == 0, low, jnp.where(lane8 == WIDTH - 1, high, x))
    for group in range(2):
        beyond0 = [lateral(upd[1 - group, q], 0) for q in range(8)]
        strip(
            group,
            lambda q: first[group, q],
            lambda q: upd[group, q],
            lambda q: mid[group, q],
            lambda q: beyond0[q][0],
            lambda q: beyond0[q][1],
            o_out[group],
            o_low[group],
            o_high[group],
            cor0[group],
            r0,
        )
        beyond1 = [lateral(upd[1 - group, q], 1) for q in range(8)]
        strip(
            group,
            lambda q: mid[group, q],
            lambda q: first[group, q],
            lambda q: mid[group, 8 + q],
            lambda q: beyond1[q][0],
            lambda q: beyond1[q][1],
            None,
            o_low[group],
            o_high[group],
            cor1[group],
            r1,
        )

    live8 = by_row(lambda slot, odd: factor(slot, 24)) > 0.5
    for group in range(2):
        for q in range(8):
            r0[group, q] = jnp.where(live8, r0[group, q], 0.0)
            r1[group, q] = jnp.where(live8, r1[group, q], 0.0)
    for q in range(8):
        for slot in range(4):
            for j, (ring, odd) in enumerate(((r1, 0), (r0, 0), (r0, 1), (r1, 1))):
                turned[pl.ds((slot * 8 + q) * 4 + j, 1), :] = ring[1, q, pl.ds(slot * 2 + odd, 1), :]
    turned[...] = turned[...].T
    lane16 = lane_iota(EDGE)
    rim = (lane16 < 2) | (lane16 >= WIDTH - 2)
    out_copies = []
    for slot in range(4):
        for q in range(8):
            src, res, k = (tr, res_t, q) if q < 4 else (ve, res_v, q - 4)
            tile = slot * 8 + q
            for r in range(0, WIDTH, EDGE):
                x = pltpu.roll(turned[pl.ds(r, EDGE), :], (-(tile * 4 + 2)) % WIDTH, 1)
                res[slot, k, pl.ds(r, EDGE), :] = jnp.where(rim, x, src[slot, k, pl.ds(r, EDGE), :])
            for ring, rr in ((0, r0), (1, r1)):
                res[slot, k, pl.ds(ring, 1), :] = rr[0, q, pl.ds(slot * 2 + 1, 1), :]
                res[slot, k, pl.ds(WIDTH - 1 - ring, 1), :] = rr[0, q, pl.ds(slot * 2, 1), :]
        for i, (res, out) in enumerate(((res_t, tr_out), (res_v, ve_out))):
            copy = pltpu.make_async_copy(res.at[slot], out.at[slot], sent.at[slot * 2 + i])
            copy.start()
            out_copies.append(copy)
    for copy in out_copies:
        copy.wait()


def shape(*dims):
    return jax.ShapeDtypeStruct(dims, F32)


def table_shape(rows):
    return jax.ShapeDtypeStruct((rows, WIDTH), I32)


def exclusive_count(mask):
    i = jnp.arange(mask.shape[-1])
    return jnp.sum(mask[..., None, :] & (i[None, :] < i[:, None]), axis=-1).astype(I32)


def permute(x, pairs):
    return lax.ppermute(x, "blk", pairs)


def column_pairs(distance):
    pairs = []
    for i in range(DEVICES):
        j = i + 16 * distance * (1 if i % 2 == 0 else -1)
        pairs.append((i, j if 0 <= j < DEVICES else i ^ 1))
    return pairs


NEAR_PAIRS = [(i, i + 48) for i in range(32) if i % 2 == 0 and i % 16 >= 12]
NEAR_PAIRS += [(i, i - 48) for i in range(48, 80) if i % 2 == 1 and i % 16 < 4]
FAR_PAIRS = [(0, 64), (67, 3)]


def exchange_z(x):
    groups = [[16 * a + 2 * z + c for z in range(8)] for a in range(16) for c in range(2)]
    return lax.all_to_all(x, "blk", 0, 0, axis_index_groups=groups, tiled=True)


def pack(picks, message, near, far):
    return pl.pallas_call(
        pack_kernel,
        out_shape=shape(8 * CHUNK, WIDTH),
        in_specs=[HB] * 7,
        out_specs=HB,
        scratch_shapes=[
            pltpu.SMEM((8, WIDTH), I32),
            pltpu.SMEM((1,), I32),
            pltpu.VMEM((48, WIDTH), F32),
            pltpu.VMEM((16, WIDTH), F32),
            pltpu.SemaphoreType.DMA((15,)),
            pltpu.SemaphoreType.DMA((1,)),
        ],
        compiler_params=params(12),
        name="pack",
    )(picks, message, *near, *far)


def sort(mine, got):
    return pl.pallas_call(
        sort_kernel,
        out_shape=(shape(SWAP, WIDTH), shape(SWAP, WIDTH)),
        in_specs=[HB, HB],
        out_specs=(VM, VM),
        scratch_shapes=[
            pltpu.SMEM((8, WIDTH), I32),
            pltpu.SMEM((8,), I32),
            pltpu.SMEM((32,), I32),
            pltpu.VMEM((8 * CHUNK, WIDTH), F32),
            pltpu.SemaphoreType.DMA((9,)),
        ],
        compiler_params=params(12),
        name="sort",
    )(mine, got)


def per_device(tracers, velocity, block_counts, land):
    tr = tracers.reshape(4, 4, WIDTH, WIDTH)
    ve = velocity.reshape(4, 4, WIDTH, WIDTH)
    swap = [(i, i ^ 1) for i in range(DEVICES)]

    grid, marks = pl.pallas_call(
        ids_kernel,
        out_shape=(table_shape(32), table_shape(8)),
        in_specs=[HB, HB],
        out_specs=(VM, VM),
        scratch_shapes=[
            pltpu.SMEM((DEVICES,), I32),
            pltpu.VMEM((ROWS, COLS), I32),
            pltpu.VMEM((32, WIDTH), I32),
            pltpu.SemaphoreType.DMA((2,)),
        ],
        compiler_params=params(12),
        cost_estimate=pl.CostEstimate(flops=2_000_000, bytes_accessed=100_000, transcendentals=0),
        name="ids",
    )(block_counts, land)
    rims = pl.pallas_call(
        rims_kernel,
        out_shape=shape(16 * EDGE, WIDTH),
        in_specs=[VM, VM],
        out_specs=VM,
        scratch_shapes=[pltpu.VMEM((WIDTH, WIDTH), F32)],
        compiler_params=params(12),
        name="rims",
    )(tr, ve)
    codes, mine, picks, load = pl.pallas_call(
        tables_kernel,
        out_shape=(table_shape(64), table_shape(8), table_shape(8), table_shape(8)),
        in_specs=[VM],
        out_specs=(VM, VM, VM, VM),
        compiler_params=params(12),
        cost_estimate=pl.CostEstimate(flops=2_000_000, bytes_accessed=100_000, transcendentals=0),
        name="tables",
    )(grid)
    other = permute(rims, swap)
    chip, message = pl.pallas_call(
        message_kernel,
        out_shape=(shape(32 * EDGE, WIDTH), shape(MSG, WIDTH)),
        in_specs=[HB, VM, VM],
        out_specs=(VM, VM),
        scratch_shapes=[pltpu.SMEM((8, WIDTH), I32), pltpu.SemaphoreType.DMA((1,))],
        compiler_params=params(12),
        name="message",
    )(marks, rims, other)
    corners = message[MSG_EDGES * EDGE :]
    far = permute(corners, FAR_PAIRS)
    near = [permute(message, NEAR_PAIRS), *[permute(message, column_pairs(d)) for d in (1, 2)]]
    near = [near[1], near[2], near[0]]
    chunks = pack(picks, message, near, (far, far))
    tr, ve, chunks = lax.optimization_barrier((tr, ve, chunks))
    tr_inner, ve_inner, inner_rims = pl.pallas_call(
        inner_kernel,
        out_shape=(shape(4, 4, WIDTH, WIDTH), shape(4, 4, WIDTH, WIDTH), shape(16 * EDGE, WIDTH)),
        in_specs=[SM, VM, VM],
        out_specs=(VM, VM, VM),
        scratch_shapes=[
            pltpu.VMEM((10, 144, WIDTH), F32),
            pltpu.VMEM((10, 144, WIDTH), F32),
            pltpu.VMEM((WIDTH, WIDTH), F32),
        ],
        compiler_params=params(12),
        cost_estimate=pl.CostEstimate(flops=60_000_000, bytes_accessed=8_000_000, transcendentals=0),
        name="inner",
    )(mine, tr, ve)
    got = exchange_z(chunks.reshape(8, CHUNK, WIDTH)).reshape(8 * CHUNK, WIDTH)
    got, tr_inner, ve_inner, inner_rims = lax.optimization_barrier((got, tr_inner, ve_inner, inner_rims))
    own, others = sort(mine, got)

    def general(args):
        _, _, codes, mine, picks, message, near = args
        corners = message[MSG_EDGES * EDGE :]
        near = [near[0], near[1], permute(message, column_pairs(3))]
        chunks = pack(picks, message, near, [permute(corners, column_pairs(d)) for d in (4, 5)])
        got = exchange_z(chunks.reshape(8, CHUNK, WIDTH)).reshape(8 * CHUNK, WIDTH)
        own, others = sort(mine, got)
        down = (lax.axis_index("blk").astype(I32) & 1) == 1
        held = jnp.concatenate([message, *near])
        send = codes[:, :4].reshape(8, 32)
        rank = exclusive_count(send > 0)
        late = jnp.arange(CAP, CAP + MORE)
        more = jnp.sum(jnp.where((send > 0)[:, None] & (rank[:, None] == late[None, :, None]), send[:, None] - 1, 0), axis=-1)
        rows = more[:, :, None] * 8 + jnp.arange(EDGE, dtype=I32)
        more = exchange_z(held[rows].reshape(8, MORE * EDGE, WIDTH)).reshape(8 * MORE * EDGE, WIDTH)
        zed = mine[:, 4:8].reshape(32)
        i32 = jnp.arange(32)
        rank = jnp.sum((zed[None] >= 0) & (zed[None] == zed[:, None]) & (i32[None] < i32[:, None]), axis=1).astype(I32)
        late = (zed >= 0) & (rank >= CAP)
        start = jnp.where(late, zed * (MORE * EDGE) + (rank - CAP) * EDGE, 0)
        start, late = [jnp.where(down, jnp.concatenate([x[16:], x[:16]]), x) for x in (start, late)]
        new = more[start[:, None] + jnp.arange(EDGE, dtype=I32)]
        old = jnp.stack([own[: 16 * EDGE], others[: 16 * EDGE]]).reshape(32, EDGE, WIDTH)
        new = jnp.where(late[:, None, None], new, old).reshape(2, 16 * EDGE, WIDTH)
        return jnp.concatenate([new[0], own[16 * EDGE :]]), jnp.concatenate([new[1], others[16 * EDGE :]])

    own, others = lax.cond(
        (load[0, 0] > CAP) | (load[0, 1] > 0),
        general,
        lambda args: (args[0], args[1]),
        (own, others, codes, mine, picks, message, near),
    )
    theirs = permute(others, swap)

    tr_new, ve_new = pl.pallas_call(
        final_kernel,
        out_shape=(shape(4, 4, WIDTH, WIDTH), shape(4, 4, WIDTH, WIDTH)),
        in_specs=[SM] + [HB] * 3 + [VM] * 4,
        out_specs=(HB, HB),
        scratch_shapes=[
            pltpu.VMEM((32 * EDGE + 2 * SWAP + EDGE, WIDTH), F32),
            pltpu.VMEM((2, EDGE, 8, WIDTH), F32),
            pltpu.VMEM((2, EDGE, 8, WIDTH), F32),
            pltpu.VMEM((2, EDGE, 8, WIDTH), F32),
            pltpu.VMEM((2, 8, 8, WIDTH), F32),
            pltpu.VMEM((2, 8, 8, WIDTH), F32),
            pltpu.VMEM((2, 8, 8, WIDTH), F32),
            pltpu.VMEM((2, 8, 8, WIDTH), F32),
            pltpu.VMEM((2, 8, 8, WIDTH), F32),
            pltpu.VMEM((WIDTH, WIDTH), F32),
            pltpu.VMEM((4, 4, WIDTH, WIDTH), F32),
            pltpu.VMEM((4, 4, WIDTH, WIDTH), F32),
            pltpu.SemaphoreType.DMA((3,)),
            pltpu.SemaphoreType.DMA((8,)),
        ],
        compiler_params=params(12),
        name="final",
    )(mine, chip, own, theirs, rims, inner_rims, tr_inner, ve_inner)
    return tr_new.reshape(tracers.shape), ve_new.reshape(velocity.shape)


def solution(mesh):
    spec = P("blk", None, None, None, None)
    return jax.shard_map(
        per_device,
        mesh=mesh,
        in_specs=(spec, spec, P(), P()),
        out_specs=(spec, spec),
        check_vma=False,
    )
```

```python
import jax
import jax.numpy as jnp
from jax import lax
from jax.experimental import pallas as pl
from jax.experimental.pallas import tpu as pltpu
from jax.sharding import PartitionSpec as P

DEVICES = 256
ROWS, COLS = 26, 34
WIDTH = 128
CAP = 7
MORE = 11
EDGE = 16
MSG_EDGES = 18
MSG = MSG_EDGES * EDGE + 8
CHUNK = CAP * EDGE + 16
SWAP = 16 * EDGE + 8
F32 = jnp.float32
I32 = jnp.int32


def params(mib):
    return pltpu.CompilerParams(vmem_limit_bytes=mib * 1024 * 1024)


VM = pl.BlockSpec(memory_space=pltpu.VMEM)
SM = pl.BlockSpec(memory_space=pltpu.SMEM)
HB = pl.BlockSpec(memory_space=pl.ANY)


CODES = 28


def lane_iota(rows):
    return lax.broadcasted_iota(I32, (rows, WIDTH), 1)


def row_iota(rows):
    return lax.broadcasted_iota(I32, (rows, WIDTH), 0)


def exact_dot(a, b):
    return jnp.dot(a.astype(jnp.bfloat16), b.astype(jnp.bfloat16), preferred_element_type=F32)


def ids_kernel(counts_hbm, land_hbm, grid, marks, counts, land, board, sem):
    copies = [pltpu.make_async_copy(counts_hbm, counts, sem.at[0]), pltpu.make_async_copy(land_hbm, land, sem.at[1])]
    for copy in copies:
        copy.start()
    for copy in copies:
        copy.wait()
    me = lax.axis_index("blk").astype(I32)
    board[...] = jnp.ones((32, WIDTH), I32)
    board[pl.ds(0, ROWS), pl.ds(0, COLS)] = land[...]
    sea = board[...] == 0
    lane, row = lane_iota(32), row_iota(32)
    ones = sea.astype(F32)
    i, j = row_iota(WIDTH), lane_iota(WIDTH)
    along = exact_dot(ones, i <= j)
    totals = exact_dot(ones, i >= 0)
    li, lj = lax.broadcasted_iota(I32, (32, 32), 0), lax.broadcasted_iota(I32, (32, 32), 1)
    pos = (exact_dot(lj < li, totals) + along - ones).astype(I32)

    def device(n, carry):
        end, owner, start = carry
        for k in range(8):
            d = n * 8 + k
            end = end + counts[d]
            past = pos >= end
            owner = jnp.where(past, d + 1, owner)
            start = jnp.where(past, end, start)
        return end, owner, start

    zero = jnp.zeros((32, WIDTH), I32)
    _, owner, start = lax.fori_loop(0, DEVICES // 8, device, (jnp.int32(0), zero, zero))
    ids = jnp.where(sea, owner * 4 + pos - start, -1)
    grid[...] = ids
    slot = (ids & 7).astype(F32)
    here = jnp.right_shift(ids, 3) == jnp.right_shift(me, 1)
    last = jnp.max(jnp.where(here, slot, 0.0))
    first_col = jnp.max(jnp.where(here & (lane == 0), slot, 0.0))
    last_col = -jnp.max(jnp.where(here & (lane == COLS - 1), -slot, -7.0))
    lane8 = lane_iota(8)
    marks[...] = jnp.where(lane8 == 0, last, jnp.where(lane8 == 1, first_col, last_col)).astype(I32)


def tables_kernel(grid, codes, mine, picks, enough):
    me = lax.axis_index("blk").astype(I32)
    column, zed, core = me >> 4, (me >> 1) & 7, me & 1
    ids = grid[...].astype(F32)
    sea = ids >= 0.0
    lane, row = lane_iota(32), row_iota(32)
    i, j = row_iota(WIDTH), lane_iota(WIDTH)
    zero = jnp.zeros((32, WIDTH), I32)

    def west(x):
        return jnp.where(lane == 0, pltpu.roll(x, WIDTH - COLS + 1, 1), pltpu.roll(x, 1, 1))

    def east(x):
        return jnp.where(lane == COLS - 1, pltpu.roll(x, COLS - 1, 1), pltpu.roll(x, WIDTH - 1, 1))

    mirror = (i + j == COLS - 1).astype(F32)
    folded = jnp.dot(ids, mirror, preferred_element_type=F32, precision=lax.Precision.HIGHEST)
    south = jnp.where(row == 0, -1.0, pltpu.roll(ids, 1, 0))
    north = jnp.where(row == ROWS - 1, folded, pltpu.roll(ids, 31, 0))
    near = [south, north, west(ids), east(ids), west(south), east(south), west(north), east(north)]
    pairs = [(near[2 * k] + 1.0) * 2048.0 + (near[2 * k + 1] + 1.0) for k in range(4)]
    place = (row * WIDTH + lane).astype(F32)

    chip = jnp.right_shift(ids.astype(I32), 3)
    kinds = []
    for k in range(4):
        source = jnp.right_shift(near[k].astype(I32), 3)
        away = sea & (source >= 0) & (source != chip)
        kinds.append(jnp.where(away, (source & 7) + jnp.where(source > chip, 8, 0), -1))
    kind_row = row_iota(16)
    counted = jnp.zeros((WIDTH, 16), F32)
    for r in range(ROWS):
        is_chip = (chip[r : r + 1, :] == i).astype(jnp.bfloat16)
        of_kind = sum((kinds[k][r : r + 1, :] == kind_row).astype(F32) for k in range(4)).astype(jnp.bfloat16)
        counted += lax.dot_general(is_chip, of_kind, (((1,), (1,)), ((), ())), preferred_element_type=F32)
    home = jnp.right_shift(chip, 3)
    beyond = zero
    for x in near:
        source = jnp.right_shift(x.astype(I32), 3)
        column_s, z_s = jnp.right_shift(source, 3), source & 7
        gap = home - column_s
        reached = (gap >= -2) & (gap <= 2)
        reached |= (gap == 3) & (column_s <= 1) & (z_s >= 6)
        reached |= (gap == -3) & (column_s <= 4) & (z_s <= 1)
        reached |= ((gap == 4) & (source == 0)) | ((gap == -4) & (source == 33))
        beyond = jnp.where(sea & (source >= 0) & ~reached, 1, beyond)
    enough[0] = ((jnp.max(counted) < CAP + 0.5) & (jnp.max(beyond.astype(F32)) < 0.5)).astype(I32)

    slot = row_iota(64)
    want = (column * 64 + slot).astype(F32)
    found = [jnp.zeros((64, WIDTH), F32) for _ in range(4)] + [jnp.full((64, WIDTH), -1.0, F32)]
    for r in range(ROWS):
        hit = ids[r : r + 1, :] == want
        for k, x in enumerate(pairs + [place]):
            found[k] = jnp.where(hit, x[r : r + 1, :], found[k])
    found = [jnp.max(x, axis=1, keepdims=True).astype(I32) for x in found]
    place = found[4]
    live = place >= 0
    block_row, block_col = jnp.right_shift(place, 7), place & 127
    top = live & (block_row == ROWS - 1)
    ids8 = []
    for k in range(4):
        ids8 += [jnp.right_shift(found[k], 11) - 1, (found[k] & 2047) - 1]
    slot1 = lax.broadcasted_iota(I32, (64, 1), 0)
    here = column * 8 + jnp.right_shift(slot1, 3)
    down = core == 1
    items = {}
    for k in range(8):
        valid = ids8[k] >= 0
        source, t = jnp.right_shift(ids8[k], 3), ids8[k] & 7
        z, delta = source & 7, jnp.abs(jnp.right_shift(source, 3) - column)
        lower, same = source < here, source == here
        items[16 + k] = valid.astype(I32)
        if k < 4:
            flow = valid & ~same & (lower != down)
            if k < 2:
                edge = t if k == 0 else t + jnp.where(top & down, 10, 0)
            else:
                edge = jnp.where(down, 11 - k, 6 + k)
            at = delta * (MSG // 8) + edge * (EDGE // 8) + 1
            items[k] = jnp.where(flow & (z == zed), at, 0)
            items[4 + k] = jnp.where(flow, z, -1)
            of = (1, 0, 3, 2)[k]
            if k == 1:
                of = jnp.where(top, 1, 0)
            close = (t * 4 + of) * (EDGE // 8)
            base = jnp.where(lower != down, 4 * EDGE, 4 * EDGE + SWAP // 8)
            far = ((slot1 & 3) * 4 + k) * (EDGE // 8) + base
            items[8 + k] = jnp.where(valid, jnp.where(same, close, far), 4 * EDGE + 2 * SWAP // 8)
        else:
            flow = valid & ((lower | same) != down)
            hi = (0, 1, 0, 1)[k - 4]
            lane_at = 2 * t + hi
            if k >= 6:
                lane_at = jnp.where(top, 2 * t + 1 - hi, 16 + 2 * t + hi)
            at = z * (CHUNK // 8) + CAP * EDGE // 8 + jnp.right_shift(delta, 2)
            items[8 + k] = jnp.where(flow, at * WIDTH + 32 * (delta & 3) + lane_at, -1)
    items[24], items[25], items[26], items[27] = live.astype(I32), top.astype(I32), block_row, block_col
    sends = [items[k] > 0 for k in range(4)]
    lane64, slot64 = lane_iota(64), row_iota(64)
    masks = jnp.zeros((64, WIDTH), F32)
    for k in range(4):
        masks = jnp.where((lane64 == k) & sends[k], 1.0, masks)
    si, sj = lax.broadcasted_iota(I32, (64, 64), 0), lax.broadcasted_iota(I32, (64, 64), 1)
    before = exact_dot((sj < si) & (jnp.right_shift(si, 3) == jnp.right_shift(sj, 3)), masks)
    rank = jnp.sum(before, axis=1, keepdims=True).astype(I32)
    placed = jnp.zeros((64, WIDTH), F32)
    for k in range(4):
        placed = jnp.where(sends[k] & (lane64 == rank), items[k].astype(F32), placed)
        rank = rank + sends[k].astype(I32)
    zi, zj = lax.broadcasted_iota(I32, (8, 64), 0), lax.broadcasted_iota(I32, (8, 64), 1)
    picks[...] = exact_dot(jnp.right_shift(zj, 3) == zi, placed).astype(I32)
    table = jnp.zeros((64, WIDTH), I32)
    for k in range(CODES):
        table = jnp.where(lane64 == k, items[k], table)
    codes[...] = table
    mine[...] = codes[pl.ds(pl.multiple_of(zed * 8, 8), 8), :]


def rims_kernel(tr, ve, out, turned):
    lane = lane_iota(WIDTH) // 4
    gathered = jnp.zeros((WIDTH, WIDTH), F32)
    for slot in range(4):
        for fl in range(8):
            ref, k = (tr, fl) if fl < 4 else (ve, fl - 4)
            for depth in range(2):
                out[pl.ds((slot * 4 + 0) * EDGE + depth * 8 + fl, 1), :] = ref[slot, k, pl.ds(depth, 1), :]
                out[pl.ds((slot * 4 + 1) * EDGE + depth * 8 + fl, 1), :] = ref[slot, k, pl.ds(127 - depth, 1), :]
            tile = slot * 8 + fl
            rolled = pltpu.roll(ref[slot, k], (4 * tile + 2) % WIDTH, 1)
            gathered = jnp.where(lane == tile, rolled, gathered)
    turned[...] = gathered.T
    for slot in range(4):
        for j, (side, depth) in enumerate([(3, 1), (3, 0), (2, 0), (2, 1)]):
            out[pl.ds((slot * 4 + side) * EDGE + depth * 8, 8), :] = turned[pl.ds(slot * 32 + j, 8, stride=4), :]


def message_kernel(table_hbm, mine, other, chip, out, table, sem):
    fetch = pltpu.make_async_copy(table_hbm, table, sem.at[0])
    fetch.start()
    core = lax.axis_index("blk").astype(I32) & 1
    flag = core == 0
    for t in range(4):
        for side in range(4):
            at = (t * 4 + side) * EDGE
            a, b = mine[pl.ds(at, EDGE), :], other[pl.ds(at, EDGE), :]
            chip[pl.ds(at, EDGE), :] = jnp.where(flag, a, b)
            chip[pl.ds(16 * EDGE + at, EDGE), :] = jnp.where(flag, b, a)
    for t in range(8):
        at = pl.multiple_of(jnp.where(flag, t * 4 + 1, t * 4) * EDGE, EDGE)
        out[pl.ds(t * EDGE, EDGE), :] = chip[pl.ds(at, EDGE), :]
        out[pl.ds((10 + t) * EDGE, EDGE), :] = chip[pl.ds((t * 4 + 1) * EDGE, EDGE), :]
    lane = lax.broadcasted_iota(I32, (8, WIDTH), 1) // 2
    corners = jnp.zeros((8, WIDTH), F32)
    for t in range(8):
        for side, base in ((1, 0), (0, 8)):
            x = chip[pl.ds((t * 4 + side) * EDGE, 8), :]
            corners = jnp.where(lane == base + t, pltpu.roll(x, 2 * (base + t) + 1, 1), corners)
    out[pl.ds(MSG_EDGES * EDGE, 8), :] = corners
    fetch.wait()
    last, first_col, last_col = table[0, 0], table[0, 1], table[0, 2]
    for e, edge in ((8, jnp.where(flag, last * 4 + 3, 2)), (9, jnp.where(flag, first_col * 4 + 2, last_col * 4 + 3))):
        at = pl.multiple_of(edge * EDGE, EDGE)
        out[pl.ds(e * EDGE, EDGE), :] = chip[pl.ds(at, EDGE), :]


def pack_kernel(picks_hbm, m0, m1, m2, m3, c4, c5, out, picks, started, held, packed, sem, sent):
    messages = (m0, m1, m2, m3)
    fetch = pltpu.make_async_copy(picks_hbm, picks, sem.at[14])
    fetch.start()
    copies = [
        pltpu.make_async_copy(m.at[pl.ds(MSG_EDGES * EDGE, 8)] if i < 4 else m, held.at[pl.ds(i * 8, 8)], sem.at[i])
        for i, m in enumerate((*messages, c4, c5))
    ]
    for copy in copies:
        copy.start()
    started[0] = 0
    fetch.wait()

    def edge(k, r):
        code = picks[k, r]

        @pl.when(code > 0)
        def _():
            started[0] = started[0] + 1
            for i, m in enumerate(messages):

                @pl.when((code > i * (MSG // 8)) & (code <= (i + 1) * (MSG // 8)))
                def _():
                    row = pl.multiple_of((code - 1 - i * (MSG // 8)) * 8, EDGE)
                    pltpu.make_async_copy(m.at[pl.ds(row, EDGE)], out.at[pl.ds(k * CHUNK + r * EDGE, EDGE)], sent.at[0]).start()

            if r + 1 < CAP:
                edge(k, r + 1)

    for k in range(8):
        edge(k, 0)
    for copy in copies:
        copy.wait()
    lane = lane_iota(8) // 32
    near_c = held[pl.ds(0, 8), :]
    for i in range(1, 4):
        near_c = jnp.where(lane == i, pltpu.roll(held[pl.ds(i * 8, 8), :], 32 * i, 1), near_c)
    packed[pl.ds(0, 8), :] = near_c
    packed[pl.ds(8, 8), :] = jnp.where(lane == 0, held[pl.ds(32, 8), :], pltpu.roll(held[pl.ds(40, 8), :], 32, 1))
    copies = [pltpu.make_async_copy(packed, out.at[pl.ds(k * CHUNK + CAP * EDGE, 16)], sem.at[6 + k]) for k in range(8)]
    for copy in copies:
        copy.start()

    def wait(i, carry):
        pltpu.make_async_copy(m0.at[pl.ds(0, EDGE)], out.at[pl.ds(0, EDGE)], sent.at[0]).wait()
        return carry

    lax.fori_loop(0, started[0], wait, 0)
    for copy in copies:
        copy.wait()


def sort_kernel(table_hbm, got_in, own, other, table, taken, rows, got, sem):
    fetch = pltpu.make_async_copy(table_hbm, table, sem.at[0])
    fetch.start()
    copies = [
        pltpu.make_async_copy(got_in.at[pl.ds(z * CHUNK, CHUNK)], got.at[pl.ds(z * CHUNK, CHUNK)], sem.at[1 + z]) for z in range(8)
    ]
    for copy in copies:
        copy.start()
    core = lax.axis_index("blk").astype(I32) & 1
    for z in range(8):
        taken[z] = 0
    fetch.wait()
    for t in range(8):
        for side in range(4):
            code = table[t, 4 + side]
            z = jnp.maximum(code, 0)
            rank = taken[z]
            taken[z] = rank + (code >= 0).astype(I32)
            rows[t * 4 + side] = z * CHUNK + jnp.minimum(rank, CAP - 1) * EDGE
    for copy in copies:
        copy.wait()
    lane = lane_iota(8)
    for half, out in enumerate((own, other)):
        first = (core ^ half) * 4
        corners = jnp.zeros((8, WIDTH), F32)
        for e in range(16):
            at = pl.multiple_of(rows[first * 4 + e], EDGE)
            out[pl.ds(e * EDGE, EDGE), :] = got[pl.ds(at, EDGE), :]
            code = table[first + e // 4, 12 + e % 4]
            turn = (e - code) & (WIDTH - 1)
            at = pl.multiple_of(jnp.right_shift(jnp.maximum(code, 0), 7) * 8, 8)
            corners = jnp.where(lane == jnp.where(code >= 0, e, -1), pltpu.roll(got[pl.ds(at, 8), :], turn, 1), corners)
        out[pl.ds(16 * EDGE, 8), :] = corners


def pressure(t0, t1, s0, s1):
    r0 = t0 * (-0.3 - 0.08 * t0 + 0.05 * s0) + 0.6 * s0
    r1 = t1 * (-0.3 - 0.08 * t1 + 0.05 * s1) + 0.6 * s1
    return 0.25 * r0, 0.5 * r0 + 0.25 * r1


def stencil(c, e, w, n, s, oe, ow, on, os, f):
    def times(o, x):
        return x if o is None else o * x

    ue, uw = 0.025 * (c[2] + e[2]), 0.025 * (w[2] + c[2])
    vn, vs = 0.025 * (c[3] + n[3]), 0.025 * (s[3] + c[3])
    ae, be = times(oe, 0.05 - ue), times(oe, 0.05 + ue)
    aw, bw = times(ow, 0.05 + uw), times(ow, 0.05 - uw)
    an, bn = times(on, 0.05 - vn), times(on, 0.05 + vn)
    as_, bs = times(os, 0.05 + vs), times(os, 0.05 - vs)
    mid = 1.0 - ((be + bw) + (bn + bs))
    out = []
    for i in range(2):
        out.append(mid * c[i] + ((ae * e[i] + aw * w[i]) + (an * n[i] + as_ * s[i])))
    for i, (lo, hi, olo, ohi) in ((2, (w, e, ow, oe)), (3, (s, n, os, on))):
        lap = (times(oe, e[i] - c[i]) + times(ow, w[i] - c[i])) + (times(on, n[i] - c[i]) + times(os, s[i] - c[i]))
        grad = times(ohi, hi[4] - c[4]) + times(olo, c[4] - lo[4])
        turn = f * c[3] if i == 2 else -(f * c[2])
        out.append(c[i] + (0.1 * turn + 0.05 * (lap - grad)))
    return out


def inner_kernel(table, tr, ve, tr_out, ve_out, rims, xa, xb, gathered):
    core = lax.axis_index("blk").astype(I32) & 1
    y16 = lax.broadcasted_iota(I32, (EDGE, WIDTH), 0).astype(F32)
    lane = lane_iota(WIDTH)
    for src in (xa, xb):
        for q in range(10):
            src[q, pl.ds(0, 8), :] = jnp.zeros((8, WIDTH), F32)
            src[q, pl.ds(136, 8), :] = jnp.zeros((8, WIDTH), F32)

    def one_slot(slot, carry):
        base = table[core * 4 + slot, 26].astype(F32) * float(WIDTH)
        alive = table[core * 4 + slot, 24] == 1
        for q in range(8):
            ref, k = (tr, q) if q < 4 else (ve, q - 4)
            xa[q, pl.ds(8, WIDTH), :] = ref[slot, k]
        for step, src in enumerate((xa, xb)):
            for r in range(8, 8 + WIDTH, EDGE):
                p0, p1 = pressure(*[src[q, pl.ds(r, EDGE), :] for q in range(4)])
                src[8, pl.ds(r, EDGE), :] = p0
                src[9, pl.ds(r, EDGE), :] = p1
            for r in range(0, WIDTH, EDGE):
                f = (base + (y16 + (r + 0.5))) * (2.0 / (ROWS * WIDTH))
                for level in range(2):
                    c, e, w, n, s = [], [], [], [], []
                    for i in range(5):
                        q = 2 * i + level
                        x = src[q, pl.ds(8 + r, EDGE), :]
                        c.append(x)
                        e.append(pltpu.roll(x, WIDTH - 1, 1))
                        w.append(pltpu.roll(x, 1, 1))
                        n.append(src[q, pl.ds(9 + r, EDGE), :])
                        s.append(src[q, pl.ds(7 + r, EDGE), :])
                    new = stencil(c, e, w, n, s, None, None, None, None, f)
                    for i in range(4):
                        if step == 0:
                            xb[2 * i + level, pl.ds(8 + r, EDGE), :] = new[i]
                        else:
                            out = tr_out if i < 2 else ve_out
                            out[slot, 2 * (i % 2) + level, pl.ds(r, EDGE), :] = jnp.where(alive, new[i], 0.0)
        for q in range(8):
            at = pl.multiple_of(slot * 4 * EDGE, EDGE)
            for ring in range(2):
                rims[pl.ds(at + ring * 8 + q, 1), :] = xb[q, pl.ds(8 + 1 + ring, 1), :]
                rims[pl.ds(at + EDGE + ring * 8 + q, 1), :] = xb[q, pl.ds(8 + 126 - ring, 1), :]
            tile = slot * 8 + q
            x = xb[q, pl.ds(8, WIDTH), :]
            a, b = pltpu.roll(x, (tile * 4 + 3) & (WIDTH - 1), 1), pltpu.roll(x, (tile * 4 + 1) & (WIDTH - 1), 1)
            mine = jnp.right_shift(lane, 2) == tile
            gathered[...] = jnp.where(mine, jnp.where((lane & 3) < 2, a, b), gathered[...])
        return carry

    gathered[...] = jnp.zeros((WIDTH, WIDTH), F32)
    lax.fori_loop(0, 4, one_slot, 0)
    gathered[...] = gathered[...].T
    for slot in range(4):
        for j, (side, ring) in enumerate([(3, 1), (3, 0), (2, 0), (2, 1)]):
            rims[pl.ds((slot * 4 + side) * EDGE + ring * 8, 8), :] = gathered[pl.ds(slot * 32 + j, 8, stride=4), :]


def lateral(x, ring):
    even = (row_iota(8) & 1) == 0
    up, down = pltpu.roll(x, 7, 0), pltpu.roll(x, 1, 0)
    back = pltpu.roll(x, WIDTH - ring, 1) if ring else x
    ahead = pltpu.roll(x, ring, 1) if ring else x
    low = jnp.where(even, pltpu.roll(up, ring + 1, 1), back)
    high = jnp.where(even, ahead, pltpu.roll(down, WIDTH - 1 - ring, 1))
    return low, high


def final_kernel(
    table, chip, own, other, edges, rims, tr, ve, tr_out, ve_out, held, hx, inn, mid, crv, upd, first, r0, r1, turned, res_t, res_v, sem, sent
):
    sizes = (8 * 4 * EDGE, SWAP, SWAP)
    starts = (0, sizes[0], sizes[0] + SWAP)
    copies = [
        pltpu.make_async_copy(x, held.at[pl.ds(at, n)], sem.at[i]) for i, (x, at, n) in enumerate(zip((chip, own, other), starts, sizes))
    ]
    for copy in copies:
        copy.start()
    held[pl.ds(starts[2] + SWAP, EDGE), :] = jnp.zeros((EDGE, WIDTH), F32)
    core = lax.axis_index("blk").astype(I32) & 1

    def item(slot, k):
        return table[core * 4 + slot, k]

    def factor(slot, k):
        return item(slot, k).astype(F32)

    i0, i1 = row_iota(WIDTH), lane_iota(WIDTH)
    mirror = (i0 + i1 == WIDTH - 1).astype(F32)
    sign = jnp.where((row_iota(EDGE) & 7) >= 4, -1.0, 1.0)
    lane8, sub8 = lane_iota(8), row_iota(8)
    even = (sub8 & 1) == 0
    sign8 = jnp.where(sub8 >= 4, -1.0, 1.0)
    where_to = ((0, 1), (0, 0), (1, 1), (1, 0))

    for slot in range(4):
        for side in range(4):
            group, odd = where_to[side]
            at = (slot * 4 + side) * EDGE
            inn[group, :, slot * 2 + odd, :] = edges[pl.ds(at, EDGE), :]
            mid[group, :, slot * 2 + odd, :] = rims[pl.ds(at, EDGE), :]
    for copy in copies:
        copy.wait()
    corners = held[pl.ds(starts[1] + 16 * EDGE, 8), :] + held[pl.ds(starts[2] + 16 * EDGE, 8), :]
    for slot in range(4):
        top = item(slot, 25) == 1
        for side in range(4):
            group, odd = where_to[side]
            x = held[pl.ds(pl.multiple_of(item(slot, 8 + side) * 8, 8), EDGE), :]
            if side == 1:
                flipped = jnp.dot(x, mirror, preferred_element_type=F32, precision=lax.Precision.HIGHEST) * sign
                x = jnp.where(top, flipped, x)
            hx[group, :, slot * 2 + odd, :] = x
        for group, odd, lo, hi in ((0, 0, 2, 3), (0, 1, 0, 1), (1, 0, 1, 3), (1, 1, 0, 2)):
            vals = []
            for which, lane in ((lo, 0), (hi, WIDTH - 1)):
                v = pltpu.roll(corners, (lane - (slot * 4 + which)) % WIDTH, 1)
                if which >= 2:
                    v = jnp.where(top, v * sign8, v)
                vals.append(v)
            crv[group, :, slot * 2 + odd, :] = jnp.where(lane8 == 0, vals[0], vals[1])

    def strip(group, c, outer, inner, low, high, o_out, o_low, o_high, cor, out):
        at_c, at_p, at_m, at_h, at_l = [], [], [], [], []
        for q in range(8):
            x = c(q)
            at_c.append(x)
            at_p.append(jnp.where(even, outer(q), inner(q)))
            at_m.append(jnp.where(even, inner(q), outer(q)))
            lo, hi = low(q), high(q)
            at_h.append(jnp.where(lane8 == WIDTH - 1, hi, pltpu.roll(x, WIDTH - 1, 1)))
            at_l.append(jnp.where(lane8 == 0, lo, pltpu.roll(x, 1, 1)))
        five = [x + list(pressure(x[0], x[1], x[2], x[3])) for x in (at_c, at_p, at_m, at_h, at_l)]
        o_pos = None if o_out is None else jnp.where(even, o_out, 1.0)
        o_neg = None if o_out is None else jnp.where(even, 1.0, o_out)
        for level in range(2):
            c, p, m, h, l = [[x[2 * i + level] for i in range(5)] for x in five]
            if group == 0:
                new = stencil(c, h, l, p, m, o_high, o_low, o_pos, o_neg, cor)
            else:
                new = stencil(c, p, m, h, l, o_pos, o_neg, o_high, o_low, cor)
            for i in range(4):
                out[group, 2 * i + level] = new[i]

    def by_row(values):
        x = jnp.zeros((8, WIDTH), F32)
        for slot in range(4):
            for odd in range(2):
                x = jnp.where(sub8 == slot * 2 + odd, values(slot, odd), x)
        return x

    def ends(x, where):
        return jnp.where(lane8 == where, x, 1.0)

    scale = 2.0 / (ROWS * WIDTH)
    base = by_row(lambda slot, odd: factor(slot, 26) * float(WIDTH))
    halo_row = by_row(
        lambda slot, odd: -1.0 if odd else jnp.where(item(slot, 25) == 1, WIDTH - 1.0, float(WIDTH)),
    )
    across = (base + lane8.astype(F32) + 0.5) * scale
    o_out, o_low, o_high, cor0, cor1 = [], [], [], [], []
    for group in range(2):
        o_out.append(by_row(lambda slot, odd: factor(slot, ((17, 16), (19, 18))[group][odd])))
        lo, hi = ((18, 19), (16, 17))[group]
        o_low.append(ends(by_row(lambda slot, odd: factor(slot, lo)), 0))
        o_high.append(ends(by_row(lambda slot, odd: factor(slot, hi)), WIDTH - 1))
        if group == 0:
            cor0.append((base + jnp.where(even, WIDTH - 1.0, 0.0) + 0.5) * scale)
            cor1.append((base + jnp.where(even, WIDTH - 2.0, 1.0) + 0.5) * scale)
        else:
            cor0.append(across)
            cor1.append(across)

    for group in range(2):
        lo, hi = ((22, 23), (20, 21)) if group == 0 else ((21, 23), (20, 22))
        corner_low = ends(by_row(lambda slot, odd: factor(slot, (lo, hi)[odd][0])), 0)
        corner_high = ends(by_row(lambda slot, odd: factor(slot, (lo, hi)[odd][1])), WIDTH - 1)
        cor = (base + halo_row + 0.5) * scale if group == 0 else across
        strip(
            group,
            lambda q: hx[group, q],
            lambda q: hx[group, 8 + q],
            lambda q: inn[group, q],
            lambda q: crv[group, q],
            lambda q: crv[group, q],
            None,
            corner_low,
            corner_high,
            cor,
            upd,
        )
    for group in range(2):
        beyond = [lateral(hx[1 - group, q], 0) for q in range(8)]
        strip(
            group,
            lambda q: inn[group, q],
            lambda q: hx[group, q],
            lambda q: inn[group, 8 + q],
            lambda q: beyond[q][0],
            lambda q: beyond[q][1],
            o_out[group],
            o_low[group],
            o_high[group],
            cor0[group],
            first,
        )
    for group in range(2):
        for q in range(8):
            for ring in (1, 2):
                low, high = lateral(first[1 - group, q], ring)
                x = mid[group, (ring - 1) * 8 + q]
                mid[group, (ring - 1) * 8 + q] = jnp.where(lane8 == 0, low, jnp.where(lane8 == WIDTH - 1, high, x))
    for group in range(2):
        beyond0 = [lateral(upd[1 - group, q], 0) for q in range(8)]
        strip(
            group,
            lambda q: first[group, q],
            lambda q: upd[group, q],
            lambda q: mid[group, q],
            lambda q: beyond0[q][0],
            lambda q: beyond0[q][1],
            o_out[group],
            o_low[group],
            o_high[group],
            cor0[group],
            r0,
        )
        beyond1 = [lateral(upd[1 - group, q], 1) for q in range(8)]
        strip(
            group,
            lambda q: mid[group, q],
            lambda q: first[group, q],
            lambda q: mid[group, 8 + q],
            lambda q: beyond1[q][0],
            lambda q: beyond1[q][1],
            None,
            o_low[group],
            o_high[group],
            cor1[group],
            r1,
        )

    live8 = by_row(lambda slot, odd: factor(slot, 24)) > 0.5
    for group in range(2):
        for q in range(8):
            r0[group, q] = jnp.where(live8, r0[group, q], 0.0)
            r1[group, q] = jnp.where(live8, r1[group, q], 0.0)
    for q in range(8):
        for slot in range(4):
            for j, (ring, odd) in enumerate(((r1, 0), (r0, 0), (r0, 1), (r1, 1))):
                turned[pl.ds((slot * 8 + q) * 4 + j, 1), :] = ring[1, q, pl.ds(slot * 2 + odd, 1), :]
    turned[...] = turned[...].T
    lane16 = lane_iota(EDGE)
    rim = (lane16 < 2) | (lane16 >= WIDTH - 2)
    out_copies = []
    for slot in range(4):
        for q in range(8):
            src, res, k = (tr, res_t, q) if q < 4 else (ve, res_v, q - 4)
            tile = slot * 8 + q
            for r in range(0, WIDTH, EDGE):
                x = pltpu.roll(turned[pl.ds(r, EDGE), :], (-(tile * 4 + 2)) % WIDTH, 1)
                res[slot, k, pl.ds(r, EDGE), :] = jnp.where(rim, x, src[slot, k, pl.ds(r, EDGE), :])
            for ring, rr in ((0, r0), (1, r1)):
                res[slot, k, pl.ds(ring, 1), :] = rr[0, q, pl.ds(slot * 2 + 1, 1), :]
                res[slot, k, pl.ds(WIDTH - 1 - ring, 1), :] = rr[0, q, pl.ds(slot * 2, 1), :]
        for i, (res, out) in enumerate(((res_t, tr_out), (res_v, ve_out))):
            copy = pltpu.make_async_copy(res.at[slot], out.at[slot], sent.at[slot * 2 + i])
            copy.start()
            out_copies.append(copy)
    for copy in out_copies:
        copy.wait()


def shape(*dims):
    return jax.ShapeDtypeStruct(dims, F32)


def table_shape(rows):
    return jax.ShapeDtypeStruct((rows, WIDTH), I32)


def exclusive_count(mask):
    i = jnp.arange(mask.shape[-1])
    return jnp.sum(mask[..., None, :] & (i[None, :] < i[:, None]), axis=-1).astype(I32)


def permute(x, pairs):
    return lax.ppermute(x, "blk", pairs)


def column_pairs(distance):
    pairs = []
    for i in range(DEVICES):
        j = i + 16 * distance * (1 if i % 2 == 0 else -1)
        pairs.append((i, j if 0 <= j < DEVICES else i ^ 1))
    return pairs


NEAR_PAIRS = [(i, i + 48) for i in range(32) if i % 2 == 0 and i % 16 >= 12]
NEAR_PAIRS += [(i, i - 48) for i in range(48, 80) if i % 2 == 1 and i % 16 < 4]
FAR_PAIRS = [(0, 64), (67, 3)]


def exchange_z(x):
    groups = [[16 * a + 2 * z + c for z in range(8)] for a in range(16) for c in range(2)]
    return lax.all_to_all(x, "blk", 0, 0, axis_index_groups=groups, tiled=True)


def pack(picks, message, near, far):
    return pl.pallas_call(
        pack_kernel,
        out_shape=shape(8 * CHUNK, WIDTH),
        in_specs=[HB] * 7,
        out_specs=HB,
        scratch_shapes=[
            pltpu.SMEM((8, WIDTH), I32),
            pltpu.SMEM((1,), I32),
            pltpu.VMEM((48, WIDTH), F32),
            pltpu.VMEM((16, WIDTH), F32),
            pltpu.SemaphoreType.DMA((15,)),
            pltpu.SemaphoreType.DMA((1,)),
        ],
        compiler_params=params(12),
        name="pack",
    )(picks, message, *near, *far)


def sort(mine, got):
    return pl.pallas_call(
        sort_kernel,
        out_shape=(shape(SWAP, WIDTH), shape(SWAP, WIDTH)),
        in_specs=[HB, HB],
        out_specs=(VM, VM),
        scratch_shapes=[
            pltpu.SMEM((8, WIDTH), I32),
            pltpu.SMEM((8,), I32),
            pltpu.SMEM((32,), I32),
            pltpu.VMEM((8 * CHUNK, WIDTH), F32),
            pltpu.SemaphoreType.DMA((9,)),
        ],
        compiler_params=params(12),
        name="sort",
    )(mine, got)


def second_round(own, others, codes, mine, message, near):
    down = (lax.axis_index("blk").astype(I32) & 1) == 1
    held = jnp.concatenate([message, *near])
    send = codes[:, :4].reshape(8, 32)
    rank = exclusive_count(send > 0)
    late = jnp.arange(CAP, CAP + MORE)
    more = jnp.sum(jnp.where((send > 0)[:, None] & (rank[:, None] == late[None, :, None]), send[:, None] - 1, 0), axis=-1)
    rows = more[:, :, None] * 8 + jnp.arange(EDGE, dtype=I32)
    more = exchange_z(held[rows].reshape(8, MORE * EDGE, WIDTH)).reshape(8 * MORE * EDGE, WIDTH)
    zed = mine[:, 4:8].reshape(32)
    i32 = jnp.arange(32)
    rank = jnp.sum((zed[None] >= 0) & (zed[None] == zed[:, None]) & (i32[None] < i32[:, None]), axis=1).astype(I32)
    late = (zed >= 0) & (rank >= CAP)
    start = jnp.where(late, zed * (MORE * EDGE) + (rank - CAP) * EDGE, 0)
    start, late = [jnp.where(down, jnp.concatenate([x[16:], x[:16]]), x) for x in (start, late)]
    new = more[start[:, None] + jnp.arange(EDGE, dtype=I32)]
    old = jnp.stack([own[: 16 * EDGE], others[: 16 * EDGE]]).reshape(32, EDGE, WIDTH)
    new = jnp.where(late[:, None, None], new, old).reshape(2, 16 * EDGE, WIDTH)
    return jnp.concatenate([new[0], own[16 * EDGE :]]), jnp.concatenate([new[1], others[16 * EDGE :]])


def run(tracers, velocity, block_counts, land, usual):
    tr = tracers.reshape(4, 4, WIDTH, WIDTH)
    ve = velocity.reshape(4, 4, WIDTH, WIDTH)
    swap = [(i, i ^ 1) for i in range(DEVICES)]

    grid, marks = pl.pallas_call(
        ids_kernel,
        out_shape=(table_shape(32), table_shape(8)),
        in_specs=[HB, HB],
        out_specs=(VM, VM),
        scratch_shapes=[
            pltpu.SMEM((DEVICES,), I32),
            pltpu.VMEM((ROWS, COLS), I32),
            pltpu.VMEM((32, WIDTH), I32),
            pltpu.SemaphoreType.DMA((2,)),
        ],
        compiler_params=params(12),
        cost_estimate=pl.CostEstimate(flops=2_000_000, bytes_accessed=100_000, transcendentals=0),
        name="ids",
    )(block_counts, land)
    rims = pl.pallas_call(
        rims_kernel,
        out_shape=shape(16 * EDGE, WIDTH),
        in_specs=[VM, VM],
        out_specs=VM,
        scratch_shapes=[pltpu.VMEM((WIDTH, WIDTH), F32)],
        compiler_params=params(12),
        name="rims",
    )(tr, ve)
    codes, mine, picks, enough = pl.pallas_call(
        tables_kernel,
        out_shape=(table_shape(64), table_shape(8), table_shape(8), jax.ShapeDtypeStruct((1,), I32)),
        in_specs=[VM],
        out_specs=(VM, VM, VM, SM),
        compiler_params=params(12),
        cost_estimate=pl.CostEstimate(flops=2_000_000, bytes_accessed=100_000, transcendentals=0),
        name="tables",
    )(grid)
    other = permute(rims, swap)
    chip, message = pl.pallas_call(
        message_kernel,
        out_shape=(shape(32 * EDGE, WIDTH), shape(MSG, WIDTH)),
        in_specs=[HB, VM, VM],
        out_specs=(VM, VM),
        scratch_shapes=[pltpu.SMEM((8, WIDTH), I32), pltpu.SemaphoreType.DMA((1,))],
        compiler_params=params(12),
        name="message",
    )(marks, rims, other)
    corners = message[MSG_EDGES * EDGE :]
    if usual:
        far = permute(corners, FAR_PAIRS)
        far = (far, far)
        near = [permute(message, NEAR_PAIRS), *[permute(message, column_pairs(d)) for d in (1, 2)]]
        near = [near[1], near[2], near[0]]
    else:
        far = [permute(corners, column_pairs(d)) for d in (4, 5)]
        near = [permute(message, column_pairs(d)) for d in (1, 2, 3)]
    chunks = pack(picks, message, near, far)
    tr, ve, chunks = lax.optimization_barrier((tr, ve, chunks))
    tr_inner, ve_inner, inner_rims = pl.pallas_call(
        inner_kernel,
        out_shape=(shape(4, 4, WIDTH, WIDTH), shape(4, 4, WIDTH, WIDTH), shape(16 * EDGE, WIDTH)),
        in_specs=[SM, VM, VM],
        out_specs=(VM, VM, VM),
        scratch_shapes=[
            pltpu.VMEM((10, 144, WIDTH), F32),
            pltpu.VMEM((10, 144, WIDTH), F32),
            pltpu.VMEM((WIDTH, WIDTH), F32),
        ],
        compiler_params=params(12),
        cost_estimate=pl.CostEstimate(flops=60_000_000, bytes_accessed=8_000_000, transcendentals=0),
        name="inner",
    )(mine, tr, ve)
    got = exchange_z(chunks.reshape(8, CHUNK, WIDTH)).reshape(8 * CHUNK, WIDTH)
    got, tr_inner, ve_inner, inner_rims = lax.optimization_barrier((got, tr_inner, ve_inner, inner_rims))
    own, others = sort(mine, got)
    if not usual:
        own, others = second_round(own, others, codes, mine, message, near)
    theirs = permute(others, swap)

    tr_new, ve_new = pl.pallas_call(
        final_kernel,
        out_shape=(shape(4, 4, WIDTH, WIDTH), shape(4, 4, WIDTH, WIDTH)),
        in_specs=[SM] + [HB] * 3 + [VM] * 4,
        out_specs=(HB, HB),
        scratch_shapes=[
            pltpu.VMEM((32 * EDGE + 2 * SWAP + EDGE, WIDTH), F32),
            pltpu.VMEM((2, EDGE, 8, WIDTH), F32),
            pltpu.VMEM((2, EDGE, 8, WIDTH), F32),
            pltpu.VMEM((2, EDGE, 8, WIDTH), F32),
            pltpu.VMEM((2, 8, 8, WIDTH), F32),
            pltpu.VMEM((2, 8, 8, WIDTH), F32),
            pltpu.VMEM((2, 8, 8, WIDTH), F32),
            pltpu.VMEM((2, 8, 8, WIDTH), F32),
            pltpu.VMEM((2, 8, 8, WIDTH), F32),
            pltpu.VMEM((WIDTH, WIDTH), F32),
            pltpu.VMEM((4, 4, WIDTH, WIDTH), F32),
            pltpu.VMEM((4, 4, WIDTH, WIDTH), F32),
            pltpu.SemaphoreType.DMA((3,)),
            pltpu.SemaphoreType.DMA((8,)),
        ],
        compiler_params=params(12),
        name="final",
    )(mine, chip, own, theirs, rims, inner_rims, tr_inner, ve_inner)
    return enough[0] != 0, tr_new.reshape(tracers.shape), ve_new.reshape(velocity.shape)


def per_device(tracers, velocity, block_counts, land):
    enough, *out = run(tracers, velocity, block_counts, land, True)

    def again(out, args):
        return run(*args, False)[1:]

    return lax.cond(enough, lambda out, args: tuple(out), again, tuple(out), (tracers, velocity, block_counts, land))


def solution(mesh):
    spec = P("blk", None, None, None, None)
    return jax.shard_map(
        per_device,
        mesh=mesh,
        in_specs=(spec, spec, P(), P()),
        out_specs=(spec, spec),
        check_vma=False,
    )
```

```python
import jax
import jax.numpy as jnp
from jax import lax
from jax.experimental import pallas as pl
from jax.experimental.pallas import tpu as pltpu
from jax.sharding import PartitionSpec as P

DEVICES = 256
ROWS, COLS = 26, 34
WIDTH = 128
CAP = 7
MORE = 11
EDGE = 16
MSG_EDGES = 18
MSG = MSG_EDGES * EDGE + 8
CHUNK = CAP * EDGE + 16
SWAP = 16 * EDGE + 8
F32 = jnp.float32
I32 = jnp.int32


def params(mib):
    return pltpu.CompilerParams(vmem_limit_bytes=mib * 1024 * 1024)


VM = pl.BlockSpec(memory_space=pltpu.VMEM)
SM = pl.BlockSpec(memory_space=pltpu.SMEM)
HB = pl.BlockSpec(memory_space=pl.ANY)


CODES = 28


def lane_iota(rows):
    return lax.broadcasted_iota(I32, (rows, WIDTH), 1)


def row_iota(rows):
    return lax.broadcasted_iota(I32, (rows, WIDTH), 0)


def exact_dot(a, b):
    return jnp.dot(a.astype(jnp.bfloat16), b.astype(jnp.bfloat16), preferred_element_type=F32)


def ids_kernel(counts_hbm, land_hbm, grid, marks, counts, land, board, sem):
    copies = [pltpu.make_async_copy(counts_hbm, counts, sem.at[0]), pltpu.make_async_copy(land_hbm, land, sem.at[1])]
    for copy in copies:
        copy.start()
    for copy in copies:
        copy.wait()
    me = lax.axis_index("blk").astype(I32)
    board[...] = jnp.ones((32, WIDTH), I32)
    board[pl.ds(0, ROWS), pl.ds(0, COLS)] = land[...]
    sea = board[...] == 0
    lane, row = lane_iota(32), row_iota(32)
    ones = sea.astype(F32)
    i, j = row_iota(WIDTH), lane_iota(WIDTH)
    along = exact_dot(ones, i <= j)
    totals = exact_dot(ones, i >= 0)
    li, lj = lax.broadcasted_iota(I32, (32, 32), 0), lax.broadcasted_iota(I32, (32, 32), 1)
    pos = (exact_dot(lj < li, totals) + along - ones).astype(I32)

    def device(n, carry):
        end, owner, start = carry
        for k in range(8):
            d = n * 8 + k
            end = end + counts[d]
            past = pos >= end
            owner = jnp.where(past, d + 1, owner)
            start = jnp.where(past, end, start)
        return end, owner, start

    zero = jnp.zeros((32, WIDTH), I32)
    _, owner, start = lax.fori_loop(0, DEVICES // 8, device, (jnp.int32(0), zero, zero))
    ids = jnp.where(sea, owner * 4 + pos - start, -1)
    grid[...] = ids
    slot = (ids & 7).astype(F32)
    here = jnp.right_shift(ids, 3) == jnp.right_shift(me, 1)
    last = jnp.max(jnp.where(here, slot, 0.0))
    first_col = jnp.max(jnp.where(here & (lane == 0), slot, 0.0))
    last_col = -jnp.max(jnp.where(here & (lane == COLS - 1), -slot, -7.0))
    lane8 = lane_iota(8)
    marks[...] = jnp.where(lane8 == 0, last, jnp.where(lane8 == 1, first_col, last_col)).astype(I32)


def tables_kernel(grid, codes, mine, picks, enough):
    me = lax.axis_index("blk").astype(I32)
    column, zed, core = me >> 4, (me >> 1) & 7, me & 1
    ids = grid[...].astype(F32)
    sea = ids >= 0.0
    lane, row = lane_iota(32), row_iota(32)
    i, j = row_iota(WIDTH), lane_iota(WIDTH)
    zero = jnp.zeros((32, WIDTH), I32)

    def west(x):
        return jnp.where(lane == 0, pltpu.roll(x, WIDTH - COLS + 1, 1), pltpu.roll(x, 1, 1))

    def east(x):
        return jnp.where(lane == COLS - 1, pltpu.roll(x, COLS - 1, 1), pltpu.roll(x, WIDTH - 1, 1))

    mirror = (i + j == COLS - 1).astype(F32)
    folded = jnp.dot(ids, mirror, preferred_element_type=F32, precision=lax.Precision.HIGHEST)
    south = jnp.where(row == 0, -1.0, pltpu.roll(ids, 1, 0))
    north = jnp.where(row == ROWS - 1, folded, pltpu.roll(ids, 31, 0))
    near = [south, north, west(ids), east(ids), west(south), east(south), west(north), east(north)]
    pairs = [(near[2 * k] + 1.0) * 2048.0 + (near[2 * k + 1] + 1.0) for k in range(4)]
    place = (row * WIDTH + lane).astype(F32)

    chip = jnp.right_shift(ids.astype(I32), 3)
    kinds = []
    for k in range(4):
        source = jnp.right_shift(near[k].astype(I32), 3)
        away = sea & (source >= 0) & (source != chip)
        kinds.append(jnp.where(away, (source & 7) + jnp.where(source > chip, 8, 0), -1))
    kind_row = row_iota(16)
    counted = jnp.zeros((WIDTH, 16), F32)
    for r in range(ROWS):
        is_chip = (chip[r : r + 1, :] == i).astype(jnp.bfloat16)
        of_kind = sum((kinds[k][r : r + 1, :] == kind_row).astype(F32) for k in range(4)).astype(jnp.bfloat16)
        counted += lax.dot_general(is_chip, of_kind, (((1,), (1,)), ((), ())), preferred_element_type=F32)
    home = jnp.right_shift(chip, 3)
    beyond = zero
    for x in near:
        source = jnp.right_shift(x.astype(I32), 3)
        column_s, z_s = jnp.right_shift(source, 3), source & 7
        gap = home - column_s
        reached = (gap >= -2) & (gap <= 2)
        reached |= (gap == 3) & (column_s <= 1) & (z_s >= 6)
        reached |= (gap == -3) & (column_s <= 4) & (z_s <= 1)
        reached |= ((gap == 4) & (source == 0)) | ((gap == -4) & (source == 33))
        beyond = jnp.where(sea & (source >= 0) & ~reached, 1, beyond)
    enough[0] = ((jnp.max(counted) < CAP + 0.5) & (jnp.max(beyond.astype(F32)) < 0.5)).astype(I32)

    slot = row_iota(64)
    want = (column * 64 + slot).astype(F32)
    found = [jnp.zeros((64, WIDTH), F32) for _ in range(4)] + [jnp.full((64, WIDTH), -1.0, F32)]
    for r in range(ROWS):
        hit = ids[r : r + 1, :] == want
        for k, x in enumerate(pairs + [place]):
            found[k] = jnp.where(hit, x[r : r + 1, :], found[k])
    found = [jnp.max(x, axis=1, keepdims=True).astype(I32) for x in found]
    place = found[4]
    live = place >= 0
    block_row, block_col = jnp.right_shift(place, 7), place & 127
    top = live & (block_row == ROWS - 1)
    ids8 = []
    for k in range(4):
        ids8 += [jnp.right_shift(found[k], 11) - 1, (found[k] & 2047) - 1]
    slot1 = lax.broadcasted_iota(I32, (64, 1), 0)
    here = column * 8 + jnp.right_shift(slot1, 3)
    down = core == 1
    items = {}
    for k in range(8):
        valid = ids8[k] >= 0
        source, t = jnp.right_shift(ids8[k], 3), ids8[k] & 7
        z, delta = source & 7, jnp.abs(jnp.right_shift(source, 3) - column)
        lower, same = source < here, source == here
        items[16 + k] = valid.astype(I32)
        if k < 4:
            flow = valid & ~same & (lower != down)
            if k < 2:
                edge = t if k == 0 else t + jnp.where(top & down, 10, 0)
            else:
                edge = jnp.where(down, 11 - k, 6 + k)
            at = delta * (MSG // 8) + edge * (EDGE // 8) + 1
            items[k] = jnp.where(flow & (z == zed), at, 0)
            items[4 + k] = jnp.where(flow, z, -1)
            of = (1, 0, 3, 2)[k]
            if k == 1:
                of = jnp.where(top, 1, 0)
            close = (t * 4 + of) * (EDGE // 8)
            base = jnp.where(lower != down, 4 * EDGE, 4 * EDGE + SWAP // 8)
            far = ((slot1 & 3) * 4 + k) * (EDGE // 8) + base
            items[8 + k] = jnp.where(valid, jnp.where(same, close, far), 4 * EDGE + 2 * SWAP // 8)
        else:
            flow = valid & ((lower | same) != down)
            hi = (0, 1, 0, 1)[k - 4]
            lane_at = 2 * t + hi
            if k >= 6:
                lane_at = jnp.where(top, 2 * t + 1 - hi, 16 + 2 * t + hi)
            at = z * (CHUNK // 8) + CAP * EDGE // 8 + jnp.right_shift(delta, 2)
            items[8 + k] = jnp.where(flow, at * WIDTH + 32 * (delta & 3) + lane_at, -1)
    items[24], items[25], items[26], items[27] = live.astype(I32), top.astype(I32), block_row, block_col
    sends = [items[k] > 0 for k in range(4)]
    lane64, slot64 = lane_iota(64), row_iota(64)
    masks = jnp.zeros((64, WIDTH), F32)
    for k in range(4):
        masks = jnp.where((lane64 == k) & sends[k], 1.0, masks)
    si, sj = lax.broadcasted_iota(I32, (64, 64), 0), lax.broadcasted_iota(I32, (64, 64), 1)
    before = exact_dot((sj < si) & (jnp.right_shift(si, 3) == jnp.right_shift(sj, 3)), masks)
    rank = jnp.sum(before, axis=1, keepdims=True).astype(I32)
    placed = jnp.zeros((64, WIDTH), F32)
    for k in range(4):
        placed = jnp.where(sends[k] & (lane64 == rank), items[k].astype(F32), placed)
        rank = rank + sends[k].astype(I32)
    zi, zj = lax.broadcasted_iota(I32, (8, 64), 0), lax.broadcasted_iota(I32, (8, 64), 1)
    picks[...] = exact_dot(jnp.right_shift(zj, 3) == zi, placed).astype(I32)
    table = jnp.zeros((64, WIDTH), I32)
    for k in range(CODES):
        table = jnp.where(lane64 == k, items[k], table)
    codes[...] = table
    mine[...] = codes[pl.ds(pl.multiple_of(zed * 8, 8), 8), :]


def rims_kernel(tr, ve, out, turned):
    lane = lane_iota(WIDTH) // 4
    gathered = jnp.zeros((WIDTH, WIDTH), F32)
    for slot in range(4):
        for fl in range(8):
            ref, k = (tr, fl) if fl < 4 else (ve, fl - 4)
            for depth in range(2):
                out[pl.ds((slot * 4 + 0) * EDGE + depth * 8 + fl, 1), :] = ref[slot, k, pl.ds(depth, 1), :]
                out[pl.ds((slot * 4 + 1) * EDGE + depth * 8 + fl, 1), :] = ref[slot, k, pl.ds(127 - depth, 1), :]
            tile = slot * 8 + fl
            rolled = pltpu.roll(ref[slot, k], (4 * tile + 2) % WIDTH, 1)
            gathered = jnp.where(lane == tile, rolled, gathered)
    turned[...] = gathered.T
    for slot in range(4):
        for j, (side, depth) in enumerate([(3, 1), (3, 0), (2, 0), (2, 1)]):
            out[pl.ds((slot * 4 + side) * EDGE + depth * 8, 8), :] = turned[pl.ds(slot * 32 + j, 8, stride=4), :]


def message_kernel(table_hbm, mine, other, chip, out, table, sem):
    fetch = pltpu.make_async_copy(table_hbm, table, sem.at[0])
    fetch.start()
    core = lax.axis_index("blk").astype(I32) & 1
    flag = core == 0
    for t in range(4):
        for side in range(4):
            at = (t * 4 + side) * EDGE
            a, b = mine[pl.ds(at, EDGE), :], other[pl.ds(at, EDGE), :]
            chip[pl.ds(at, EDGE), :] = jnp.where(flag, a, b)
            chip[pl.ds(16 * EDGE + at, EDGE), :] = jnp.where(flag, b, a)
    for t in range(8):
        at = pl.multiple_of(jnp.where(flag, t * 4 + 1, t * 4) * EDGE, EDGE)
        out[pl.ds(t * EDGE, EDGE), :] = chip[pl.ds(at, EDGE), :]
        out[pl.ds((10 + t) * EDGE, EDGE), :] = chip[pl.ds((t * 4 + 1) * EDGE, EDGE), :]
    lane = lax.broadcasted_iota(I32, (8, WIDTH), 1) // 2
    corners = jnp.zeros((8, WIDTH), F32)
    for t in range(8):
        for side, base in ((1, 0), (0, 8)):
            x = chip[pl.ds((t * 4 + side) * EDGE, 8), :]
            corners = jnp.where(lane == base + t, pltpu.roll(x, 2 * (base + t) + 1, 1), corners)
    out[pl.ds(MSG_EDGES * EDGE, 8), :] = corners
    fetch.wait()
    last, first_col, last_col = table[0, 0], table[0, 1], table[0, 2]
    for e, edge in ((8, jnp.where(flag, last * 4 + 3, 2)), (9, jnp.where(flag, first_col * 4 + 2, last_col * 4 + 3))):
        at = pl.multiple_of(edge * EDGE, EDGE)
        out[pl.ds(e * EDGE, EDGE), :] = chip[pl.ds(at, EDGE), :]


def pack_kernel(picks_hbm, m0, m1, m2, m3, c4, c5, out, picks, started, held, packed, sem, sent):
    messages = (m0, m1, m2, m3)
    fetch = pltpu.make_async_copy(picks_hbm, picks, sem.at[14])
    fetch.start()
    copies = [
        pltpu.make_async_copy(m.at[pl.ds(MSG_EDGES * EDGE, 8)] if i < 4 else m, held.at[pl.ds(i * 8, 8)], sem.at[i])
        for i, m in enumerate((*messages, c4, c5))
    ]
    for copy in copies:
        copy.start()
    started[0] = 0
    fetch.wait()

    def edge(k, r):
        code = picks[k, r]

        @pl.when(code > 0)
        def _():
            started[0] = started[0] + 1
            for i, m in enumerate(messages):

                @pl.when((code > i * (MSG // 8)) & (code <= (i + 1) * (MSG // 8)))
                def _():
                    row = pl.multiple_of((code - 1 - i * (MSG // 8)) * 8, EDGE)
                    pltpu.make_async_copy(m.at[pl.ds(row, EDGE)], out.at[pl.ds(k * CHUNK + r * EDGE, EDGE)], sent.at[0]).start()

            if r + 1 < CAP:
                edge(k, r + 1)

    for k in range(8):
        edge(k, 0)
    for copy in copies:
        copy.wait()
    lane = lane_iota(8) // 32
    near_c = held[pl.ds(0, 8), :]
    for i in range(1, 4):
        near_c = jnp.where(lane == i, pltpu.roll(held[pl.ds(i * 8, 8), :], 32 * i, 1), near_c)
    packed[pl.ds(0, 8), :] = near_c
    packed[pl.ds(8, 8), :] = jnp.where(lane == 0, held[pl.ds(32, 8), :], pltpu.roll(held[pl.ds(40, 8), :], 32, 1))
    copies = [pltpu.make_async_copy(packed, out.at[pl.ds(k * CHUNK + CAP * EDGE, 16)], sem.at[6 + k]) for k in range(8)]
    for copy in copies:
        copy.start()

    def wait(i, carry):
        pltpu.make_async_copy(m0.at[pl.ds(0, EDGE)], out.at[pl.ds(0, EDGE)], sent.at[0]).wait()
        return carry

    lax.fori_loop(0, started[0], wait, 0)
    for copy in copies:
        copy.wait()


def sort_kernel(table_hbm, got_in, own, other, table, taken, rows, got, sem):
    fetch = pltpu.make_async_copy(table_hbm, table, sem.at[0])
    fetch.start()
    copies = [
        pltpu.make_async_copy(got_in.at[pl.ds(z * CHUNK, CHUNK)], got.at[pl.ds(z * CHUNK, CHUNK)], sem.at[1 + z]) for z in range(8)
    ]
    for copy in copies:
        copy.start()
    core = lax.axis_index("blk").astype(I32) & 1
    for z in range(8):
        taken[z] = 0
    fetch.wait()
    for t in range(8):
        for side in range(4):
            code = table[t, 4 + side]
            z = jnp.maximum(code, 0)
            rank = taken[z]
            taken[z] = rank + (code >= 0).astype(I32)
            rows[t * 4 + side] = z * CHUNK + jnp.minimum(rank, CAP - 1) * EDGE
    for copy in copies:
        copy.wait()
    lane = lane_iota(8)
    for half, out in enumerate((own, other)):
        first = (core ^ half) * 4
        corners = jnp.zeros((8, WIDTH), F32)
        for e in range(16):
            at = pl.multiple_of(rows[first * 4 + e], EDGE)
            out[pl.ds(e * EDGE, EDGE), :] = got[pl.ds(at, EDGE), :]
            code = table[first + e // 4, 12 + e % 4]
            turn = (e - code) & (WIDTH - 1)
            at = pl.multiple_of(jnp.right_shift(jnp.maximum(code, 0), 7) * 8, 8)
            corners = jnp.where(lane == jnp.where(code >= 0, e, -1), pltpu.roll(got[pl.ds(at, 8), :], turn, 1), corners)
        out[pl.ds(16 * EDGE, 8), :] = corners


def pressure(t0, t1, s0, s1):
    r0 = t0 * (-0.3 - 0.08 * t0 + 0.05 * s0) + 0.6 * s0
    r1 = t1 * (-0.3 - 0.08 * t1 + 0.05 * s1) + 0.6 * s1
    return 0.25 * r0, 0.5 * r0 + 0.25 * r1


def stencil(c, e, w, n, s, oe, ow, on, os, f):
    def times(o, x):
        return x if o is None else o * x

    ue, uw = 0.025 * (c[2] + e[2]), 0.025 * (w[2] + c[2])
    vn, vs = 0.025 * (c[3] + n[3]), 0.025 * (s[3] + c[3])
    ae, be = times(oe, 0.05 - ue), times(oe, 0.05 + ue)
    aw, bw = times(ow, 0.05 + uw), times(ow, 0.05 - uw)
    an, bn = times(on, 0.05 - vn), times(on, 0.05 + vn)
    as_, bs = times(os, 0.05 + vs), times(os, 0.05 - vs)
    mid = 1.0 - ((be + bw) + (bn + bs))
    out = []
    for i in range(2):
        out.append(mid * c[i] + ((ae * e[i] + aw * w[i]) + (an * n[i] + as_ * s[i])))
    for i, (lo, hi, olo, ohi) in ((2, (w, e, ow, oe)), (3, (s, n, os, on))):
        lap = (times(oe, e[i] - c[i]) + times(ow, w[i] - c[i])) + (times(on, n[i] - c[i]) + times(os, s[i] - c[i]))
        grad = times(ohi, hi[4] - c[4]) + times(olo, c[4] - lo[4])
        turn = f * c[3] if i == 2 else -(f * c[2])
        out.append(c[i] + (0.1 * turn + 0.05 * (lap - grad)))
    return out


def inner_kernel(table, tr, ve, tr_out, ve_out, rims, xa, xb, gathered):
    core = lax.axis_index("blk").astype(I32) & 1
    y16 = lax.broadcasted_iota(I32, (EDGE, WIDTH), 0).astype(F32)
    lane = lane_iota(WIDTH)
    for src in (xa, xb):
        for q in range(10):
            src[q, pl.ds(0, 8), :] = jnp.zeros((8, WIDTH), F32)
            src[q, pl.ds(136, 8), :] = jnp.zeros((8, WIDTH), F32)

    def one_slot(slot, carry):
        base = table[core * 4 + slot, 26].astype(F32) * float(WIDTH)
        alive = table[core * 4 + slot, 24] == 1
        for q in range(8):
            ref, k = (tr, q) if q < 4 else (ve, q - 4)
            xa[q, pl.ds(8, WIDTH), :] = ref[slot, k]
        for step, src in enumerate((xa, xb)):
            for r in range(8, 8 + WIDTH, EDGE):
                p0, p1 = pressure(*[src[q, pl.ds(r, EDGE), :] for q in range(4)])
                src[8, pl.ds(r, EDGE), :] = p0
                src[9, pl.ds(r, EDGE), :] = p1
            for r in range(0, WIDTH, EDGE):
                f = (base + (y16 + (r + 0.5))) * (2.0 / (ROWS * WIDTH))
                for level in range(2):
                    c, e, w, n, s = [], [], [], [], []
                    for i in range(5):
                        q = 2 * i + level
                        x = src[q, pl.ds(8 + r, EDGE), :]
                        c.append(x)
                        e.append(pltpu.roll(x, WIDTH - 1, 1))
                        w.append(pltpu.roll(x, 1, 1))
                        n.append(src[q, pl.ds(9 + r, EDGE), :])
                        s.append(src[q, pl.ds(7 + r, EDGE), :])
                    new = stencil(c, e, w, n, s, None, None, None, None, f)
                    for i in range(4):
                        if step == 0:
                            xb[2 * i + level, pl.ds(8 + r, EDGE), :] = new[i]
                        else:
                            out = tr_out if i < 2 else ve_out
                            out[slot, 2 * (i % 2) + level, pl.ds(r, EDGE), :] = jnp.where(alive, new[i], 0.0)
        for q in range(8):
            at = pl.multiple_of(slot * 4 * EDGE, EDGE)
            for ring in range(2):
                rims[pl.ds(at + ring * 8 + q, 1), :] = xb[q, pl.ds(8 + 1 + ring, 1), :]
                rims[pl.ds(at + EDGE + ring * 8 + q, 1), :] = xb[q, pl.ds(8 + 126 - ring, 1), :]
            tile = slot * 8 + q
            x = xb[q, pl.ds(8, WIDTH), :]
            a, b = pltpu.roll(x, (tile * 4 + 3) & (WIDTH - 1), 1), pltpu.roll(x, (tile * 4 + 1) & (WIDTH - 1), 1)
            mine = jnp.right_shift(lane, 2) == tile
            gathered[...] = jnp.where(mine, jnp.where((lane & 3) < 2, a, b), gathered[...])
        return carry

    gathered[...] = jnp.zeros((WIDTH, WIDTH), F32)
    lax.fori_loop(0, 4, one_slot, 0)
    gathered[...] = gathered[...].T
    for slot in range(4):
        for j, (side, ring) in enumerate([(3, 1), (3, 0), (2, 0), (2, 1)]):
            rims[pl.ds((slot * 4 + side) * EDGE + ring * 8, 8), :] = gathered[pl.ds(slot * 32 + j, 8, stride=4), :]


def lateral(x, ring):
    even = (row_iota(8) & 1) == 0
    up, down = pltpu.roll(x, 7, 0), pltpu.roll(x, 1, 0)
    back = pltpu.roll(x, WIDTH - ring, 1) if ring else x
    ahead = pltpu.roll(x, ring, 1) if ring else x
    low = jnp.where(even, pltpu.roll(up, ring + 1, 1), back)
    high = jnp.where(even, ahead, pltpu.roll(down, WIDTH - 1 - ring, 1))
    return low, high


def final_kernel(
    table, chip, own, other, edges, rims, tr, ve, tr_out, ve_out, held, hx, inn, mid, crv, upd, first, r0, r1, turned, res_t, res_v, sem, sent
):
    sizes = (8 * 4 * EDGE, SWAP, SWAP)
    starts = (0, sizes[0], sizes[0] + SWAP)
    copies = [
        pltpu.make_async_copy(x, held.at[pl.ds(at, n)], sem.at[i]) for i, (x, at, n) in enumerate(zip((chip, own, other), starts, sizes))
    ]
    for copy in copies:
        copy.start()
    held[pl.ds(starts[2] + SWAP, EDGE), :] = jnp.zeros((EDGE, WIDTH), F32)
    core = lax.axis_index("blk").astype(I32) & 1

    def item(slot, k):
        return table[core * 4 + slot, k]

    def factor(slot, k):
        return item(slot, k).astype(F32)

    i0, i1 = row_iota(WIDTH), lane_iota(WIDTH)
    mirror = (i0 + i1 == WIDTH - 1).astype(F32)
    sign = jnp.where((row_iota(EDGE) & 7) >= 4, -1.0, 1.0)
    lane8, sub8 = lane_iota(8), row_iota(8)
    even = (sub8 & 1) == 0
    sign8 = jnp.where(sub8 >= 4, -1.0, 1.0)
    where_to = ((0, 1), (0, 0), (1, 1), (1, 0))

    for slot in range(4):
        for side in range(4):
            group, odd = where_to[side]
            at = (slot * 4 + side) * EDGE
            inn[group, :, slot * 2 + odd, :] = edges[pl.ds(at, EDGE), :]
            mid[group, :, slot * 2 + odd, :] = rims[pl.ds(at, EDGE), :]
    for copy in copies:
        copy.wait()
    corners = held[pl.ds(starts[1] + 16 * EDGE, 8), :] + held[pl.ds(starts[2] + 16 * EDGE, 8), :]
    for slot in range(4):
        top = item(slot, 25) == 1
        for side in range(4):
            group, odd = where_to[side]
            x = held[pl.ds(pl.multiple_of(item(slot, 8 + side) * 8, 8), EDGE), :]
            if side == 1:
                flipped = jnp.dot(x, mirror, preferred_element_type=F32, precision=lax.Precision.HIGHEST) * sign
                x = jnp.where(top, flipped, x)
            hx[group, :, slot * 2 + odd, :] = x
        for group, odd, lo, hi in ((0, 0, 2, 3), (0, 1, 0, 1), (1, 0, 1, 3), (1, 1, 0, 2)):
            vals = []
            for which, lane in ((lo, 0), (hi, WIDTH - 1)):
                v = pltpu.roll(corners, (lane - (slot * 4 + which)) % WIDTH, 1)
                if which >= 2:
                    v = jnp.where(top, v * sign8, v)
                vals.append(v)
            crv[group, :, slot * 2 + odd, :] = jnp.where(lane8 == 0, vals[0], vals[1])

    def strip(group, c, outer, inner, low, high, o_out, o_low, o_high, cor, out):
        at_c, at_p, at_m, at_h, at_l = [], [], [], [], []
        for q in range(8):
            x = c(q)
            at_c.append(x)
            at_p.append(jnp.where(even, outer(q), inner(q)))
            at_m.append(jnp.where(even, inner(q), outer(q)))
            lo, hi = low(q), high(q)
            at_h.append(jnp.where(lane8 == WIDTH - 1, hi, pltpu.roll(x, WIDTH - 1, 1)))
            at_l.append(jnp.where(lane8 == 0, lo, pltpu.roll(x, 1, 1)))
        five = [x + list(pressure(x[0], x[1], x[2], x[3])) for x in (at_c, at_p, at_m, at_h, at_l)]
        o_pos = None if o_out is None else jnp.where(even, o_out, 1.0)
        o_neg = None if o_out is None else jnp.where(even, 1.0, o_out)
        for level in range(2):
            c, p, m, h, l = [[x[2 * i + level] for i in range(5)] for x in five]
            if group == 0:
                new = stencil(c, h, l, p, m, o_high, o_low, o_pos, o_neg, cor)
            else:
                new = stencil(c, p, m, h, l, o_pos, o_neg, o_high, o_low, cor)
            for i in range(4):
                out[group, 2 * i + level] = new[i]

    def by_row(values):
        x = jnp.zeros((8, WIDTH), F32)
        for slot in range(4):
            for odd in range(2):
                x = jnp.where(sub8 == slot * 2 + odd, values(slot, odd), x)
        return x

    def ends(x, where):
        return jnp.where(lane8 == where, x, 1.0)

    scale = 2.0 / (ROWS * WIDTH)
    base = by_row(lambda slot, odd: factor(slot, 26) * float(WIDTH))
    halo_row = by_row(
        lambda slot, odd: -1.0 if odd else jnp.where(item(slot, 25) == 1, WIDTH - 1.0, float(WIDTH)),
    )
    across = (base + lane8.astype(F32) + 0.5) * scale
    o_out, o_low, o_high, cor0, cor1 = [], [], [], [], []
    for group in range(2):
        o_out.append(by_row(lambda slot, odd: factor(slot, ((17, 16), (19, 18))[group][odd])))
        lo, hi = ((18, 19), (16, 17))[group]
        o_low.append(ends(by_row(lambda slot, odd: factor(slot, lo)), 0))
        o_high.append(ends(by_row(lambda slot, odd: factor(slot, hi)), WIDTH - 1))
        if group == 0:
            cor0.append((base + jnp.where(even, WIDTH - 1.0, 0.0) + 0.5) * scale)
            cor1.append((base + jnp.where(even, WIDTH - 2.0, 1.0) + 0.5) * scale)
        else:
            cor0.append(across)
            cor1.append(across)

    for group in range(2):
        lo, hi = ((22, 23), (20, 21)) if group == 0 else ((21, 23), (20, 22))
        corner_low = ends(by_row(lambda slot, odd: factor(slot, (lo, hi)[odd][0])), 0)
        corner_high = ends(by_row(lambda slot, odd: factor(slot, (lo, hi)[odd][1])), WIDTH - 1)
        cor = (base + halo_row + 0.5) * scale if group == 0 else across
        strip(
            group,
            lambda q: hx[group, q],
            lambda q: hx[group, 8 + q],
            lambda q: inn[group, q],
            lambda q: crv[group, q],
            lambda q: crv[group, q],
            None,
            corner_low,
            corner_high,
            cor,
            upd,
        )
    for group in range(2):
        beyond = [lateral(hx[1 - group, q], 0) for q in range(8)]
        strip(
            group,
            lambda q: inn[group, q],
            lambda q: hx[group, q],
            lambda q: inn[group, 8 + q],
            lambda q: beyond[q][0],
            lambda q: beyond[q][1],
            o_out[group],
            o_low[group],
            o_high[group],
            cor0[group],
            first,
        )
    for group in range(2):
        for q in range(8):
            for ring in (1, 2):
                low, high = lateral(first[1 - group, q], ring)
                x = mid[group, (ring - 1) * 8 + q]
                mid[group, (ring - 1) * 8 + q] = jnp.where(lane8 == 0, low, jnp.where(lane8 == WIDTH - 1, high, x))
    for group in range(2):
        beyond0 = [lateral(upd[1 - group, q], 0) for q in range(8)]
        strip(
            group,
            lambda q: first[group, q],
            lambda q: upd[group, q],
            lambda q: mid[group, q],
            lambda q: beyond0[q][0],
            lambda q: beyond0[q][1],
            o_out[group],
            o_low[group],
            o_high[group],
            cor0[group],
            r0,
        )
        beyond1 = [lateral(upd[1 - group, q], 1) for q in range(8)]
        strip(
            group,
            lambda q: mid[group, q],
            lambda q: first[group, q],
            lambda q: mid[group, 8 + q],
            lambda q: beyond1[q][0],
            lambda q: beyond1[q][1],
            None,
            o_low[group],
            o_high[group],
            cor1[group],
            r1,
        )

    live8 = by_row(lambda slot, odd: factor(slot, 24)) > 0.5
    for group in range(2):
        for q in range(8):
            r0[group, q] = jnp.where(live8, r0[group, q], 0.0)
            r1[group, q] = jnp.where(live8, r1[group, q], 0.0)
    for q in range(8):
        for slot in range(4):
            for j, (ring, odd) in enumerate(((r1, 0), (r0, 0), (r0, 1), (r1, 1))):
                turned[pl.ds((slot * 8 + q) * 4 + j, 1), :] = ring[1, q, pl.ds(slot * 2 + odd, 1), :]
    turned[...] = turned[...].T
    lane16 = lane_iota(EDGE)
    rim = (lane16 < 2) | (lane16 >= WIDTH - 2)
    out_copies = []
    for slot in range(4):
        for q in range(8):
            src, res, k = (tr, res_t, q) if q < 4 else (ve, res_v, q - 4)
            tile = slot * 8 + q
            for r in range(0, WIDTH, EDGE):
                x = pltpu.roll(turned[pl.ds(r, EDGE), :], (-(tile * 4 + 2)) % WIDTH, 1)
                res[slot, k, pl.ds(r, EDGE), :] = jnp.where(rim, x, src[slot, k, pl.ds(r, EDGE), :])
            for ring, rr in ((0, r0), (1, r1)):
                res[slot, k, pl.ds(ring, 1), :] = rr[0, q, pl.ds(slot * 2 + 1, 1), :]
                res[slot, k, pl.ds(WIDTH - 1 - ring, 1), :] = rr[0, q, pl.ds(slot * 2, 1), :]
            if k == 3:
                out = tr_out if q < 4 else ve_out
                copy = pltpu.make_async_copy(res.at[slot], out.at[slot], sent.at[slot * 2 + q // 4])
                copy.start()
                out_copies.append(copy)
    for copy in out_copies:
        copy.wait()


def shape(*dims):
    return jax.ShapeDtypeStruct(dims, F32)


def table_shape(rows):
    return jax.ShapeDtypeStruct((rows, WIDTH), I32)


def exclusive_count(mask):
    i = jnp.arange(mask.shape[-1])
    return jnp.sum(mask[..., None, :] & (i[None, :] < i[:, None]), axis=-1).astype(I32)


def permute(x, pairs):
    return lax.ppermute(x, "blk", pairs)


def column_pairs(distance):
    pairs = []
    for i in range(DEVICES):
        j = i + 16 * distance * (1 if i % 2 == 0 else -1)
        pairs.append((i, j if 0 <= j < DEVICES else i ^ 1))
    return pairs


NEAR_PAIRS = [(i, i + 48) for i in range(32) if i % 2 == 0 and i % 16 >= 12]
NEAR_PAIRS += [(i, i - 48) for i in range(48, 80) if i % 2 == 1 and i % 16 < 4]
FAR_PAIRS = [(0, 64), (67, 3)]


def exchange_z(x):
    groups = [[16 * a + 2 * z + c for z in range(8)] for a in range(16) for c in range(2)]
    return lax.all_to_all(x, "blk", 0, 0, axis_index_groups=groups, tiled=True)


def pack(picks, message, near, far):
    return pl.pallas_call(
        pack_kernel,
        out_shape=shape(8 * CHUNK, WIDTH),
        in_specs=[HB] * 7,
        out_specs=HB,
        scratch_shapes=[
            pltpu.SMEM((8, WIDTH), I32),
            pltpu.SMEM((1,), I32),
            pltpu.VMEM((48, WIDTH), F32),
            pltpu.VMEM((16, WIDTH), F32),
            pltpu.SemaphoreType.DMA((15,)),
            pltpu.SemaphoreType.DMA((1,)),
        ],
        compiler_params=params(12),
        name="pack",
    )(picks, message, *near, *far)


def sort(mine, got):
    return pl.pallas_call(
        sort_kernel,
        out_shape=(shape(SWAP, WIDTH), shape(SWAP, WIDTH)),
        in_specs=[HB, HB],
        out_specs=(VM, VM),
        scratch_shapes=[
            pltpu.SMEM((8, WIDTH), I32),
            pltpu.SMEM((8,), I32),
            pltpu.SMEM((32,), I32),
            pltpu.VMEM((8 * CHUNK, WIDTH), F32),
            pltpu.SemaphoreType.DMA((9,)),
        ],
        compiler_params=params(12),
        name="sort",
    )(mine, got)


def second_round(own, others, codes, mine, message, near):
    down = (lax.axis_index("blk").astype(I32) & 1) == 1
    held = jnp.concatenate([message, *near])
    send = codes[:, :4].reshape(8, 32)
    rank = exclusive_count(send > 0)
    late = jnp.arange(CAP, CAP + MORE)
    more = jnp.sum(jnp.where((send > 0)[:, None] & (rank[:, None] == late[None, :, None]), send[:, None] - 1, 0), axis=-1)
    rows = more[:, :, None] * 8 + jnp.arange(EDGE, dtype=I32)
    more = exchange_z(held[rows].reshape(8, MORE * EDGE, WIDTH)).reshape(8 * MORE * EDGE, WIDTH)
    zed = mine[:, 4:8].reshape(32)
    i32 = jnp.arange(32)
    rank = jnp.sum((zed[None] >= 0) & (zed[None] == zed[:, None]) & (i32[None] < i32[:, None]), axis=1).astype(I32)
    late = (zed >= 0) & (rank >= CAP)
    start = jnp.where(late, zed * (MORE * EDGE) + (rank - CAP) * EDGE, 0)
    start, late = [jnp.where(down, jnp.concatenate([x[16:], x[:16]]), x) for x in (start, late)]
    new = more[start[:, None] + jnp.arange(EDGE, dtype=I32)]
    old = jnp.stack([own[: 16 * EDGE], others[: 16 * EDGE]]).reshape(32, EDGE, WIDTH)
    new = jnp.where(late[:, None, None], new, old).reshape(2, 16 * EDGE, WIDTH)
    return jnp.concatenate([new[0], own[16 * EDGE :]]), jnp.concatenate([new[1], others[16 * EDGE :]])


def run(tracers, velocity, block_counts, land, usual):
    tr = tracers.reshape(4, 4, WIDTH, WIDTH)
    ve = velocity.reshape(4, 4, WIDTH, WIDTH)
    swap = [(i, i ^ 1) for i in range(DEVICES)]

    grid, marks = pl.pallas_call(
        ids_kernel,
        out_shape=(table_shape(32), table_shape(8)),
        in_specs=[HB, HB],
        out_specs=(VM, VM),
        scratch_shapes=[
            pltpu.SMEM((DEVICES,), I32),
            pltpu.VMEM((ROWS, COLS), I32),
            pltpu.VMEM((32, WIDTH), I32),
            pltpu.SemaphoreType.DMA((2,)),
        ],
        compiler_params=params(12),
        cost_estimate=pl.CostEstimate(flops=2_000_000, bytes_accessed=100_000, transcendentals=0),
        name="ids",
    )(block_counts, land)
    rims = pl.pallas_call(
        rims_kernel,
        out_shape=shape(16 * EDGE, WIDTH),
        in_specs=[VM, VM],
        out_specs=VM,
        scratch_shapes=[pltpu.VMEM((WIDTH, WIDTH), F32)],
        compiler_params=params(12),
        name="rims",
    )(tr, ve)
    codes, mine, picks, enough = pl.pallas_call(
        tables_kernel,
        out_shape=(table_shape(64), table_shape(8), table_shape(8), jax.ShapeDtypeStruct((1,), I32)),
        in_specs=[VM],
        out_specs=(VM, VM, VM, SM),
        compiler_params=params(12),
        cost_estimate=pl.CostEstimate(flops=2_000_000, bytes_accessed=100_000, transcendentals=0),
        name="tables",
    )(grid)
    other = permute(rims, swap)
    chip, message = pl.pallas_call(
        message_kernel,
        out_shape=(shape(32 * EDGE, WIDTH), shape(MSG, WIDTH)),
        in_specs=[HB, VM, VM],
        out_specs=(VM, VM),
        scratch_shapes=[pltpu.SMEM((8, WIDTH), I32), pltpu.SemaphoreType.DMA((1,))],
        compiler_params=params(12),
        name="message",
    )(marks, rims, other)
    corners = message[MSG_EDGES * EDGE :]
    if usual:
        far = permute(corners, FAR_PAIRS)
        far = (far, far)
        near = [permute(message, NEAR_PAIRS), *[permute(message, column_pairs(d)) for d in (1, 2)]]
        near = [near[1], near[2], near[0]]
    else:
        far = [permute(corners, column_pairs(d)) for d in (4, 5)]
        near = [permute(message, column_pairs(d)) for d in (1, 2, 3)]
    chunks = pack(picks, message, near, far)
    tr, ve, chunks = lax.optimization_barrier((tr, ve, chunks))
    tr_inner, ve_inner, inner_rims = pl.pallas_call(
        inner_kernel,
        out_shape=(shape(4, 4, WIDTH, WIDTH), shape(4, 4, WIDTH, WIDTH), shape(16 * EDGE, WIDTH)),
        in_specs=[SM, VM, VM],
        out_specs=(VM, VM, VM),
        scratch_shapes=[
            pltpu.VMEM((10, 144, WIDTH), F32),
            pltpu.VMEM((10, 144, WIDTH), F32),
            pltpu.VMEM((WIDTH, WIDTH), F32),
        ],
        compiler_params=params(12),
        cost_estimate=pl.CostEstimate(flops=60_000_000, bytes_accessed=8_000_000, transcendentals=0),
        name="inner",
    )(mine, tr, ve)
    got = exchange_z(chunks.reshape(8, CHUNK, WIDTH)).reshape(8 * CHUNK, WIDTH)
    got, tr_inner, ve_inner, inner_rims = lax.optimization_barrier((got, tr_inner, ve_inner, inner_rims))
    own, others = sort(mine, got)
    if not usual:
        own, others = second_round(own, others, codes, mine, message, near)
    theirs = permute(others, swap)

    tr_new, ve_new = pl.pallas_call(
        final_kernel,
        out_shape=(shape(4, 4, WIDTH, WIDTH), shape(4, 4, WIDTH, WIDTH)),
        in_specs=[SM] + [HB] * 3 + [VM] * 4,
        out_specs=(HB, HB),
        scratch_shapes=[
            pltpu.VMEM((32 * EDGE + 2 * SWAP + EDGE, WIDTH), F32),
            pltpu.VMEM((2, EDGE, 8, WIDTH), F32),
            pltpu.VMEM((2, EDGE, 8, WIDTH), F32),
            pltpu.VMEM((2, EDGE, 8, WIDTH), F32),
            pltpu.VMEM((2, 8, 8, WIDTH), F32),
            pltpu.VMEM((2, 8, 8, WIDTH), F32),
            pltpu.VMEM((2, 8, 8, WIDTH), F32),
            pltpu.VMEM((2, 8, 8, WIDTH), F32),
            pltpu.VMEM((2, 8, 8, WIDTH), F32),
            pltpu.VMEM((WIDTH, WIDTH), F32),
            pltpu.VMEM((4, 4, WIDTH, WIDTH), F32),
            pltpu.VMEM((4, 4, WIDTH, WIDTH), F32),
            pltpu.SemaphoreType.DMA((3,)),
            pltpu.SemaphoreType.DMA((8,)),
        ],
        compiler_params=params(12),
        name="final",
    )(mine, chip, own, theirs, rims, inner_rims, tr_inner, ve_inner)
    return enough[0] != 0, tr_new.reshape(tracers.shape), ve_new.reshape(velocity.shape)


def per_device(tracers, velocity, block_counts, land):
    enough, *out = run(tracers, velocity, block_counts, land, True)

    def again(out, args):
        return run(*args, False)[1:]

    return lax.cond(enough, lambda out, args: tuple(out), again, tuple(out), (tracers, velocity, block_counts, land))


def solution(mesh):
    spec = P("blk", None, None, None, None)
    return jax.shard_map(
        per_device,
        mesh=mesh,
        in_specs=(spec, spec, P(), P()),
        out_specs=(spec, spec),
        check_vma=False,
    )
```
